32 devices in a mesh: req: 8 (over y, x, core), head: 4 (over z).
Axes of the slice: x: 2, y: 2, z: 4, core: 2. Of those that a mesh axis runs over, the one named last changes fastest.
Arguments:
- queries: bfloat16 [256, 8192], P('req', 'head'), may hold values from -64 to 64
- key_new: bfloat16 [256, 1024], P('req', 'head'), may hold values from -6 to 6
- value_new: bfloat16 [256, 1024], P('req', 'head'), may hold values from -6 to 6
- key_pool: bfloat16 [1536, 128, 1024], P('req', None, 'head'), may hold values from -10 to 10
- value_pool: bfloat16 [1536, 128, 1024], P('req', None, 'head'), may hold values from -6 to 6
- page_table: int32 [256, 64], P('req'), may hold values from -1 to 1535, as said below
- lengths: int32 [256], P('req'), may hold values from 1 to 8192, as said below
- residual_in: bfloat16 [256, 8192], P('head', 'req'), may hold values from -3 to 3
- w_out: bfloat16 [8192, 8192], P('head', 'req'), may hold values from -0.5 to 0.5
- norm_gain: bfloat16 [8192], replicated, may hold values from 0.25 to 1.75
- w_gate: bfloat16 [8192, 29568], P(None, ('req', 'head')), may hold values from -0.0625 to 0.0625
- w_up: bfloat16 [8192, 29568], P(None, ('req', 'head')), may hold values from -0.0625 to 0.0625
- w_down: bfloat16 [29568, 8192], P(('req', 'head')), may hold values from -0.0625 to 0.0625
Outputs:
- output: bfloat16 [256, 8192], P('head', 'req')
The draws below stay inside these ranges and needn't reach their ends.
Inputs may be any that keep to these rules, and one draw needn't show every extreme that they name: `page_table`: entry k of request b is a pool page for k < ceil(lengths[b] / 128) and -1 otherwise; no pool page appears twice in the table. `lengths`: one request holds exactly 8192 cached tokens.
All inputs are finite; a program needn't handle non-finite values.
Results may differ from the reference program's by a relative error of at most 0.009.
Values may be sent and summed in bfloat16 or wider, within the bound.
No kernel may reach another device: no remote copies, remote signals or barrier semaphores. Data moves between devices by JAX's collectives and lax.ppermute only.
A program may use at most 128 MiB of HBM per device.

```python
import math
import jax
import jax.numpy as jnp
from jax import lax

D = 8192
FF = 29568
HEADS = 64
KV_HEADS = 8
HEAD_DIM = 128
PAGE = 128
MAX_PAGES = 64
REQUESTS = 256
POOL = 1536


def page_layout(key):
    base = jax.random.fold_in(key, 11)
    key_heavy, key_counts, key_tail, key_order = jax.random.split(base, 4)
    req_index = jnp.arange(REQUESTS, dtype=jnp.int32)
    heavy = jax.random.randint(key_heavy, (), 0, REQUESTS)
    counts = 1 + jnp.min(jax.random.randint(key_counts, (12, REQUESTS), 0, MAX_PAGES - 1), axis=0)
    others = jnp.where(req_index == heavy, 0, counts)
    fits = jnp.cumsum(others) + (REQUESTS - 1 - req_index) <= POOL - MAX_PAGES
    pages = jnp.where(req_index == heavy, MAX_PAGES, jnp.where(fits, counts, 1)).astype(jnp.int32)
    tail = jax.random.randint(key_tail, (REQUESTS,), 1, PAGE + 1)
    lengths = (pages - 1) * PAGE + jnp.where(req_index == heavy, PAGE, tail)
    order = jax.random.permutation(key_order, POOL).astype(jnp.int32)
    offsets = jnp.cumsum(pages) - pages
    slot_index = jnp.arange(MAX_PAGES, dtype=jnp.int32)
    flat_index = jnp.minimum(offsets[:, None] + slot_index[None, :], POOL - 1)
    table = jnp.where(slot_index[None, :] < pages[:, None], order[flat_index], -1)
    return (lengths.astype(jnp.int32), table.astype(jnp.int32))


def draw_lengths(key, part):
    return page_layout(key)[0]


def draw_page_table(key, part):
    return page_layout(key)[1]


def draw_key_pool(key, part):
    noise = jax.random.truncated_normal(jax.random.fold_in(key, 1), -6.0, 6.0, (POOL, PAGE, KV_HEADS, HEAD_DIM), jnp.float32)
    return noise.reshape(POOL, PAGE, KV_HEADS * HEAD_DIM).astype(jnp.bfloat16)


def draw_queries(key, part):
    group_size = HEADS // KV_HEADS
    noise = jax.random.truncated_normal(jax.random.fold_in(key, 3), -6.0, 6.0, (REQUESTS, KV_HEADS, group_size, HEAD_DIM), jnp.float32)
    values = noise
    return values.reshape(REQUESTS, HEADS * HEAD_DIM).astype(jnp.bfloat16)


def strengthened(array, rng, source, target, parts, factor):
    owner, partner = [(jnp.arange(array.shape[dim]) // (array.shape[dim] // parts)).reshape([-1 if axis == dim else 1 for axis in range(array.ndim)]) for dim in (source, target)]
    chosen = jax.random.permutation(rng, parts)[partner]
    strong = (owner == chosen) | (owner == (partner + parts // 2) % parts)
    return jnp.where(strong, factor * array, array)


def block_scale(key, shape, pieces, low, largest):
    factor_of = 1.0
    for dim, parts in pieces:
        steps = jax.random.uniform(jax.random.fold_in(jax.random.fold_in(key, 6), dim), (parts,), jnp.float32, low / len(pieces), largest / len(pieces))
        factor_of = factor_of * jnp.repeat(jnp.exp(steps), shape[dim] // parts).reshape((-1,) + (1,) * (len(shape) - 1 - dim))
    return factor_of


def scatter_about(key, extent, width, limit, cuts=(), kind=jnp.bfloat16):
    drawn = width * jax.random.normal(key, extent, jnp.float32)
    if cuts:
        drawn = drawn * block_scale(key, extent, cuts, -0.22, 0.18)
    return jnp.clip(drawn, -limit, limit).astype(kind)


def heavy_noise(stream_key, shape, width, most, shards, heavy, kind=jnp.bfloat16):
    result = width * jax.random.normal(stream_key, shape, jnp.float32)
    if shards:
        result = result * block_scale(stream_key, shape, shards, -0.22, 0.18)
    return jnp.clip(strengthened(result, jax.random.fold_in(stream_key, 3), *heavy), -most, most).astype(kind)


def setup_inputs(seed: int = 0) -> dict:
    key_of = jax.random.split(jax.random.key(seed), 14)
    queries = draw_queries(jax.random.fold_in(key_of[13], 71), 0)
    key_new = scatter_about(key_of[1], (REQUESTS, KV_HEADS * HEAD_DIM), 1.0, 6.0, ((0, 8), (1, 4)))
    value_new = scatter_about(key_of[2], (REQUESTS, KV_HEADS * HEAD_DIM), 1.0, 6.0, ((0, 8), (1, 4)))
    key_pool = draw_key_pool(jax.random.fold_in(key_of[13], 71), 0)
    value_pool = scatter_about(key_of[4], (POOL, PAGE, KV_HEADS * HEAD_DIM), 1.0, 6.0, ((0, 8), (2, 4)))
    page_table = draw_page_table(jax.random.fold_in(key_of[13], 71), 0)
    lengths = draw_lengths(jax.random.fold_in(key_of[13], 71), 0)
    residual_in = scatter_about(key_of[7], (REQUESTS, D), 0.5, 3.0, ((0, 4), (1, 8)))
    w_out = scatter_about(key_of[8], (HEADS * HEAD_DIM, D), HEAD_DIM ** -0.5, 0.5, ((0, 4), (1, 8)))
    norm_gain = jnp.clip(1.0 + 0.15 * jax.random.normal(key_of[9], (D,), jnp.float32), 0.25, 1.75).astype(jnp.bfloat16)
    w_gate = scatter_about(key_of[10], (D, FF), D ** -0.5, 0.0625, ((1, 32),))
    w_up = scatter_about(key_of[11], (D, FF), D ** -0.5, 0.0625, ((1, 32),))
    w_down = heavy_noise(key_of[12], (FF, D), FF ** -0.5, 0.0625, ((0, 32),), (0, 1, 32, 2.75))
    return {"queries": queries, "key_new": key_new, "value_new": value_new, "key_pool": key_pool, "value_pool": value_pool, "page_table": page_table, "lengths": lengths, "residual_in": residual_in, "w_out": w_out, "norm_gain": norm_gain, "w_gate": w_gate, "w_up": w_up, "w_down": w_down}


NEGATIVE_FILL = -1e+30
NORM_EPS = 1e-06

def reference(queries, key_new, value_new, key_pool, value_pool, page_table, lengths, residual_in, w_out, norm_gain, w_gate, w_up, w_down):
    score_scale = 1.0 / math.sqrt(HEAD_DIM)
    group_size = HEADS // KV_HEADS

    def attend_one(request_data):
        query_row, key_row, value_row, page_row, length = request_data
        page_ids = jnp.maximum(page_row, 0).astype(jnp.int32)
        page_keys = key_pool[page_ids].reshape(MAX_PAGES, PAGE, KV_HEADS, HEAD_DIM).astype(jnp.float32)
        page_values = value_pool[page_ids].reshape(MAX_PAGES, PAGE, KV_HEADS, HEAD_DIM).astype(jnp.float32)
        q_heads = query_row.reshape(KV_HEADS, group_size, HEAD_DIM).astype(jnp.float32)
        scores = jnp.einsum('kgd,pskd->pkgs', q_heads, page_keys) * score_scale
        token_pos = jnp.arange(MAX_PAGES, dtype=jnp.int32)[:, None] * PAGE + jnp.arange(PAGE, dtype=jnp.int32)[None, :]
        is_valid = (token_pos < length)[:, None, None, :]
        masked = jnp.where(is_valid, scores, NEGATIVE_FILL)
        page_max = lax.optimization_barrier(jnp.max(masked, axis=3))
        weights = jnp.where(is_valid, jnp.exp(masked - page_max[..., None]), 0.0).astype(jnp.bfloat16)
        page_sum = lax.optimization_barrier(jnp.sum(weights.astype(jnp.float32), axis=3))
        page_acc = jnp.einsum('pkgs,pskd->pkgd', weights.astype(jnp.float32), page_values)
        own_score = jnp.einsum('kgd,kd->kg', q_heads, key_row.reshape(KV_HEADS, HEAD_DIM).astype(jnp.float32)) * score_scale
        top_score = jnp.maximum(lax.optimization_barrier(jnp.max(page_max, axis=0)), own_score)
        factor = jnp.exp(page_max - top_score[None])
        own_factor = jnp.exp(own_score - top_score)
        weight_total = lax.optimization_barrier(jnp.sum(factor * page_sum, axis=0)) + own_factor
        own_values = value_row.reshape(KV_HEADS, 1, HEAD_DIM).astype(jnp.float32)
        accum = lax.optimization_barrier(jnp.sum(factor[..., None] * page_acc, axis=0)) + own_factor[..., None] * own_values
        return (accum / weight_total[..., None]).reshape(HEADS * HEAD_DIM).astype(jnp.bfloat16)
    attention = lax.map(attend_one, (queries, key_new, value_new, page_table, lengths))
    projected = jnp.dot(attention, w_out, preferred_element_type=jnp.float32)
    state = (residual_in.astype(jnp.float32) + projected).astype(jnp.bfloat16)
    state_wide = state.astype(jnp.float32)
    mean_square = lax.optimization_barrier(jnp.mean(state_wide * state_wide, axis=1, keepdims=True))
    normed = (state_wide * lax.rsqrt(mean_square + NORM_EPS) * norm_gain.astype(jnp.float32)[None, :]).astype(jnp.bfloat16)
    gate_proj = jnp.dot(normed, w_gate, preferred_element_type=jnp.float32)
    up_proj = jnp.dot(normed, w_up, preferred_element_type=jnp.float32)
    hidden = (jax.nn.silu(gate_proj) * up_proj).astype(jnp.bfloat16)
    down_sum = jnp.dot(hidden, w_down, preferred_element_type=jnp.float32)
    return (state.astype(jnp.float32) + down_sum).astype(jnp.bfloat16)
```

```python
import functools
import math

import jax
import jax.numpy as jnp
from jax import lax
from jax.experimental import pallas as pl
from jax.experimental.pallas import tpu as pltpu
from jax.sharding import PartitionSpec as P

HEAD_DIM = 128
LO = 64
NEGATIVE_FILL = -1e30
NORM_EPS = 1e-06
BF16 = jnp.bfloat16
F32 = jnp.float32


def swap(array, axis, bits):
    size = lax.axis_size(axis)
    return lax.ppermute(array, axis, [(i, i ^ bits) for i in range(size)])


def whole(shape):
    return pl.BlockSpec(shape, lambda *_: (0,) * len(shape))


def in_vmem(array):
    return pltpu.with_memory_space_constraint(array, pltpu.VMEM)


def params(mebibytes=24):
    return pltpu.CompilerParams(vmem_limit_bytes=mebibytes * 1024 * 1024)


def pack_kernel(page_len, lengths, table, queries, out):
    reqs, slots = table.shape
    query_rows = queries.shape[0]
    inverse_rows = out.shape[0] - query_rows
    high = lax.broadcasted_iota(jnp.int32, (inverse_rows, slots), 0)
    lane = lax.broadcasted_iota(jnp.int32, (2 * LO, slots), 0)
    first = lax.broadcasted_iota(jnp.int32, (1, slots), 1) * page_len
    total = jnp.zeros((inverse_rows, 2 * LO), F32)
    for r in range(reqs):
        ids = table[pl.ds(r, 1), :]
        tokens = jnp.clip(lengths[r] - first, 0, page_len)
        row_hit = jnp.where((ids >> 6) == high, 1.0, 0.0).astype(BF16)
        held = jnp.where(lane < LO, r + 1, tokens)
        lane_hit = jnp.where((ids & (LO - 1)) == (lane & (LO - 1)), held, 0).astype(F32).astype(BF16)
        total += lax.dot_general(
            row_hit, lane_hit, (((1,), (1,)), ((), ())), preferred_element_type=F32
        )
    out[pl.ds(0, query_rows), :] = queries[...]
    out[pl.ds(query_rows, inverse_rows), :] = total.astype(BF16)


def attend_kernel(
    heads, kv_local, reqs, step_pages, owners, tokens, near, far, keys, values, near_out, far_out,
    query, score, top, weight, acc,
):
    chips = near.shape[0]
    steps = keys.shape[0] // step_pages
    rows = reqs * heads
    group = heads // kv_local
    scale = 1.0 / math.sqrt(HEAD_DIM)
    lane = lax.broadcasted_iota(jnp.int32, (heads, HEAD_DIM), 1)
    head = lax.broadcasted_iota(jnp.int32, (heads, HEAD_DIM), 0)

    for side, ref in enumerate((near, far)):
        for chip in range(chips):
            at = (side * chips + chip) * rows
            query[pl.ds(at, rows), :] = ref[chip, pl.ds(0, rows), :].astype(F32)
    top[...] = jnp.full(top.shape, NEGATIVE_FILL, F32)
    weight[...] = jnp.zeros(weight.shape, F32)
    acc[...] = jnp.zeros(acc.shape, F32)

    def place(page):
        return pl.ds(pl.multiple_of(owners[page] * heads, heads), heads)

    @pl.loop(0, steps)
    def _(step):
        first = step * step_pages
        scores = []
        for p in range(step_pages):
            q = query[place(first + p), :]
            q = jnp.concatenate(
                [jnp.where(head // group == kv, q, 0.0) for kv in range(kv_local)], axis=1
            ).astype(BF16)
            s = lax.dot_general(
                q, keys[first + p], (((1,), (1,)), ((), ())), preferred_element_type=F32
            ) * scale
            scores.append(jnp.where(lane < tokens[first + p], s, NEGATIVE_FILL))
        best = [jnp.max(s, axis=1, keepdims=True) for s in scores]
        for p in range(step_pages):
            score[first + p] = scores[p]
        for p in range(step_pages):
            at = place(first + p)
            top[at, :] = jnp.maximum(top[at, :], best[p])

    top[...] = top[...].astype(BF16).astype(F32)

    @pl.loop(0, steps)
    def _(step):
        first = step * step_pages
        sums, parts = [], []
        for p in range(step_pages):
            page = first + p
            w = jnp.exp(score[page] - top[place(page), :])
            w = jnp.where(lane < tokens[page], w, 0.0).astype(BF16)
            a = jnp.dot(w, values[page], preferred_element_type=F32)
            part = a[:, :HEAD_DIM]
            for kv in range(1, kv_local):
                part = jnp.where(
                    head // group == kv, a[:, kv * HEAD_DIM : (kv + 1) * HEAD_DIM], part
                )
            parts.append(part)
            sums.append(jnp.sum(w.astype(F32), axis=1, keepdims=True))
        for p in range(step_pages):
            at = place(first + p)
            acc[at, :] += parts[p]
            weight[at, :] += sums[p]

    lane3 = lax.broadcasted_iota(jnp.int32, (reqs, heads, HEAD_DIM), 2)
    head3 = lax.broadcasted_iota(jnp.int32, (reqs, heads, HEAD_DIM), 1)
    for side, ref in enumerate((near_out, far_out)):
        for chip in range(chips):
            at = pl.ds((side * chips + chip) * rows, rows)
            ref[chip, pl.ds(0, rows), :] = acc[at, :].astype(BF16)
            t = top[at, :].reshape(reqs, heads, HEAD_DIM)
            s = weight[at, :].reshape(reqs, heads, HEAD_DIM)
            s_high = s.astype(BF16).astype(F32)
            stats = jnp.where(lane3 == head3 + 2 * heads, s - s_high, 0.0)
            stats = jnp.where(lane3 == head3 + heads, s_high, stats)
            stats = jnp.where(lane3 == head3, t, stats)
            ref[chip, pl.ds(rows, reqs), :] = jnp.sum(stats, axis=1).astype(BF16)


def combine_kernel(heads, queries, key_new, value_new, *refs):
    parts, out = refs[:-1], refs[-1]
    rows = queries.shape[0]
    reqs = rows // heads
    lane3 = lax.broadcasted_iota(jnp.int32, (reqs, heads, HEAD_DIM), 2)
    head3 = lax.broadcasted_iota(jnp.int32, (reqs, heads, HEAD_DIM), 1)
    diagonal = lane3 == head3

    def narrow(array):
        return jnp.sum(jnp.where(diagonal, array.reshape(reqs, heads, HEAD_DIM), 0.0), axis=1)

    def wide(array):
        return jnp.sum(jnp.where(diagonal, array[:, None, :], 0.0), axis=2, keepdims=True)

    own = jnp.sum(queries[...].astype(F32) * key_new[...].astype(F32), axis=1, keepdims=True)
    own = narrow(jnp.broadcast_to(own * (1.0 / math.sqrt(HEAD_DIM)), (rows, HEAD_DIM)))
    stats = [part[pl.ds(rows, reqs), :].astype(F32) for part in parts]
    best = functools.reduce(jnp.maximum, stats, own)
    own_factor = jnp.exp(own - best)
    factors = [jnp.exp(stat - best) for stat in stats]
    total = own_factor
    for stat, factor in zip(stats, factors):
        total += factor * (
            pltpu.roll(stat, HEAD_DIM - heads, 1) + pltpu.roll(stat, HEAD_DIM - 2 * heads, 1)
        )
    share = 1.0 / total
    attention = wide(own_factor * share) * value_new[...].astype(F32).reshape(
        reqs, heads, HEAD_DIM
    )
    for part, factor in zip(parts, factors):
        attention += wide(factor * share) * part[pl.ds(0, rows), :].astype(F32).reshape(
            reqs, heads, HEAD_DIM
        )
    out[...] = attention.reshape(reqs, heads * HEAD_DIM).astype(BF16)


def project_kernel(place, near, far, w_out, *refs):
    outs, lines = refs[:-1], refs[-1]
    chips, reqs = near.shape[:2]
    block = outs[0].shape[0]

    @pl.when(pl.program_id(0) == 0)
    def _():
        for side, ref in enumerate((near, far)):
            for chip in range(chips):
                first = (place[0] ^ (2 * chip + side)) * reqs
                at = ((first // block) ^ place[1]) * block + first % block
                lines[pl.ds(pl.multiple_of(at, reqs), reqs), :] = ref[chip]

    product = jnp.dot(lines[...], w_out[...], preferred_element_type=F32)
    for a, out in enumerate(outs):
        out[...] = product[a * block : (a + 1) * block].astype(out.dtype)


def hidden_kernel(groups, place, *refs):
    pieces, (gain, w_gate, w_up, out, lines, square, gate, up) = refs[:-8], refs[-8:]
    step = pl.program_id(0)
    steps = len(pieces) // groups

    @pl.when(step == 0)
    def _():
        square[...] = jnp.zeros(square.shape, F32)
        gate[...] = jnp.zeros(gate.shape, F32)
        up[...] = jnp.zeros(up.shape, F32)

    for t in range(steps):

        @pl.when(step == t)
        def _():
            at = 0
            for piece in pieces[t * groups : (t + 1) * groups]:
                here = pl.ds(at, piece.shape[0])
                at += piece.shape[0]
                state = piece[...].astype(F32)
                square[here, :] += jnp.sum(state * state, axis=1, keepdims=True)
                lines[here, :] = (state * gain[0].astype(F32)).astype(BF16)

    contract = (((1,), (1,)), ((), ()))
    gate[...] += lax.dot_general(lines[...], w_gate[...], contract, preferred_element_type=F32)
    up[...] += lax.dot_general(lines[...], w_up[...], contract, preferred_element_type=F32)

    @pl.when(step == steps - 1)
    def _():
        width = steps * lines.shape[1]
        factor = lax.rsqrt(square[:, 0:1] * (1.0 / width) + NORM_EPS)
        g = gate[...] * factor
        out[...] = (g / (1.0 + jnp.exp(-g)) * (up[...] * factor)).astype(BF16)


def down_kernel(bounds, place, hidden, w_down, *outs):
    count = len(bounds)
    for side in range(2):

        @pl.when(pl.program_id(0) == side)
        def _():
            product = jnp.dot(hidden[...], w_down[...], preferred_element_type=F32)
            for (first, size), out in zip(bounds, outs[side * count : (side + 1) * count]):
                out[...] = product[first : first + size].astype(out.dtype)


def shards(
    queries, key_new, value_new, key_pool, value_pool, page_table, lengths, residual_in,
    w_out, norm_gain, w_gate, w_up, w_down,
):
    req_devices = lax.axis_size("req")
    head_devices = lax.axis_size("head")
    chips = req_devices // 2
    reqs = queries.shape[0]
    heads = queries.shape[1] // HEAD_DIM
    kv_local = key_new.shape[1] // HEAD_DIM
    group = heads // kv_local
    rows = reqs * heads
    pages, page_len = key_pool.shape[:2]
    me = lax.axis_index("req")
    place = jnp.stack([me, lax.axis_index("head")]).astype(jnp.int32)
    vmem = pl.BlockSpec(memory_space=pltpu.VMEM)

    inverse_rows = -(-(pages * req_devices // LO) // 16) * 16
    own_queries = queries.reshape(rows, HEAD_DIM)
    payload = pl.pallas_call(
        functools.partial(pack_kernel, page_len),
        out_shape=jax.ShapeDtypeStruct((rows + inverse_rows, HEAD_DIM), BF16),
        in_specs=[pl.BlockSpec(memory_space=pltpu.SMEM), vmem, vmem],
        out_specs=vmem,
        compiler_params=params(),
        name="pack",
    )(lengths, page_table, own_queries)
    near = jnp.stack([payload] + [swap(payload, "req", 2 * c) for c in range(1, chips)])
    far = swap(near, "req", 1)

    per_device = pages // LO
    inverse = jnp.concatenate([near[:, rows:], far[:, rows:]]).astype(jnp.int32)
    inverse = lax.dynamic_slice_in_dim(inverse, me * per_device, per_device, axis=1)
    found, held = inverse[..., :LO], inverse[..., LO:]
    first = (jnp.arange(req_devices, dtype=jnp.int32) * reqs - 1)[:, None, None]
    owners = jnp.sum(jnp.where(found > 0, found + first, 0), axis=0).reshape(pages)
    tokens = jnp.sum(held, axis=0).reshape(pages)

    step_pages = 16
    total_rows = rows * req_devices
    smem = pl.BlockSpec(memory_space=pltpu.SMEM)
    sent = jax.ShapeDtypeStruct((chips, rows + reqs, HEAD_DIM), BF16)
    near_out, far_out = pl.pallas_call(
        functools.partial(attend_kernel, heads, kv_local, reqs, step_pages),
        out_shape=(sent, sent),
        in_specs=[smem, smem, vmem, vmem, vmem, vmem],
        out_specs=[vmem, vmem],
        scratch_shapes=[
            pltpu.VMEM((total_rows, HEAD_DIM), F32),
            pltpu.VMEM((pages, heads, HEAD_DIM), F32),
            pltpu.VMEM((total_rows, HEAD_DIM), F32),
            pltpu.VMEM((total_rows, HEAD_DIM), F32),
            pltpu.VMEM((total_rows, HEAD_DIM), F32),
        ],
        compiler_params=params(16),
        name="attend",
    )(owners, tokens, near, far, in_vmem(key_pool), in_vmem(value_pool))

    parts = [near_out[0], swap(far_out[0], "req", 1)]
    for c in range(1, chips):
        parts += [swap(near_out[c], "req", 2 * c), swap(far_out[c], "req", 2 * c + 1)]

    def per_head(array):
        array = array.reshape(reqs, kv_local, 1, HEAD_DIM)
        array = jnp.broadcast_to(array, (reqs, kv_local, group, HEAD_DIM))
        return array.reshape(rows, HEAD_DIM)

    attention = pl.pallas_call(
        functools.partial(combine_kernel, heads),
        out_shape=jax.ShapeDtypeStruct((reqs, heads * HEAD_DIM), BF16),
        in_specs=[vmem] * (3 + len(parts)),
        out_specs=vmem,
        compiler_params=params(),
        name="combine",
    )(own_queries, per_head(key_new), per_head(value_new), *parts)

    near = jnp.stack([attention] + [swap(attention, "req", 2 * c) for c in range(1, chips)])
    far = swap(near, "req", 1)
    block = reqs * req_devices // head_devices
    columns = w_out.shape[1]
    step_columns = 256
    summed = pl.pallas_call(
        project_kernel,
        out_shape=[
            jax.ShapeDtypeStruct((block, columns), F32 if a == 0 else BF16)
            for a in range(head_devices)
        ],
        grid_spec=pltpu.PrefetchScalarGridSpec(
            num_scalar_prefetch=1,
            grid=(columns // step_columns,),
            in_specs=[
                whole(near.shape),
                whole(far.shape),
                pl.BlockSpec((w_out.shape[0], step_columns), lambda s, *_: (0, s)),
            ],
            out_specs=[pl.BlockSpec((block, step_columns), lambda s, *_: (0, s))] * head_devices,
            scratch_shapes=[pltpu.VMEM((block * head_devices, w_out.shape[0]), BF16)],
        ),
        compiler_params=params(),
        name="project",
    )(place, near, far, w_out)
    state = residual_in.astype(F32) + summed[0]
    for a in range(1, head_devices):
        state += swap(summed[a], "head", a).astype(F32)
    state = state.astype(BF16)

    pieces = {0: state}
    for a in range(1, head_devices):
        pieces[a] = swap(state, "head", a)
    if head_devices <= 4:
        row_groups = [[a] for a in range(head_devices)]
    else:
        row_groups = [[0], list(range(1, head_devices))]
    count = len(row_groups)
    grouped = [
        pieces[g[0]] if len(g) == 1 else jnp.concatenate([pieces[a] for a in g]) for g in row_groups
    ]
    near = [[x if c == 0 else swap(x, "req", 2 * c) for x in grouped] for c in range(chips)]
    far = [[swap(x, "req", 1) for x in line] for line in near]
    operands = []
    for c in range(chips):
        operands += near[c] + far[c]
    all_rows = block * head_devices
    hidden_width = w_gate.shape[1]
    hidden = pl.pallas_call(
        functools.partial(hidden_kernel, count),
        out_shape=jax.ShapeDtypeStruct((all_rows, hidden_width), BF16),
        grid_spec=pltpu.PrefetchScalarGridSpec(
            num_scalar_prefetch=1,
            grid=(req_devices,),
            in_specs=[whole(x.shape) for x in operands]
            + [
                pl.BlockSpec((1, 1, columns), lambda s, at: (at[0] ^ s, 0, 0)),
                pl.BlockSpec((hidden_width, columns), lambda s, at: (0, at[0] ^ s)),
                pl.BlockSpec((hidden_width, columns), lambda s, at: (0, at[0] ^ s)),
            ],
            out_specs=whole((all_rows, hidden_width)),
            scratch_shapes=[
                pltpu.VMEM((all_rows, columns), BF16),
                pltpu.VMEM((all_rows, HEAD_DIM), F32),
                pltpu.VMEM((all_rows, hidden_width), F32),
                pltpu.VMEM((all_rows, hidden_width), F32),
            ],
        ),
        compiler_params=params(),
        name="hidden",
    )(place, *operands, norm_gain.reshape(req_devices, 1, columns), w_gate.T, w_up.T)

    bounds, at = [], 0
    for g in row_groups:
        bounds.append((at, len(g) * block))
        at += len(g) * block
    shapes = [jax.ShapeDtypeStruct((size, columns), BF16) for _, size in bounds] * 2
    received = [[] for _ in row_groups]
    for c in list(range(1, chips)) + [0]:
        halves = pl.pallas_call(
            functools.partial(down_kernel, bounds),
            out_shape=shapes,
            grid_spec=pltpu.PrefetchScalarGridSpec(
                num_scalar_prefetch=1,
                grid=(2,),
                in_specs=[
                    whole(hidden.shape),
                    pl.BlockSpec(
                        (hidden_width, columns),
                        lambda s, at, c=c: (0, at[0] ^ (2 * c + 1 - s)),
                    ),
                ],
                out_specs=[whole(s.shape) for s in shapes],
            ),
            compiler_params=params(),
            name="down",
        )(place, hidden, w_down)
        for g in range(count):
            both = swap(halves[g], "req", 1).astype(F32) + halves[count + g].astype(F32)
            received[g].append(both if c == 0 else swap(both.astype(BF16), "req", 2 * c))
    output = state.astype(F32)
    for g, arrays in zip(row_groups, received):
        total = functools.reduce(jnp.add, [x.astype(F32) for x in arrays])
        for n, a in enumerate(g):
            part = total[n * block : (n + 1) * block]
            output += part if a == 0 else swap(part.astype(BF16), "head", a).astype(F32)
    return output.astype(BF16)


def solution(mesh):
    return jax.shard_map(
        shards,
        mesh=mesh,
        in_specs=(
            P("req", "head"),
            P("req", "head"),
            P("req", "head"),
            P("req", None, "head"),
            P("req", None, "head"),
            P("req", None),
            P("req"),
            P("head", "req"),
            P("head", "req"),
            P(),
            P(None, ("req", "head")),
            P(None, ("req", "head")),
            P(("req", "head"), None),
        ),
        out_specs=P("head", "req"),
        check_vma=False,
    )
```

```python
import functools
import math

import jax
import jax.numpy as jnp
from jax import lax
from jax.experimental import pallas as pl
from jax.experimental.pallas import tpu as pltpu
from jax.sharding import PartitionSpec as P

HEAD_DIM = 128
LO = 64
NEGATIVE_FILL = -1e30
NORM_EPS = 1e-06
BF16 = jnp.bfloat16
F32 = jnp.float32


def swap(array, axis, bits):
    size = lax.axis_size(axis)
    return lax.ppermute(array, axis, [(i, i ^ bits) for i in range(size)])


def whole(shape):
    return pl.BlockSpec(shape, lambda *_: (0,) * len(shape))


def in_vmem(array):
    return pltpu.with_memory_space_constraint(array, pltpu.VMEM)


def in_hbm(array):
    return pltpu.with_memory_space_constraint(array, pltpu.HBM)


def params(mebibytes=8):
    return pltpu.CompilerParams(vmem_limit_bytes=mebibytes * 1024 * 1024)


def stage_kernel(count, pieces, *refs):
    sources, outs, sems = refs[:count], refs[-1 - count : -1], refs[-1]
    copies = []
    for n in range(count):
        rows = sources[n].shape[0] // pieces // 16 * 16
        for p in range(pieces):
            size = rows if p < pieces - 1 else sources[n].shape[0] - rows * (pieces - 1)
            here = pl.ds(p * rows, size)
            copies.append(
                pltpu.make_async_copy(
                    sources[n].at[here], outs[n].at[here], sems.at[n * pieces + p]
                )
            )
    for copy in copies:
        copy.start()
    for copy in copies:
        copy.wait()


def staged(after, *arrays, name):
    pieces = 4
    size = sum(math.prod(array.shape) * 2 for array in arrays)
    return pl.pallas_call(
        functools.partial(stage_kernel, len(arrays), pieces),
        out_shape=[jax.ShapeDtypeStruct(array.shape, array.dtype) for array in arrays],
        in_specs=[pl.BlockSpec(memory_space=pl.ANY)] * (len(arrays) + len(after)),
        out_specs=[pl.BlockSpec(memory_space=pl.ANY)] * len(arrays),
        scratch_shapes=[pltpu.SemaphoreType.DMA((len(arrays) * pieces,))],
        compiler_params=params(1),
        cost_estimate=pl.CostEstimate(flops=0, bytes_accessed=size, transcendentals=0),
        name=name,
    )(*[in_hbm(array) for array in arrays], *after)


def split_kernel(count, steps, place, *refs):
    sources, outs, sems = refs[:count], refs[-1 - count * steps : -1], refs[-1]
    copies = []
    for n, source in enumerate(sources):
        width = outs[n * steps].shape[1]
        for t in range(steps):
            here = pl.ds(pl.multiple_of((place[0] ^ t) * width, width), width)
            k = n * steps + t
            copies.append(pltpu.make_async_copy(source.at[:, here], outs[k], sems.at[k]))
    for copy in copies:
        copy.start()
    for copy in copies:
        copy.wait()


def staged_blocks(place, steps, after, *arrays, name):
    anywhere = pl.BlockSpec(memory_space=pl.ANY)
    count = len(arrays)
    size = sum(math.prod(array.shape) * 2 for array in arrays)
    blocks = pl.pallas_call(
        functools.partial(split_kernel, count, steps),
        out_shape=[
            jax.ShapeDtypeStruct((array.shape[0], array.shape[1] // steps), array.dtype)
            for array in arrays
            for _ in range(steps)
        ],
        in_specs=[pl.BlockSpec(memory_space=pltpu.SMEM)] + [anywhere] * (count + len(after)),
        out_specs=[anywhere] * (count * steps),
        scratch_shapes=[pltpu.SemaphoreType.DMA((count * steps,))],
        compiler_params=params(1),
        cost_estimate=pl.CostEstimate(flops=0, bytes_accessed=size, transcendentals=0),
        name=name,
    )(place, *[in_hbm(array) for array in arrays], *after)
    return [blocks[n * steps : (n + 1) * steps] for n in range(count)]


def pack_kernel(page_len, place, lengths, table, queries, out):
    del place
    reqs, slots = table.shape
    query_rows = queries.shape[0]
    inverse_rows = out.shape[0] - query_rows
    high = lax.broadcasted_iota(jnp.int32, (inverse_rows, slots), 0)
    lane = lax.broadcasted_iota(jnp.int32, (2 * LO, slots), 0)
    first = lax.broadcasted_iota(jnp.int32, (1, slots), 1) * page_len
    total = jnp.zeros((inverse_rows, 2 * LO), F32)
    for r in range(reqs):
        ids = table[pl.ds(r, 1), :]
        tokens = jnp.clip(lengths[r] - first, 0, page_len)
        row_hit = jnp.where((ids >> 6) == high, 1.0, 0.0).astype(BF16)
        held = jnp.where(lane < LO, r + 1, tokens)
        lane_hit = jnp.where((ids & (LO - 1)) == (lane & (LO - 1)), held, 0).astype(F32).astype(BF16)
        total += lax.dot_general(
            row_hit, lane_hit, (((1,), (1,)), ((), ())), preferred_element_type=F32
        )
    out[pl.ds(0, query_rows), :] = queries[...]
    out[pl.ds(query_rows, inverse_rows), :] = total.astype(BF16)


def stack_kernel(count, *refs):
    out = refs[-1]
    at = 0
    for piece in refs[:count]:
        out[pl.ds(at, piece.shape[0]), :] = piece[...]
        at += piece.shape[0]


def stacked(pieces, *after):
    vmem = pl.BlockSpec(memory_space=pltpu.VMEM)
    rows = sum(piece.shape[0] for piece in pieces)
    return pl.pallas_call(
        functools.partial(stack_kernel, len(pieces)),
        out_shape=jax.ShapeDtypeStruct((rows, pieces[0].shape[1]), pieces[0].dtype),
        in_specs=[vmem] * len(pieces) + [pl.BlockSpec(memory_space=pl.ANY)] * len(after),
        out_specs=vmem,
        compiler_params=params(4),
        name="stack",
    )(*pieces, *after)


def attend_kernel(
    heads, kv_local, reqs, step_pages, place, near, far, keys, values, *refs
):
    outs, (query, score, top, weight, acc, found, index, sem) = refs[:-8], refs[-8:]
    chips = len(outs) // 2
    pages = keys.shape[0]
    steps = pages // step_pages
    rows = reqs * heads
    stride = near.shape[0] // chips
    inverse_rows = stride - rows
    group = heads // kv_local
    scale = 1.0 / math.sqrt(HEAD_DIM)
    lane = lax.broadcasted_iota(jnp.int32, (heads, HEAD_DIM), 1)
    head = lax.broadcasted_iota(jnp.int32, (heads, HEAD_DIM), 0)

    wanted = place[0] * (pages // LO) + lax.broadcasted_iota(jnp.int32, (8, inverse_rows), 0)
    pick = jnp.where(lax.broadcasted_iota(jnp.int32, (8, inverse_rows), 1) == wanted, 1.0, 0.0)
    half = lax.broadcasted_iota(jnp.int32, (8, 2 * LO), 1)
    total = jnp.zeros((8, 2 * LO), F32)
    for side, ref in enumerate((near, far)):
        for chip in range(chips):
            at = (side * chips + chip) * rows
            query[pl.ds(at, rows), :] = ref[pl.ds(chip * stride, rows), :].astype(F32)
            part = jnp.dot(
                pick.astype(BF16),
                ref[pl.ds(chip * stride + rows, inverse_rows), :],
                preferred_element_type=F32,
            )
            base = (side * chips + chip) * reqs - 1
            total += jnp.where((half < LO) & (part > 0.0), part + base, part)
    found[...] = total.astype(jnp.int32)
    copy = pltpu.make_async_copy(found, index, sem)
    copy.start()
    top[...] = jnp.full(top.shape, NEGATIVE_FILL, F32)
    weight[...] = jnp.zeros(weight.shape, F32)
    acc[...] = jnp.zeros(acc.shape, F32)
    copy.wait()

    def rows_of(page):
        return pl.ds(pl.multiple_of(index[page // LO, page % LO] * heads, heads), heads)

    def tokens_of(page):
        return index[page // LO, LO + page % LO]

    @pl.loop(0, steps)
    def _(step):
        first = step * step_pages
        scores = []
        for p in range(step_pages):
            q = query[rows_of(first + p), :]
            q = jnp.concatenate(
                [jnp.where(head // group == kv, q, 0.0) for kv in range(kv_local)], axis=1
            ).astype(BF16)
            s = lax.dot_general(
                q, keys[first + p], (((1,), (1,)), ((), ())), preferred_element_type=F32
            ) * scale
            scores.append(jnp.where(lane < tokens_of(first + p), s, NEGATIVE_FILL))
        best = [jnp.max(s, axis=1, keepdims=True) for s in scores]
        for p in range(step_pages):
            score[first + p] = scores[p]
        for p in range(step_pages):
            at = rows_of(first + p)
            top[at, :] = jnp.maximum(top[at, :], best[p])

    top[...] = top[...].astype(BF16).astype(F32)

    @pl.loop(0, steps)
    def _(step):
        first = step * step_pages
        sums, parts = [], []
        for p in range(step_pages):
            page = first + p
            w = jnp.exp(score[page] - top[rows_of(page), :])
            w = jnp.where(lane < tokens_of(page), w, 0.0).astype(BF16)
            a = jnp.dot(w, values[page], preferred_element_type=F32)
            part = a[:, :HEAD_DIM]
            for kv in range(1, kv_local):
                part = jnp.where(
                    head // group == kv, a[:, kv * HEAD_DIM : (kv + 1) * HEAD_DIM], part
                )
            parts.append(part)
            sums.append(jnp.sum(w.astype(F32), axis=1, keepdims=True))
        for p in range(step_pages):
            at = rows_of(first + p)
            acc[at, :] += parts[p]
            weight[at, :] += sums[p]

    lane3 = lax.broadcasted_iota(jnp.int32, (reqs, heads, HEAD_DIM), 2)
    head3 = lax.broadcasted_iota(jnp.int32, (reqs, heads, HEAD_DIM), 1)
    for n, out in enumerate(outs):
        at = pl.ds(n * rows, rows)
        out[pl.ds(0, rows), :] = acc[at, :].astype(BF16)
        t = top[at, :].reshape(reqs, heads, HEAD_DIM)
        s = weight[at, :].reshape(reqs, heads, HEAD_DIM)
        s_high = s.astype(BF16).astype(F32)
        stats = jnp.where(lane3 == head3 + 2 * heads, s - s_high, 0.0)
        stats = jnp.where(lane3 == head3 + heads, s_high, stats)
        stats = jnp.where(lane3 == head3, t, stats)
        out[pl.ds(rows, reqs), :] = jnp.sum(stats, axis=1).astype(BF16)


def combine_kernel(heads, queries, key_new, value_new, *refs):
    parts, out = refs[2:-1], refs[-1]
    rows = queries.shape[0]
    reqs = rows // heads
    lane3 = lax.broadcasted_iota(jnp.int32, (reqs, heads, HEAD_DIM), 2)
    head3 = lax.broadcasted_iota(jnp.int32, (reqs, heads, HEAD_DIM), 1)
    diagonal = lane3 == head3

    def narrow(array):
        return jnp.sum(jnp.where(diagonal, array.reshape(reqs, heads, HEAD_DIM), 0.0), axis=1)

    def wide(array):
        return jnp.sum(jnp.where(diagonal, array[:, None, :], 0.0), axis=2, keepdims=True)

    def per_head(ref):
        kv_local = ref.shape[1] // HEAD_DIM
        array = ref[...].astype(F32)
        return jnp.concatenate(
            [
                jnp.broadcast_to(
                    array[:, None, kv * HEAD_DIM : (kv + 1) * HEAD_DIM],
                    (reqs, heads // kv_local, HEAD_DIM),
                )
                for kv in range(kv_local)
            ],
            axis=1,
        )

    own = queries[...].astype(F32).reshape(reqs, heads, HEAD_DIM) * per_head(key_new)
    own = jnp.sum(own, axis=2, keepdims=True) * (1.0 / math.sqrt(HEAD_DIM))
    own = narrow(jnp.broadcast_to(own, (reqs, heads, HEAD_DIM)))
    stats = [part[pl.ds(rows, reqs), :].astype(F32) for part in parts]
    best = functools.reduce(jnp.maximum, stats, own)
    own_factor = jnp.exp(own - best)
    factors = [jnp.exp(stat - best) for stat in stats]
    total = own_factor
    for stat, factor in zip(stats, factors):
        total += factor * (
            pltpu.roll(stat, HEAD_DIM - heads, 1) + pltpu.roll(stat, HEAD_DIM - 2 * heads, 1)
        )
    share = 1.0 / total
    attention = wide(own_factor * share) * per_head(value_new)
    for part, factor in zip(parts, factors):
        attention += wide(factor * share) * part[pl.ds(0, rows), :].astype(F32).reshape(
            reqs, heads, HEAD_DIM
        )
    out[...] = attention.reshape(reqs, heads * HEAD_DIM).astype(BF16)


def project_kernel(chips, place, *refs):
    near, far, w_out = refs[:chips], refs[chips : 2 * chips], refs[2 * chips]
    outs, lines = refs[2 * chips + 1 : -1], refs[-1]
    reqs = near[0].shape[0]
    block = outs[0].shape[0]

    for side, line in enumerate((near, far)):
        for chip in range(chips):
            first = (place[0] ^ (2 * chip + side)) * reqs
            at = ((first // block) ^ place[1]) * block + first % block
            lines[pl.ds(pl.multiple_of(at, reqs), reqs), :] = line[chip][...]

    product = jnp.dot(lines[...], w_out[...], preferred_element_type=F32)
    for a, out in enumerate(outs):
        out[...] = product[a * block : (a + 1) * block].astype(out.dtype)


def state_kernel(ready, residual, *refs):
    del ready
    total = residual[...].astype(F32)
    for part in refs[:-1]:
        total += part[...].astype(F32)
    refs[-1][...] = total.astype(BF16)


def gain_kernel(gain, out):
    out[...] = gain[...].astype(F32)


def hidden_kernel(groups, chip, last, total_width, place, *refs):
    pieces, refs = refs[: 2 * groups], refs[2 * groups :]
    gain, w_gate, w_up = refs[0], refs[1:3], refs[3:5]
    before = refs[5:8] if chip else None
    outs, lines = refs[8 if chip else 5 : -1], refs[-1]
    width = lines.shape[2]
    rows, units = outs[0].shape
    contract = (((1,), (1,)), ((), ()))
    square = [None] * groups
    for side in range(2):
        scale = gain[pl.ds(place[0] ^ (2 * chip + side), 1), :]
        at = 0
        for n, piece in enumerate(pieces[side * groups : (side + 1) * groups]):
            state = piece[...].astype(F32)
            part = jnp.sum(state * state, axis=1, keepdims=True)
            square[n] = part if side == 0 else square[n] + part
            lines[side, pl.ds(at, piece.shape[0]), :] = (state * scale).astype(BF16)
            at += piece.shape[0]
    square = jnp.broadcast_to(jnp.concatenate(square, axis=0), (rows, HEAD_DIM))
    if before is not None:
        square = square + before[2][...]
    factor = lax.rsqrt(square[:, 0:1] * (1.0 / total_width) + NORM_EPS)
    for first in range(0, units, 512):
        here = slice(first, min(first + 512, units))
        sums = []
        for n, weight in enumerate((w_gate, w_up)):
            total = None if before is None else before[n][:, here]
            for side in range(2):
                part = lax.dot_general(
                    lines[side], weight[side][here, :], contract, preferred_element_type=F32
                )
                total = part if total is None else total + part
            sums.append(total)
        if last:
            gate = sums[0] * factor
            outs[0][:, here] = (gate / (1.0 + jnp.exp(-gate)) * (sums[1] * factor)).astype(BF16)
        else:
            outs[0][:, here], outs[1][:, here] = sums
    if not last:
        outs[2][...] = square


def down_kernel(bounds, hidden, far, near, *outs):
    count = len(bounds)
    for side, weight in enumerate((far, near)):
        product = jnp.dot(hidden[...], weight[...], preferred_element_type=F32)
        for (first, size), out in zip(bounds, outs[side * count : (side + 1) * count]):
            out[...] = product[first : first + size].astype(out.dtype)


def shards(
    queries, key_new, value_new, key_pool, value_pool, page_table, lengths, residual_in,
    w_out, norm_gain, w_gate, w_up, w_down,
):
    req_devices = lax.axis_size("req")
    head_devices = lax.axis_size("head")
    chips = req_devices // 2
    reqs = queries.shape[0]
    heads = queries.shape[1] // HEAD_DIM
    kv_local = key_new.shape[1] // HEAD_DIM
    hidden_width = w_down.shape[0]
    rows = reqs * heads
    pages, page_len = key_pool.shape[:2]
    me = lax.axis_index("req")
    place = jnp.stack([me, lax.axis_index("head")]).astype(jnp.int32)
    vmem = pl.BlockSpec(memory_space=pltpu.VMEM)
    smem = pl.BlockSpec(memory_space=pltpu.SMEM)

    inverse_rows = -(-(pages * req_devices // LO) // 16) * 16
    own_queries = queries.reshape(rows, HEAD_DIM)
    payload = pl.pallas_call(
        functools.partial(pack_kernel, page_len),
        out_shape=jax.ShapeDtypeStruct((rows + inverse_rows, HEAD_DIM), BF16),
        in_specs=[smem, smem, vmem, vmem],
        out_specs=vmem,
        compiler_params=params(),
        name="pack",
    )(place, lengths, page_table, own_queries)
    near = [payload] + [swap(payload, "req", 2 * c) for c in range(1, chips)]
    columns = w_out.shape[1]
    gain = pl.pallas_call(
        gain_kernel,
        out_shape=jax.ShapeDtypeStruct((req_devices, columns), F32),
        in_specs=[vmem],
        out_specs=vmem,
        compiler_params=params(1),
        name="gain",
    )(norm_gain.reshape(req_devices, columns))
    keys, values = staged([payload, gain], key_pool, value_pool, name="stage_pools")
    near = stacked(near, keys)
    far = swap(near, "req", 1)

    step_pages = 16
    total_rows = rows * req_devices
    anywhere = pl.BlockSpec(memory_space=pl.ANY)
    sent = jax.ShapeDtypeStruct((rows + reqs, HEAD_DIM), BF16)
    partials = pl.pallas_call(
        functools.partial(attend_kernel, heads, kv_local, reqs, step_pages),
        out_shape=[sent] * req_devices,
        in_specs=[smem, vmem, vmem, vmem, vmem],
        out_specs=[vmem] * req_devices,
        scratch_shapes=[
            pltpu.VMEM((total_rows, HEAD_DIM), F32),
            pltpu.VMEM((pages, heads, HEAD_DIM), F32),
            pltpu.VMEM((total_rows, HEAD_DIM), F32),
            pltpu.VMEM((total_rows, HEAD_DIM), F32),
            pltpu.VMEM((total_rows, HEAD_DIM), F32),
            pltpu.VMEM((8, 2 * LO), jnp.int32),
            pltpu.SMEM((8, 2 * LO), jnp.int32),
            pltpu.SemaphoreType.DMA,
        ],
        compiler_params=params(16),
        name="attend",
    )(place, near, far, keys, values)
    w_out, = staged([partials[0]], w_out, name="stage_out")
    w_gate, w_up = staged_blocks(
        place, req_devices, [partials[0]], w_gate.T, w_up.T, name="stage_hidden"
    )

    near_out, far_out = partials[:chips], partials[chips:]
    parts = [near_out[0], swap(far_out[0], "req", 1)]
    for c in range(1, chips):
        parts += [swap(near_out[c], "req", 2 * c), swap(far_out[c], "req", 2 * c + 1)]
    attention = pl.pallas_call(
        functools.partial(combine_kernel, heads),
        out_shape=jax.ShapeDtypeStruct((reqs, heads * HEAD_DIM), BF16),
        in_specs=[vmem] * 3 + [anywhere] * 2 + [vmem] * len(parts),
        out_specs=vmem,
        compiler_params=params(4),
        name="combine",
    )(own_queries, key_new, value_new, w_gate[0], w_out, *parts)

    near = [attention] + [swap(attention, "req", 2 * c) for c in range(1, chips)]
    far = [swap(x, "req", 1) for x in near]
    block = reqs * req_devices // head_devices
    summed = pl.pallas_call(
        functools.partial(project_kernel, chips),
        out_shape=[
            jax.ShapeDtypeStruct((block, columns), F32 if a == 0 else BF16)
            for a in range(head_devices)
        ],
        in_specs=[smem] + [vmem] * (2 * chips + 1),
        out_specs=[vmem] * head_devices,
        scratch_shapes=[pltpu.VMEM((block * head_devices, w_out.shape[0]), BF16)],
        compiler_params=params(5),
        name="project",
    )(place, *near, *far, w_out)
    w_down, = staged_blocks(place, req_devices, [summed[0]], w_down, name="stage_down")
    terms = [summed[0]] + [swap(summed[a], "head", a) for a in range(1, head_devices)]
    state = pl.pallas_call(
        state_kernel,
        out_shape=jax.ShapeDtypeStruct((block, columns), BF16),
        in_specs=[anywhere] + [vmem] * (1 + head_devices),
        out_specs=vmem,
        compiler_params=params(4),
        name="state",
    )(w_down[0], residual_in, *terms)

    pieces = {0: state}
    for a in range(1, head_devices):
        pieces[a] = swap(state, "head", a)
    row_groups = [[0], [1], list(range(2, head_devices))]
    count = len(row_groups)
    grouped = [
        pieces[g[0]] if len(g) == 1 else stacked([pieces[a] for a in g]) for g in row_groups
    ]
    near = [[x if c == 0 else swap(x, "req", 2 * c) for x in grouped] for c in range(chips)]
    far = [[swap(x, "req", 1) for x in line] for line in near]
    all_rows = block * head_devices
    sums = []
    for c in range(chips):
        last = c == chips - 1
        sums = pl.pallas_call(
            functools.partial(hidden_kernel, count, c, last, columns * req_devices),
            out_shape=[jax.ShapeDtypeStruct((all_rows, hidden_width), BF16)]
            if last
            else [
                jax.ShapeDtypeStruct((all_rows, hidden_width), F32),
                jax.ShapeDtypeStruct((all_rows, hidden_width), F32),
                jax.ShapeDtypeStruct((all_rows, HEAD_DIM), F32),
            ],
            in_specs=[smem] + [vmem] * (2 * count + 5 + len(sums)),
            out_specs=[vmem] if last else [vmem] * 3,
            scratch_shapes=[pltpu.VMEM((2, all_rows, columns), BF16)],
            input_output_aliases={} if c == 0 or last else {2 * count + 6 + n: n for n in range(3)},
            compiler_params=params(5),
            cost_estimate=pl.CostEstimate(
                flops=8 * all_rows * columns * hidden_width, bytes_accessed=0, transcendentals=0
            ),
            name="hidden",
        )(
            place, *near[c], *far[c], gain, *w_gate[2 * c : 2 * c + 2], *w_up[2 * c : 2 * c + 2], *sums
        )
    hidden, = sums

    bounds, at = [], 0
    for g in row_groups:
        bounds.append((at, len(g) * block))
        at += len(g) * block
    shapes = [jax.ShapeDtypeStruct((size, columns), BF16) for _, size in bounds] * 2
    received = [[] for _ in row_groups]
    for c in list(range(1, chips)) + [0]:
        halves = pl.pallas_call(
            functools.partial(down_kernel, bounds),
            out_shape=shapes,
            in_specs=[vmem] * 3,
            out_specs=[vmem] * len(shapes),
            compiler_params=params(5),
            cost_estimate=pl.CostEstimate(
                flops=4 * all_rows * columns * hidden_width, bytes_accessed=0, transcendentals=0
            ),
            name="down",
        )(hidden, w_down[2 * c + 1], w_down[2 * c])
        for g in range(count):
            both = swap(halves[g], "req", 1).astype(F32) + halves[count + g].astype(F32)
            received[g].append(both if c == 0 else swap(both.astype(BF16), "req", 2 * c))
    output = state.astype(F32)
    for g, arrays in zip(row_groups, received):
        total = functools.reduce(jnp.add, [x.astype(F32) for x in arrays])
        for n, a in enumerate(g):
            part = total[n * block : (n + 1) * block]
            output += part if a == 0 else swap(part.astype(BF16), "head", a).astype(F32)
    return output.astype(BF16)


def solution(mesh):
    return jax.shard_map(
        shards,
        mesh=mesh,
        in_specs=(
            P("req", "head"),
            P("req", "head"),
            P("req", "head"),
            P("req", None, "head"),
            P("req", None, "head"),
            P("req", None),
            P("req"),
            P("head", "req"),
            P("head", "req"),
            P(),
            P(None, ("req", "head")),
            P(None, ("req", "head")),
            P(("req", "head"), None),
        ),
        out_specs=P("head", "req"),
        check_vma=False,
    )
```

```python
import functools
import math

import jax
import jax.numpy as jnp
from jax import lax
from jax.experimental import pallas as pl
from jax.experimental.pallas import tpu as pltpu
from jax.sharding import PartitionSpec as P

HEAD_DIM = 128
LO = 64
NEGATIVE_FILL = -1e30
NORM_EPS = 1e-06
BF16 = jnp.bfloat16
F32 = jnp.float32


def swap(array, axis, bits):
    size = lax.axis_size(axis)
    return lax.ppermute(array, axis, [(i, i ^ bits) for i in range(size)])


def whole(shape):
    return pl.BlockSpec(shape, lambda *_: (0,) * len(shape))


def in_vmem(array):
    return pltpu.with_memory_space_constraint(array, pltpu.VMEM)


def in_hbm(array):
    return pltpu.with_memory_space_constraint(array, pltpu.HBM)


def params(mebibytes=8):
    return pltpu.CompilerParams(vmem_limit_bytes=mebibytes * 1024 * 1024)


def stage_kernel(count, pieces, *refs):
    sources, outs, sems = refs[:count], refs[-1 - count : -1], refs[-1]
    copies = []
    for n in range(count):
        rows = sources[n].shape[0] // pieces // 16 * 16
        for p in range(pieces):
            size = rows if p < pieces - 1 else sources[n].shape[0] - rows * (pieces - 1)
            here = pl.ds(p * rows, size)
            copies.append(
                pltpu.make_async_copy(
                    sources[n].at[here], outs[n].at[here], sems.at[n * pieces + p]
                )
            )
    for copy in copies:
        copy.start()
    for copy in copies:
        copy.wait()


def staged(after, *arrays, name):
    pieces = 4
    size = sum(math.prod(array.shape) * 2 for array in arrays)
    return pl.pallas_call(
        functools.partial(stage_kernel, len(arrays), pieces),
        out_shape=[jax.ShapeDtypeStruct(array.shape, array.dtype) for array in arrays],
        in_specs=[pl.BlockSpec(memory_space=pl.ANY)] * (len(arrays) + len(after)),
        out_specs=[pl.BlockSpec(memory_space=pl.ANY)] * len(arrays),
        scratch_shapes=[pltpu.SemaphoreType.DMA((len(arrays) * pieces,))],
        compiler_params=params(1),
        cost_estimate=pl.CostEstimate(flops=0, bytes_accessed=size, transcendentals=0),
        name=name,
    )(*[in_hbm(array) for array in arrays], *after)


def split_kernel(count, wanted, place, *refs):
    sources, outs, sems = refs[:count], refs[-1 - len(wanted) : -1], refs[-1]
    copies = []
    for k, ((n, t), out) in enumerate(zip(wanted, outs)):
        width = out.shape[1]
        here = pl.ds(pl.multiple_of((place[0] ^ t) * width, width), width)
        copies.append(pltpu.make_async_copy(sources[n].at[:, here], out, sems.at[k]))
    for copy in copies:
        copy.start()
    for copy in copies:
        copy.wait()


def staged_blocks(place, width, after, arrays, wanted, name):
    anywhere = pl.BlockSpec(memory_space=pl.ANY)
    shapes = [jax.ShapeDtypeStruct((arrays[n].shape[0], width), arrays[n].dtype) for n, _ in wanted]
    return pl.pallas_call(
        functools.partial(split_kernel, len(arrays), wanted),
        out_shape=shapes,
        in_specs=[pl.BlockSpec(memory_space=pltpu.SMEM)] + [anywhere] * (len(arrays) + len(after)),
        out_specs=[anywhere] * len(wanted),
        scratch_shapes=[pltpu.SemaphoreType.DMA((len(wanted),))],
        compiler_params=params(1),
        cost_estimate=pl.CostEstimate(
            flops=0,
            bytes_accessed=sum(2 * math.prod(shape.shape) for shape in shapes),
            transcendentals=0,
        ),
        name=name,
    )(place, *[in_hbm(array) for array in arrays], *after)


def pack_kernel(page_len, place, lengths, table, queries, out):
    del place
    reqs, slots = table.shape
    query_rows = queries.shape[0] * queries.shape[1] // HEAD_DIM
    inverse_rows = out.shape[0] - query_rows
    high = lax.broadcasted_iota(jnp.int32, (inverse_rows, slots), 0)
    lane = lax.broadcasted_iota(jnp.int32, (2 * LO, slots), 0)
    first = lax.broadcasted_iota(jnp.int32, (1, slots), 1) * page_len
    total = jnp.zeros((inverse_rows, 2 * LO), F32)
    for r in range(reqs):
        ids = table[pl.ds(r, 1), :]
        tokens = jnp.clip(lengths[r] - first, 0, page_len)
        row_hit = jnp.where((ids >> 6) == high, 1.0, 0.0).astype(BF16)
        held = jnp.where(lane < LO, r + 1, tokens)
        lane_hit = jnp.where((ids & (LO - 1)) == (lane & (LO - 1)), held, 0).astype(F32).astype(BF16)
        total += lax.dot_general(
            row_hit, lane_hit, (((1,), (1,)), ((), ())), preferred_element_type=F32
        )
    own = queries[...].astype(F32).reshape(query_rows, HEAD_DIM)
    out[pl.ds(0, query_rows), :] = own.astype(BF16)
    out[pl.ds(query_rows, inverse_rows), :] = total.astype(BF16)


def stack_kernel(count, *refs):
    out = refs[-1]
    at = 0
    for piece in refs[:count]:
        out[pl.ds(at, piece.shape[0]), :] = piece[...]
        at += piece.shape[0]


def stacked(pieces, *after):
    vmem = pl.BlockSpec(memory_space=pltpu.VMEM)
    rows = sum(piece.shape[0] for piece in pieces)
    return pl.pallas_call(
        functools.partial(stack_kernel, len(pieces)),
        out_shape=jax.ShapeDtypeStruct((rows, pieces[0].shape[1]), pieces[0].dtype),
        in_specs=[vmem] * len(pieces) + [pl.BlockSpec(memory_space=pl.ANY)] * len(after),
        out_specs=vmem,
        compiler_params=params(4),
        name="stack",
    )(*pieces, *after)


def rows_kernel(first, source, out):
    out[...] = source[pl.ds(first, out.shape[0]), :]


def cut_rows(array, first, size):
    vmem = pl.BlockSpec(memory_space=pltpu.VMEM)
    return pl.pallas_call(
        functools.partial(rows_kernel, first),
        out_shape=jax.ShapeDtypeStruct((size, array.shape[1]), array.dtype),
        in_specs=[vmem],
        out_specs=vmem,
        compiler_params=params(2),
        name="rows",
    )(array)


def attend_kernel(
    devices, heads, kv_local, reqs, step_pages, place, near, far, keys, value_pool, *refs
):
    w_out, w_up, refs = refs[0], refs[1], refs[2:]
    outs, refs = refs[:-11], refs[-11:]
    outs, w_out_copy, w_up_copies = outs[:devices], outs[devices], outs[devices + 1 :]
    query, score, top, weight, acc, found, index, values, sem, value_sem, out_sem = refs
    chips = len(outs) // 2
    pages = keys.shape[0]
    steps = pages // step_pages
    rows = reqs * heads
    stride = near.shape[0] // chips
    inverse_rows = stride - rows
    group = heads // kv_local
    scale = 1.0 / math.sqrt(HEAD_DIM)
    lane = lax.broadcasted_iota(jnp.int32, (heads, HEAD_DIM), 1)
    head = lax.broadcasted_iota(jnp.int32, (heads, HEAD_DIM), 0)

    cut = pages // value_sem.shape[0]
    loads = [
        pltpu.make_async_copy(
            value_pool.at[pl.ds(n * cut, cut)], values.at[pl.ds(n * cut, cut)], value_sem.at[n]
        )
        for n in range(value_sem.shape[0])
    ]
    for load in loads:
        load.start()

    wanted = place[0] * (pages // LO) + lax.broadcasted_iota(jnp.int32, (8, inverse_rows), 0)
    pick = jnp.where(lax.broadcasted_iota(jnp.int32, (8, inverse_rows), 1) == wanted, 1.0, 0.0)
    half = lax.broadcasted_iota(jnp.int32, (8, 2 * LO), 1)
    total = jnp.zeros((8, 2 * LO), F32)
    for side, ref in enumerate((near, far)):
        for chip in range(chips):
            at = (side * chips + chip) * rows
            query[pl.ds(at, rows), :] = ref[pl.ds(chip * stride, rows), :].astype(F32)
            part = jnp.dot(
                pick.astype(BF16),
                ref[pl.ds(chip * stride + rows, inverse_rows), :],
                preferred_element_type=F32,
            )
            base = (side * chips + chip) * reqs - 1
            total += jnp.where((half < LO) & (part > 0.0), part + base, part)
    found[...] = total.astype(jnp.int32)
    copy = pltpu.make_async_copy(found, index, sem)
    copy.start()
    top[...] = jnp.full(top.shape, NEGATIVE_FILL, F32)
    weight[...] = jnp.zeros(weight.shape, F32)
    acc[...] = jnp.zeros(acc.shape, F32)
    copy.wait()

    def rows_of(page):
        return pl.ds(pl.multiple_of(index[page // LO, page % LO] * heads, heads), heads)

    def tokens_of(page):
        return index[page // LO, LO + page % LO]

    @pl.loop(0, steps)
    def _(step):
        first = step * step_pages
        scores = []
        for p in range(step_pages):
            q = query[rows_of(first + p), :]
            q = jnp.concatenate(
                [jnp.where(head // group == kv, q, 0.0) for kv in range(kv_local)], axis=1
            ).astype(BF16)
            s = lax.dot_general(
                q, keys[first + p], (((1,), (1,)), ((), ())), preferred_element_type=F32
            ) * scale
            scores.append(jnp.where(lane < tokens_of(first + p), s, NEGATIVE_FILL))
        best = [jnp.max(s, axis=1, keepdims=True) for s in scores]
        for p in range(step_pages):
            score[first + p] = scores[p]
        for p in range(step_pages):
            at = rows_of(first + p)
            top[at, :] = jnp.maximum(top[at, :], best[p])

    top[...] = top[...].astype(BF16).astype(F32)
    for load in loads:
        load.wait()
    weight_loads = [pltpu.make_async_copy(w_out, w_out_copy, out_sem.at[len(w_up_copies)])]
    for t, copied in enumerate(w_up_copies):
        width = copied.shape[1]
        here = pl.ds(pl.multiple_of((place[0] ^ t) * width, width), width)
        weight_loads.append(pltpu.make_async_copy(w_up.at[:, here], copied, out_sem.at[t]))
    for load in weight_loads:
        load.start()

    @pl.loop(0, steps)
    def _(step):
        first = step * step_pages
        sums, parts = [], []
        for p in range(step_pages):
            page = first + p
            w = jnp.exp(score[page] - top[rows_of(page), :])
            w = jnp.where(lane < tokens_of(page), w, 0.0).astype(BF16)
            a = jnp.dot(w, values[page], preferred_element_type=F32)
            part = a[:, :HEAD_DIM]
            for kv in range(1, kv_local):
                part = jnp.where(
                    head // group == kv, a[:, kv * HEAD_DIM : (kv + 1) * HEAD_DIM], part
                )
            parts.append(part)
            sums.append(jnp.sum(w.astype(F32), axis=1, keepdims=True))
        for p in range(step_pages):
            at = rows_of(first + p)
            acc[at, :] += parts[p]
            weight[at, :] += sums[p]

    lane3 = lax.broadcasted_iota(jnp.int32, (reqs, heads, HEAD_DIM), 2)
    head3 = lax.broadcasted_iota(jnp.int32, (reqs, heads, HEAD_DIM), 1)
    for n, out in enumerate(outs):
        at = pl.ds(n * rows, rows)
        out[pl.ds(0, rows), :] = acc[at, :].astype(BF16)
        t = top[at, :].reshape(reqs, heads, HEAD_DIM)
        s = weight[at, :].reshape(reqs, heads, HEAD_DIM)
        s_high = s.astype(BF16).astype(F32)
        stats = jnp.where(lane3 == head3 + 2 * heads, s - s_high, 0.0)
        stats = jnp.where(lane3 == head3 + heads, s_high, stats)
        stats = jnp.where(lane3 == head3, t, stats)
        out[pl.ds(rows, reqs), :] = jnp.sum(stats, axis=1).astype(BF16)
    for load in weight_loads:
        load.wait()


def combine_kernel(heads, queries, key_new, value_new, *refs):
    parts, out = refs[1:-1], refs[-1]
    reqs = key_new.shape[0]
    rows = reqs * heads
    lane3 = lax.broadcasted_iota(jnp.int32, (reqs, heads, HEAD_DIM), 2)
    head3 = lax.broadcasted_iota(jnp.int32, (reqs, heads, HEAD_DIM), 1)
    diagonal = lane3 == head3

    def narrow(array):
        return jnp.sum(jnp.where(diagonal, array.reshape(reqs, heads, HEAD_DIM), 0.0), axis=1)

    def wide(array):
        return jnp.sum(jnp.where(diagonal, array[:, None, :], 0.0), axis=2, keepdims=True)

    def per_head(ref):
        kv_local = ref.shape[1] // HEAD_DIM
        array = ref[...].astype(F32)
        return jnp.concatenate(
            [
                jnp.broadcast_to(
                    array[:, None, kv * HEAD_DIM : (kv + 1) * HEAD_DIM],
                    (reqs, heads // kv_local, HEAD_DIM),
                )
                for kv in range(kv_local)
            ],
            axis=1,
        )

    own = queries[pl.ds(0, rows), :].astype(F32).reshape(reqs, heads, HEAD_DIM) * per_head(key_new)
    own = jnp.sum(own, axis=2, keepdims=True) * (1.0 / math.sqrt(HEAD_DIM))
    own = narrow(jnp.broadcast_to(own, (reqs, heads, HEAD_DIM)))
    stats = [part[pl.ds(rows, reqs), :].astype(F32) for part in parts]
    best = functools.reduce(jnp.maximum, stats, own)
    own_factor = jnp.exp(own - best)
    factors = [jnp.exp(stat - best) for stat in stats]
    total = own_factor
    for stat, factor in zip(stats, factors):
        total += factor * (
            pltpu.roll(stat, HEAD_DIM - heads, 1) + pltpu.roll(stat, HEAD_DIM - 2 * heads, 1)
        )
    share = 1.0 / total
    attention = wide(own_factor * share) * per_head(value_new)
    for part, factor in zip(parts, factors):
        attention += wide(factor * share) * part[pl.ds(0, rows), :].astype(F32).reshape(
            reqs, heads, HEAD_DIM
        )
    out[...] = attention.reshape(reqs, heads * HEAD_DIM).astype(BF16)


def project_kernel(chips, place, *refs):
    near, far, w_out = refs[:chips], refs[chips : 2 * chips], refs[2 * chips]
    outs, lines = refs[2 * chips + 1 : -1], refs[-1]
    reqs = near[0].shape[0]
    block = outs[0].shape[0]

    for side, line in enumerate((near, far)):
        for chip in range(chips):
            first = (place[0] ^ (2 * chip + side)) * reqs
            at = ((first // block) ^ place[1]) * block + first % block
            lines[pl.ds(pl.multiple_of(at, reqs), reqs), :] = line[chip][...]

    product = jnp.dot(lines[...], w_out[...], preferred_element_type=F32)
    for a, out in enumerate(outs):
        out[...] = product[a * block : (a + 1) * block].astype(out.dtype)


def state_kernel(ready, residual, *refs):
    del ready
    total = residual[...].astype(F32)
    for part in refs[:-1]:
        total += part[...].astype(F32)
    refs[-1][...] = total.astype(BF16)


def gain_kernel(gain, out):
    out[...] = gain[...].astype(F32)


def hidden_kernel(groups, chip, last, total_width, place, *refs):
    pieces, refs = refs[: 2 * groups], refs[2 * groups :]
    gain, w_gate, w_up = refs[0], refs[1:3], refs[3:5]
    before = refs[5:8] if chip else None
    outs, lines = refs[8 if chip else 5 : -1], refs[-1]
    width = lines.shape[2]
    rows, units = outs[0].shape
    contract = (((1,), (1,)), ((), ()))
    square = [None] * groups
    for side in range(2):
        scale = gain[pl.ds(place[0] ^ (2 * chip + side), 1), :]
        at = 0
        for n, piece in enumerate(pieces[side * groups : (side + 1) * groups]):
            state = piece[...].astype(F32)
            part = jnp.sum(state * state, axis=1, keepdims=True)
            square[n] = part if side == 0 else square[n] + part
            lines[side, pl.ds(at, piece.shape[0]), :] = (state * scale).astype(BF16)
            at += piece.shape[0]
    square = jnp.broadcast_to(jnp.concatenate(square, axis=0), (rows, HEAD_DIM))
    if before is not None:
        square = square + before[2][...]
    factor = lax.rsqrt(square[:, 0:1] * (1.0 / total_width) + NORM_EPS)
    for first in range(0, units, 512):
        here = slice(first, min(first + 512, units))
        sums = []
        for n, weight in enumerate((w_gate, w_up)):
            total = None if before is None else before[n][:, here]
            for side in range(2):
                part = lax.dot_general(
                    lines[side], weight[side][here, :], contract, preferred_element_type=F32
                )
                total = part if total is None else total + part
            sums.append(total)
        if last:
            gate = sums[0] * factor
            outs[0][:, here] = (gate / (1.0 + jnp.exp(-gate)) * (sums[1] * factor)).astype(BF16)
        else:
            outs[0][:, here], outs[1][:, here] = sums
    if not last:
        outs[2][...] = square


def down_kernel(hidden, far, near, *refs):
    far_out, near_out = refs[-2:]
    for weight, out in ((far, far_out), (near, near_out)):
        out[...] = jnp.dot(hidden[...], weight[...], preferred_element_type=F32).astype(out.dtype)


def merge_kernel(block, layout, passed, mine, other, *refs):
    outs = refs[len(refs) - len(layout) :]
    for out, blocks in zip(outs, layout):
        for n, a in enumerate(blocks):
            here = pl.ds(a * block, block)
            total = mine[here, :] + other[here, :].astype(F32)
            if a in passed:
                total += refs[0][pl.ds(passed.index(a) * block, block), :].astype(F32)
            out[pl.ds(n * block, block), :] = total.astype(out.dtype)


def total_kernel(count, *refs):
    parts, outs = refs[:count], refs[count:]
    at = 0
    for out in outs:
        here = pl.ds(at, out.shape[0])
        at += out.shape[0]
        total = parts[0][here, :]
        for part in parts[1:]:
            total = total + part[here, :].astype(F32)
        out[...] = total.astype(out.dtype)


def shards(
    queries, key_new, value_new, key_pool, value_pool, page_table, lengths, residual_in,
    w_out, norm_gain, w_gate, w_up, w_down,
):
    req_devices = lax.axis_size("req")
    head_devices = lax.axis_size("head")
    chips = req_devices // 2
    reqs = queries.shape[0]
    heads = queries.shape[1] // HEAD_DIM
    kv_local = key_new.shape[1] // HEAD_DIM
    hidden_width = w_down.shape[0]
    rows = reqs * heads
    pages, page_len = key_pool.shape[:2]
    me = lax.axis_index("req")
    place = jnp.stack([me, lax.axis_index("head")]).astype(jnp.int32)
    vmem = pl.BlockSpec(memory_space=pltpu.VMEM)
    smem = pl.BlockSpec(memory_space=pltpu.SMEM)

    inverse_rows = -(-(pages * req_devices // LO) // 16) * 16
    payload = pl.pallas_call(
        functools.partial(pack_kernel, page_len),
        out_shape=jax.ShapeDtypeStruct((rows + inverse_rows, HEAD_DIM), BF16),
        in_specs=[smem, smem, vmem, vmem],
        out_specs=vmem,
        compiler_params=params(),
        name="pack",
    )(place, in_hbm(lengths), in_hbm(page_table), queries)
    near = [payload] + [swap(payload, "req", 2 * c) for c in range(1, chips)]
    columns = w_out.shape[1]
    gain = pl.pallas_call(
        gain_kernel,
        out_shape=jax.ShapeDtypeStruct((req_devices, columns), F32),
        in_specs=[vmem],
        out_specs=vmem,
        compiler_params=params(1),
        name="gain",
    )(norm_gain.reshape(req_devices, columns))
    keys, = staged([payload, gain], key_pool, name="stage_keys")
    near = stacked(near, keys)
    far = swap(near, "req", 1)

    step_pages = 16
    total_rows = rows * req_devices
    anywhere = pl.BlockSpec(memory_space=pl.ANY)
    sent = jax.ShapeDtypeStruct((rows + reqs, HEAD_DIM), BF16)
    copied = jax.ShapeDtypeStruct((hidden_width, columns), BF16)
    steps, early, w_up = range(req_devices), 3 * req_devices // 8, w_up.T
    attended = pl.pallas_call(
        functools.partial(attend_kernel, req_devices, heads, kv_local, reqs, step_pages),
        out_shape=[sent] * req_devices
        + [jax.ShapeDtypeStruct(w_out.shape, BF16)]
        + [copied] * early,
        in_specs=[smem, vmem, vmem, vmem] + [anywhere] * 3,
        out_specs=[vmem] * req_devices + [anywhere] * (1 + early),
        scratch_shapes=[
            pltpu.VMEM((total_rows, HEAD_DIM), F32),
            pltpu.VMEM((pages, heads, HEAD_DIM), F32),
            pltpu.VMEM((total_rows, HEAD_DIM), F32),
            pltpu.VMEM((total_rows, HEAD_DIM), F32),
            pltpu.VMEM((total_rows, HEAD_DIM), F32),
            pltpu.VMEM((8, 2 * LO), jnp.int32),
            pltpu.SMEM((8, 2 * LO), jnp.int32),
            pltpu.VMEM(value_pool.shape, BF16),
            pltpu.SemaphoreType.DMA,
            pltpu.SemaphoreType.DMA((4,)),
            pltpu.SemaphoreType.DMA((early + 1,)),
        ],
        compiler_params=params(24),
        name="attend",
    )(place, near, far, keys, in_hbm(value_pool), in_hbm(w_out), in_hbm(w_up))
    partials, w_out, first_up = (
        attended[:req_devices], attended[req_devices], attended[req_devices + 1 :]
    )
    w_gate = staged_blocks(
        place, columns, [partials[0]], [w_gate.T], [(0, t) for t in steps], "stage_gate"
    )

    near_out, far_out = partials[:chips], partials[chips:]
    parts = [near_out[0], swap(far_out[0], "req", 1)]
    for c in range(1, chips):
        parts += [swap(near_out[c], "req", 2 * c), swap(far_out[c], "req", 2 * c + 1)]
    attention = pl.pallas_call(
        functools.partial(combine_kernel, heads),
        out_shape=jax.ShapeDtypeStruct((reqs, heads * HEAD_DIM), BF16),
        in_specs=[vmem] * 3 + [anywhere] + [vmem] * len(parts),
        out_specs=vmem,
        compiler_params=params(4),
        name="combine",
    )(payload, key_new, value_new, w_gate[0], *parts)

    near = [attention] + [swap(attention, "req", 2 * c) for c in range(1, chips)]
    far = [swap(x, "req", 1) for x in near]
    block = reqs * req_devices // head_devices
    summed = pl.pallas_call(
        functools.partial(project_kernel, chips),
        out_shape=[
            jax.ShapeDtypeStruct((block, columns), F32 if a == 0 else BF16)
            for a in range(head_devices)
        ],
        in_specs=[smem] + [vmem] * (2 * chips + 1),
        out_specs=[vmem] * head_devices,
        scratch_shapes=[pltpu.VMEM((block * head_devices, w_out.shape[0]), BF16)],
        compiler_params=params(5),
        name="project",
    )(place, *near, *far, w_out)
    later = [(0, t) for t in steps[early:]] + [(1, t) for t in steps]
    blocks = staged_blocks(place, columns, [summed[0]], [w_up, w_down], later, "stage_up_down")
    w_up, w_down = [*first_up, *blocks[: -len(steps)]], blocks[-len(steps) :]
    terms = [summed[0]] + [swap(summed[a], "head", a) for a in range(1, head_devices)]
    state = pl.pallas_call(
        state_kernel,
        out_shape=jax.ShapeDtypeStruct((block, columns), BF16),
        in_specs=[anywhere] + [vmem] * (1 + head_devices),
        out_specs=vmem,
        compiler_params=params(4),
        name="state",
    )(w_down[0], residual_in, *terms)

    pieces = [state] + [swap(state, "head", a) for a in range(1, head_devices)]
    squares = chips == 4 and head_devices == 4

    def spread(array):
        return [array] + [swap(array, "req", 2 * c) for c in range(1, chips)]

    if squares:
        own_x, own_y = swap(state, "req", 2), swap(state, "req", 4)
        late = stacked(pieces[1:], own_x, own_y)
        late_x, late_y = swap(late, "req", 2), swap(late, "req", 4)
        across = [
            swap(stacked([own_x, cut_rows(late_x, 0, block)]), "req", 4),
            swap(cut_rows(late_y, block, 2 * block), "req", 2),
        ]
        near = [[state, late], [own_x, late_x], [own_y, late_y], across]
    else:
        first = spread(state)
        rest = spread(stacked(pieces[1:], *first[1:]))
        near = [[first[c], rest[c]] for c in range(chips)]
    all_rows = block * head_devices
    sums = []
    for c in range(chips):
        last = c == chips - 1
        if squares and last:
            near[c] = [stacked(near[c], after)]
        far = [swap(x, "req", 1) for x in near[c]]
        count = len(far)
        sums = pl.pallas_call(
            functools.partial(hidden_kernel, count, c, last, columns * req_devices),
            out_shape=[jax.ShapeDtypeStruct((all_rows, hidden_width), BF16)]
            if last
            else [
                jax.ShapeDtypeStruct((all_rows, hidden_width), F32),
                jax.ShapeDtypeStruct((all_rows, hidden_width), F32),
                jax.ShapeDtypeStruct((all_rows, HEAD_DIM), F32),
            ],
            in_specs=[smem] + [vmem] * (2 * count + 5 + len(sums)),
            out_specs=[vmem] if last else [vmem] * 3,
            scratch_shapes=[pltpu.VMEM((2, all_rows, columns), BF16)],
            input_output_aliases={} if c == 0 or last else {2 * count + 6 + n: n for n in range(2)},
            compiler_params=params(5),
            cost_estimate=pl.CostEstimate(
                flops=8 * all_rows * columns * hidden_width, bytes_accessed=0, transcendentals=0
            ),
            name="hidden",
        )(
            place, *near[c], *far, gain, *w_gate[2 * c : 2 * c + 2], *w_up[2 * c : 2 * c + 2], *sums
        )
        if c == 1:
            after = sums[2]
    hidden, = sums


    def down(c, *after):
        far_part, near_part = pl.pallas_call(
            down_kernel,
            out_shape=[
                jax.ShapeDtypeStruct((all_rows, columns), BF16),
                jax.ShapeDtypeStruct((all_rows, columns), F32),
            ],
            in_specs=[vmem] * 3 + [anywhere] * len(after),
            out_specs=[vmem] * 2,
            compiler_params=params(5),
            cost_estimate=pl.CostEstimate(
                flops=4 * all_rows * columns * hidden_width, bytes_accessed=0, transcendentals=0
            ),
            name="down",
        )(hidden, w_down[2 * c + 1], w_down[2 * c], *after)
        return near_part, swap(far_part, "req", 1)

    def merge(c, layout, halves, passed=(), extra=()):
        return pl.pallas_call(
            functools.partial(merge_kernel, block, layout, passed),
            out_shape=[
                jax.ShapeDtypeStruct((len(blocks) * block, columns), BF16 if c else F32)
                for blocks in layout
            ],
            in_specs=[vmem] * (2 + len(extra)),
            out_specs=[vmem] * len(layout),
            compiler_params=params(4),
            name="merge",
        )(*halves, *extra)

    def total(blocks, parts):
        return pl.pallas_call(
            functools.partial(total_kernel, len(parts)),
            out_shape=[
                jax.ShapeDtypeStruct((block, columns), BF16 if a else F32) for a in blocks
            ],
            in_specs=[vmem] * len(parts),
            out_specs=[vmem] * len(blocks),
            compiler_params=params(4),
            name="total",
        )(*parts)

    totals = {}
    if squares:
        corner = down(3)
        halves_x = down(1)
        by_x, by_y = merge(3, [[2, 0], [3, 1]], corner)
        halves_y = down(2, by_x)
        halves_own = down(0, by_x)
        by_x, by_y = swap(by_x, "req", 2), swap(by_y, "req", 4)
        layout = [[1, 0], [2, 3]]
        own = merge(0, layout, halves_own)
        to_x = merge(1, layout, halves_x, (3, 1), (by_y,))
        to_y = merge(2, layout, halves_y, (2, 0), (by_x,))
        for n, blocks in enumerate(layout):
            parts = [own[n], swap(to_x[n], "req", 2), swap(to_y[n], "req", 4)]
            totals.update(zip(blocks, total(blocks, parts)))
    else:
        layout = [list(range(1, head_devices)), [0]]
        merged = [merge(c, layout, down(c)) for c in range(chips)]
        for n, blocks in enumerate(layout):
            parts = [merged[0][n]] + [swap(merged[c][n], "req", 2 * c) for c in range(1, chips)]
            totals.update(zip(blocks, total(blocks, parts)))
    output = state.astype(F32) + totals[0]
    for a in range(head_devices - 1, 0, -1):
        output += swap(totals[a], "head", a).astype(F32)
    return output.astype(BF16)


def solution(mesh):
    return jax.shard_map(
        shards,
        mesh=mesh,
        in_specs=(
            P("req", "head"),
            P("req", "head"),
            P("req", "head"),
            P("req", None, "head"),
            P("req", None, "head"),
            P("req", None),
            P("req"),
            P("head", "req"),
            P("head", "req"),
            P(),
            P(None, ("req", "head")),
            P(None, ("req", "head")),
            P(("req", "head"), None),
        ),
        out_specs=P("head", "req"),
        check_vma=False,
    )
```

```python
import functools
import math

import jax
import jax.numpy as jnp
from jax import lax
from jax.experimental import pallas as pl
from jax.experimental.pallas import tpu as pltpu
from jax.sharding import PartitionSpec as P

HEAD_DIM = 128
LO = 64
NEGATIVE_FILL = -1e30
NORM_EPS = 1e-06
BF16 = jnp.bfloat16
F32 = jnp.float32


def swap(array, axis, bits):
    size = lax.axis_size(axis)
    return lax.ppermute(array, axis, [(i, i ^ bits) for i in range(size)])


def whole(shape):
    return pl.BlockSpec(shape, lambda *_: (0,) * len(shape))


def in_vmem(array):
    return pltpu.with_memory_space_constraint(array, pltpu.VMEM)


def in_hbm(array):
    return pltpu.with_memory_space_constraint(array, pltpu.HBM)


def params(mebibytes=8):
    return pltpu.CompilerParams(vmem_limit_bytes=mebibytes * 1024 * 1024)


def stage_kernel(count, pieces, *refs):
    sources, outs, sems = refs[:count], refs[-1 - count : -1], refs[-1]
    copies = []
    for n in range(count):
        rows = sources[n].shape[0] // pieces // 16 * 16
        for p in range(pieces):
            size = rows if p < pieces - 1 else sources[n].shape[0] - rows * (pieces - 1)
            here = pl.ds(p * rows, size)
            copies.append(
                pltpu.make_async_copy(
                    sources[n].at[here], outs[n].at[here], sems.at[n * pieces + p]
                )
            )
    for copy in copies:
        copy.start()
    for copy in copies:
        copy.wait()


def staged(after, *arrays, name):
    pieces = 4
    size = sum(math.prod(array.shape) * 2 for array in arrays)
    return pl.pallas_call(
        functools.partial(stage_kernel, len(arrays), pieces),
        out_shape=[jax.ShapeDtypeStruct(array.shape, array.dtype) for array in arrays],
        in_specs=[pl.BlockSpec(memory_space=pl.ANY)] * (len(arrays) + len(after)),
        out_specs=[pl.BlockSpec(memory_space=pl.ANY)] * len(arrays),
        scratch_shapes=[pltpu.SemaphoreType.DMA((len(arrays) * pieces,))],
        compiler_params=params(1),
        cost_estimate=pl.CostEstimate(flops=0, bytes_accessed=size, transcendentals=0),
        name=name,
    )(*[in_hbm(array) for array in arrays], *after)


def split_kernel(count, wanted, place, *refs):
    sources, outs, sems = refs[:count], refs[-1 - len(wanted) : -1], refs[-1]
    copies = []
    for k, ((n, t), out) in enumerate(zip(wanted, outs)):
        width = out.shape[1]
        here = pl.ds(pl.multiple_of((place[0] ^ t) * width, width), width)
        copies.append(pltpu.make_async_copy(sources[n].at[:, here], out, sems.at[k]))
    for copy in copies:
        copy.start()
    for copy in copies:
        copy.wait()


def staged_blocks(place, width, after, arrays, wanted, name):
    anywhere = pl.BlockSpec(memory_space=pl.ANY)
    shapes = [jax.ShapeDtypeStruct((arrays[n].shape[0], width), arrays[n].dtype) for n, _ in wanted]
    return pl.pallas_call(
        functools.partial(split_kernel, len(arrays), wanted),
        out_shape=shapes,
        in_specs=[pl.BlockSpec(memory_space=pltpu.SMEM)] + [anywhere] * (len(arrays) + len(after)),
        out_specs=[anywhere] * len(wanted),
        scratch_shapes=[pltpu.SemaphoreType.DMA((len(wanted),))],
        compiler_params=params(1),
        cost_estimate=pl.CostEstimate(
            flops=0,
            bytes_accessed=sum(2 * math.prod(shape.shape) for shape in shapes),
            transcendentals=0,
        ),
        name=name,
    )(place, *[in_hbm(array) for array in arrays], *after)


def pack_kernel(page_len, place, lengths, table, queries, out):
    del place
    reqs, slots = table.shape
    query_rows = queries.shape[0] * queries.shape[1] // HEAD_DIM
    inverse_rows = out.shape[0] - query_rows
    high = lax.broadcasted_iota(jnp.int32, (inverse_rows, slots), 0)
    lane = lax.broadcasted_iota(jnp.int32, (2 * LO, slots), 0)
    first = lax.broadcasted_iota(jnp.int32, (1, slots), 1) * page_len
    total = jnp.zeros((inverse_rows, 2 * LO), F32)
    for r in range(reqs):
        ids = table[pl.ds(r, 1), :]
        tokens = jnp.clip(lengths[r] - first, 0, page_len)
        row_hit = jnp.where((ids >> 6) == high, 1.0, 0.0).astype(BF16)
        held = jnp.where(lane < LO, r + 1, tokens)
        lane_hit = jnp.where((ids & (LO - 1)) == (lane & (LO - 1)), held, 0).astype(F32).astype(BF16)
        total += lax.dot_general(
            row_hit, lane_hit, (((1,), (1,)), ((), ())), preferred_element_type=F32
        )
    own = queries[...].astype(F32).reshape(query_rows, HEAD_DIM)
    out[pl.ds(0, query_rows), :] = own.astype(BF16)
    out[pl.ds(query_rows, inverse_rows), :] = total.astype(BF16)


def stack_kernel(count, *refs):
    out = refs[-1]
    at = 0
    for piece in refs[:count]:
        out[pl.ds(at, piece.shape[0]), :] = piece[...]
        at += piece.shape[0]


def stacked(pieces, *after):
    vmem = pl.BlockSpec(memory_space=pltpu.VMEM)
    rows = sum(piece.shape[0] for piece in pieces)
    return pl.pallas_call(
        functools.partial(stack_kernel, len(pieces)),
        out_shape=jax.ShapeDtypeStruct((rows, pieces[0].shape[1]), pieces[0].dtype),
        in_specs=[vmem] * len(pieces) + [pl.BlockSpec(memory_space=pl.ANY)] * len(after),
        out_specs=vmem,
        compiler_params=params(4),
        name="stack",
    )(*pieces, *after)


def rows_kernel(first, source, out):
    out[...] = source[pl.ds(first, out.shape[0]), :]


def cut_rows(array, first, size):
    vmem = pl.BlockSpec(memory_space=pltpu.VMEM)
    return pl.pallas_call(
        functools.partial(rows_kernel, first),
        out_shape=jax.ShapeDtypeStruct((size, array.shape[1]), array.dtype),
        in_specs=[vmem],
        out_specs=vmem,
        compiler_params=params(2),
        name="rows",
    )(array)


def attend_kernel(
    devices, heads, kv_local, reqs, step_pages, place, near, far, keys, value_pool, *refs
):
    w_out, w_up, refs = refs[0], refs[1], refs[2:]
    outs, refs = refs[:-11], refs[-11:]
    outs, w_out_copy, w_up_copies = outs[:devices], outs[devices], outs[devices + 1 :]
    query, score, top, weight, acc, found, index, values, sem, value_sem, out_sem = refs
    chips = len(outs) // 2
    pages = keys.shape[0]
    steps = pages // step_pages
    rows = reqs * heads
    stride = near.shape[0] // chips
    inverse_rows = stride - rows
    group = heads // kv_local
    scale = 1.0 / math.sqrt(HEAD_DIM)
    lane = lax.broadcasted_iota(jnp.int32, (heads, HEAD_DIM), 1)
    head = lax.broadcasted_iota(jnp.int32, (heads, HEAD_DIM), 0)

    cut = pages // value_sem.shape[0]
    loads = [
        pltpu.make_async_copy(
            value_pool.at[pl.ds(n * cut, cut)], values.at[pl.ds(n * cut, cut)], value_sem.at[n]
        )
        for n in range(value_sem.shape[0])
    ]
    for load in loads:
        load.start()

    wanted = place[0] * (pages // LO) + lax.broadcasted_iota(jnp.int32, (8, inverse_rows), 0)
    pick = jnp.where(lax.broadcasted_iota(jnp.int32, (8, inverse_rows), 1) == wanted, 1.0, 0.0)
    half = lax.broadcasted_iota(jnp.int32, (8, 2 * LO), 1)
    total = jnp.zeros((8, 2 * LO), F32)
    for side, ref in enumerate((near, far)):
        for chip in range(chips):
            at = (side * chips + chip) * rows
            query[pl.ds(at, rows), :] = ref[pl.ds(chip * stride, rows), :].astype(F32)
            part = jnp.dot(
                pick.astype(BF16),
                ref[pl.ds(chip * stride + rows, inverse_rows), :],
                preferred_element_type=F32,
            )
            base = (side * chips + chip) * reqs - 1
            total += jnp.where((half < LO) & (part > 0.0), part + base, part)
    found[...] = total.astype(jnp.int32)
    copy = pltpu.make_async_copy(found, index, sem)
    copy.start()
    top[...] = jnp.full(top.shape, NEGATIVE_FILL, F32)
    weight[...] = jnp.zeros(weight.shape, F32)
    acc[...] = jnp.zeros(acc.shape, F32)
    copy.wait()

    def rows_of(page):
        return pl.ds(pl.multiple_of(index[page // LO, page % LO] * heads, heads), heads)

    def tokens_of(page):
        return index[page // LO, LO + page % LO]

    @pl.loop(0, steps)
    def _(step):
        first = step * step_pages
        scores = []
        for p in range(step_pages):
            q = query[rows_of(first + p), :]
            q = jnp.concatenate(
                [jnp.where(head // group == kv, q, 0.0) for kv in range(kv_local)], axis=1
            ).astype(BF16)
            s = lax.dot_general(
                q, keys[first + p], (((1,), (1,)), ((), ())), preferred_element_type=F32
            ) * scale
            scores.append(jnp.where(lane < tokens_of(first + p), s, NEGATIVE_FILL))
        best = [jnp.max(s, axis=1, keepdims=True) for s in scores]
        for p in range(step_pages):
            score[first + p] = scores[p]
        for p in range(step_pages):
            at = rows_of(first + p)
            top[at, :] = jnp.maximum(top[at, :], best[p])

    top[...] = top[...].astype(BF16).astype(F32)
    for load in loads:
        load.wait()
    weight_loads = [pltpu.make_async_copy(w_out, w_out_copy, out_sem.at[len(w_up_copies)])]
    for t, copied in enumerate(w_up_copies):
        width = copied.shape[1]
        here = pl.ds(pl.multiple_of((place[0] ^ t) * width, width), width)
        weight_loads.append(pltpu.make_async_copy(w_up.at[:, here], copied, out_sem.at[t]))
    for load in weight_loads:
        load.start()

    @pl.loop(0, steps)
    def _(step):
        first = step * step_pages
        sums, parts = [], []
        for p in range(step_pages):
            page = first + p
            w = jnp.exp(score[page] - top[rows_of(page), :])
            w = jnp.where(lane < tokens_of(page), w, 0.0).astype(BF16)
            a = jnp.dot(w, values[page], preferred_element_type=F32)
            part = a[:, :HEAD_DIM]
            for kv in range(1, kv_local):
                part = jnp.where(
                    head // group == kv, a[:, kv * HEAD_DIM : (kv + 1) * HEAD_DIM], part
                )
            parts.append(part)
            sums.append(jnp.sum(w.astype(F32), axis=1, keepdims=True))
        for p in range(step_pages):
            at = rows_of(first + p)
            acc[at, :] += parts[p]
            weight[at, :] += sums[p]

    lane3 = lax.broadcasted_iota(jnp.int32, (reqs, heads, HEAD_DIM), 2)
    head3 = lax.broadcasted_iota(jnp.int32, (reqs, heads, HEAD_DIM), 1)
    for n, out in enumerate(outs):
        at = pl.ds(n * rows, rows)
        out[pl.ds(0, rows), :] = acc[at, :].astype(BF16)
        t = top[at, :].reshape(reqs, heads, HEAD_DIM)
        s = weight[at, :].reshape(reqs, heads, HEAD_DIM)
        s_high = s.astype(BF16).astype(F32)
        stats = jnp.where(lane3 == head3 + 2 * heads, s - s_high, 0.0)
        stats = jnp.where(lane3 == head3 + heads, s_high, stats)
        stats = jnp.where(lane3 == head3, t, stats)
        out[pl.ds(rows, reqs), :] = jnp.sum(stats, axis=1).astype(BF16)
    for load in weight_loads:
        load.wait()


def join_kernel(heads, reqs, *refs):
    count = len(refs) // 3
    rows = reqs * heads
    lane = lax.broadcasted_iota(jnp.int32, (reqs, HEAD_DIM), 1)
    lane3 = lax.broadcasted_iota(jnp.int32, (reqs, heads, HEAD_DIM), 2)
    head3 = lax.broadcasted_iota(jnp.int32, (reqs, heads, HEAD_DIM), 1)

    def wide(array):
        return jnp.sum(jnp.where(lane3 == head3, array[:, None, :], 0.0), axis=2, keepdims=True)

    for n in range(count):
        pair, out = (refs[n], refs[count + n]), refs[2 * count + n]
        stats = [ref[pl.ds(rows, reqs), :].astype(F32) for ref in pair]
        best = jnp.maximum(*stats)
        weight, acc = 0.0, 0.0
        for stat, ref in zip(stats, pair):
            factor = jnp.exp(stat - best)
            weight += factor * (
                pltpu.roll(stat, HEAD_DIM - heads, 1) + pltpu.roll(stat, HEAD_DIM - 2 * heads, 1)
            )
            part = ref[pl.ds(0, rows), :].astype(F32).reshape(reqs, heads, HEAD_DIM)
            acc += wide(factor) * part
        high = weight.astype(BF16).astype(F32)
        low = pltpu.roll(weight - high, 2 * heads, 1)
        joined = jnp.where(lane < 2 * heads, pltpu.roll(high, heads, 1), low)
        joined = jnp.where(lane < heads, best, jnp.where(lane < 3 * heads, joined, 0.0))
        out[pl.ds(0, rows), :] = acc.reshape(rows, HEAD_DIM).astype(BF16)
        out[pl.ds(rows, reqs), :] = joined.astype(BF16)


def combine_kernel(heads, queries, key_new, value_new, *refs):
    parts, out = refs[1:-1], refs[-1]
    reqs = key_new.shape[0]
    rows = reqs * heads
    lane3 = lax.broadcasted_iota(jnp.int32, (reqs, heads, HEAD_DIM), 2)
    head3 = lax.broadcasted_iota(jnp.int32, (reqs, heads, HEAD_DIM), 1)
    diagonal = lane3 == head3

    def narrow(array):
        return jnp.sum(jnp.where(diagonal, array.reshape(reqs, heads, HEAD_DIM), 0.0), axis=1)

    def wide(array):
        return jnp.sum(jnp.where(diagonal, array[:, None, :], 0.0), axis=2, keepdims=True)

    def per_head(ref):
        kv_local = ref.shape[1] // HEAD_DIM
        array = ref[...].astype(F32)
        return jnp.concatenate(
            [
                jnp.broadcast_to(
                    array[:, None, kv * HEAD_DIM : (kv + 1) * HEAD_DIM],
                    (reqs, heads // kv_local, HEAD_DIM),
                )
                for kv in range(kv_local)
            ],
            axis=1,
        )

    own = queries[pl.ds(0, rows), :].astype(F32).reshape(reqs, heads, HEAD_DIM) * per_head(key_new)
    own = jnp.sum(own, axis=2, keepdims=True) * (1.0 / math.sqrt(HEAD_DIM))
    own = narrow(jnp.broadcast_to(own, (reqs, heads, HEAD_DIM)))
    stats = [part[pl.ds(rows, reqs), :].astype(F32) for part in parts]
    best = functools.reduce(jnp.maximum, stats, own)
    own_factor = jnp.exp(own - best)
    factors = [jnp.exp(stat - best) for stat in stats]
    total = own_factor
    for stat, factor in zip(stats, factors):
        total += factor * (
            pltpu.roll(stat, HEAD_DIM - heads, 1) + pltpu.roll(stat, HEAD_DIM - 2 * heads, 1)
        )
    share = 1.0 / total
    attention = wide(own_factor * share) * per_head(value_new)
    for part, factor in zip(parts, factors):
        attention += wide(factor * share) * part[pl.ds(0, rows), :].astype(F32).reshape(
            reqs, heads, HEAD_DIM
        )
    out[...] = attention.reshape(reqs, heads * HEAD_DIM).astype(BF16)


def project_kernel(chips, place, *refs):
    near, far, w_out = refs[:chips], refs[chips : 2 * chips], refs[2 * chips]
    outs, lines = refs[2 * chips + 1 : -1], refs[-1]
    reqs = near[0].shape[0]
    block = outs[0].shape[0]

    for side, line in enumerate((near, far)):
        for chip in range(chips):
            first = (place[0] ^ (2 * chip + side)) * reqs
            at = ((first // block) ^ place[1]) * block + first % block
            lines[pl.ds(pl.multiple_of(at, reqs), reqs), :] = line[chip][...]

    product = jnp.dot(lines[...], w_out[...], preferred_element_type=F32)
    for a, out in enumerate(outs):
        out[...] = product[a * block : (a + 1) * block].astype(out.dtype)


def state_kernel(ready, residual, *refs):
    del ready
    total = residual[...].astype(F32)
    for part in refs[:-1]:
        total += part[...].astype(F32)
    refs[-1][...] = total.astype(BF16)


def gain_kernel(gain, out):
    out[...] = gain[...].astype(F32)


def hidden_kernel(groups, waits, chip, last, total_width, place, *refs):
    pieces, refs = refs[: 2 * groups], refs[2 * groups :]
    gain, w_gate, w_up = refs[0], refs[1:3], refs[3:5]
    before = refs[5:8] if chip else None
    outs, lines = refs[(8 if chip else 5) + waits : -1], refs[-1]
    rows = lines.shape[1]
    units = w_gate[0].shape[0]
    contract = (((1,), (1,)), ((), ()))
    square = [None] * groups
    for side in range(2):
        scale = gain[pl.ds(place[0] ^ (2 * chip + side), 1), :]
        at = 0
        for n, piece in enumerate(pieces[side * groups : (side + 1) * groups]):
            state = piece[...].astype(F32)
            part = jnp.sum(state * state, axis=1, keepdims=True)
            square[n] = part if side == 0 else square[n] + part
            lines[side, pl.ds(at, piece.shape[0]), :] = (state * scale).astype(BF16)
            at += piece.shape[0]
    square = jnp.broadcast_to(jnp.concatenate(square, axis=0), (rows, HEAD_DIM))
    if before is not None:
        square = square + before[2][...]
    if last:
        factor = lax.rsqrt(square.T[0:1, :] * (1.0 / total_width) + NORM_EPS)
    for first in range(0, units, 512):
        here = slice(first, min(first + 512, units))
        sums = []
        for n, weight in enumerate((w_gate, w_up)):
            total = None if before is None else before[n][here, :]
            for side in range(2):
                part = lax.dot_general(
                    weight[side][here, :], lines[side], contract, preferred_element_type=F32
                )
                total = part if total is None else total + part
            sums.append(total)
        if last:
            gate = sums[0] * factor
            hidden = gate / (1.0 + jnp.exp(-gate)) * (sums[1] * factor)
            outs[0][:, here] = hidden.T.astype(BF16)
        else:
            outs[0][here, :], outs[1][here, :] = sums
    if not last:
        outs[2][...] = square


def down_kernel(hidden, far, near, *refs):
    far_out, near_out = refs[-2:]
    for weight, out in ((far, far_out), (near, near_out)):
        out[...] = jnp.dot(hidden[...], weight[...], preferred_element_type=F32).astype(out.dtype)


def merge_kernel(block, layout, passed, mine, other, *refs):
    outs = refs[len(refs) - len(layout) :]
    for out, blocks in zip(outs, layout):
        for n, a in enumerate(blocks):
            here = pl.ds(a * block, block)
            total = mine[here, :] + other[here, :].astype(F32)
            if a in passed:
                total += refs[0][pl.ds(passed.index(a) * block, block), :].astype(F32)
            out[pl.ds(n * block, block), :] = total.astype(out.dtype)


def total_kernel(count, *refs):
    parts, outs = refs[:count], refs[count:]
    at = 0
    for out in outs:
        here = pl.ds(at, out.shape[0])
        at += out.shape[0]
        total = parts[0][here, :]
        for part in parts[1:]:
            total = total + part[here, :].astype(F32)
        out[...] = total.astype(out.dtype)


def shards(
    queries, key_new, value_new, key_pool, value_pool, page_table, lengths, residual_in,
    w_out, norm_gain, w_gate, w_up, w_down,
):
    req_devices = lax.axis_size("req")
    head_devices = lax.axis_size("head")
    chips = req_devices // 2
    reqs = queries.shape[0]
    heads = queries.shape[1] // HEAD_DIM
    kv_local = key_new.shape[1] // HEAD_DIM
    hidden_width = w_down.shape[0]
    rows = reqs * heads
    pages, page_len = key_pool.shape[:2]
    me = lax.axis_index("req")
    place = jnp.stack([me, lax.axis_index("head")]).astype(jnp.int32)
    vmem = pl.BlockSpec(memory_space=pltpu.VMEM)
    smem = pl.BlockSpec(memory_space=pltpu.SMEM)

    inverse_rows = -(-(pages * req_devices // LO) // 16) * 16
    payload = pl.pallas_call(
        functools.partial(pack_kernel, page_len),
        out_shape=jax.ShapeDtypeStruct((rows + inverse_rows, HEAD_DIM), BF16),
        in_specs=[smem, smem, vmem, vmem],
        out_specs=vmem,
        compiler_params=params(),
        name="pack",
    )(place, in_hbm(lengths), in_hbm(page_table), queries)
    near = [payload] + [swap(payload, "req", 2 * c) for c in range(1, chips)]
    columns = w_out.shape[1]
    gain = pl.pallas_call(
        gain_kernel,
        out_shape=jax.ShapeDtypeStruct((req_devices, columns), F32),
        in_specs=[vmem],
        out_specs=vmem,
        compiler_params=params(1),
        name="gain",
    )(norm_gain.reshape(req_devices, columns))
    keys, = staged([payload, gain], key_pool, name="stage_keys")
    near = stacked(near, keys)
    far = swap(near, "req", 1)

    step_pages = 16
    total_rows = rows * req_devices
    anywhere = pl.BlockSpec(memory_space=pl.ANY)
    sent = jax.ShapeDtypeStruct((rows + reqs, HEAD_DIM), BF16)
    copied = jax.ShapeDtypeStruct((hidden_width, columns), BF16)
    steps, early, w_up = range(req_devices), 3 * req_devices // 8, w_up.T
    attended = pl.pallas_call(
        functools.partial(attend_kernel, req_devices, heads, kv_local, reqs, step_pages),
        out_shape=[sent] * req_devices
        + [jax.ShapeDtypeStruct(w_out.shape, BF16)]
        + [copied] * early,
        in_specs=[smem, vmem, vmem, vmem] + [anywhere] * 3,
        out_specs=[vmem] * req_devices + [anywhere] * (1 + early),
        scratch_shapes=[
            pltpu.VMEM((total_rows, HEAD_DIM), F32),
            pltpu.VMEM((pages, heads, HEAD_DIM), F32),
            pltpu.VMEM((total_rows, HEAD_DIM), F32),
            pltpu.VMEM((total_rows, HEAD_DIM), F32),
            pltpu.VMEM((total_rows, HEAD_DIM), F32),
            pltpu.VMEM((8, 2 * LO), jnp.int32),
            pltpu.SMEM((8, 2 * LO), jnp.int32),
            pltpu.VMEM(value_pool.shape, BF16),
            pltpu.SemaphoreType.DMA,
            pltpu.SemaphoreType.DMA((4,)),
            pltpu.SemaphoreType.DMA((early + 1,)),
        ],
        compiler_params=params(24),
        name="attend",
    )(place, near, far, keys, in_hbm(value_pool), in_hbm(w_out), in_hbm(w_up))
    partials, w_out, first_up = (
        attended[:req_devices], attended[req_devices], attended[req_devices + 1 :]
    )
    joined = pl.pallas_call(
        functools.partial(join_kernel, heads, reqs),
        out_shape=[sent] * chips,
        in_specs=[vmem] * (2 * chips),
        out_specs=[vmem] * chips,
        compiler_params=params(6),
        name="join",
    )(*partials[:chips], *[swap(part, "req", 1) for part in partials[chips:]])
    w_gate = staged_blocks(
        place, columns, [joined[0]], [w_gate.T], [(0, t) for t in steps], "stage_gate"
    )

    parts = [joined[0]] + [swap(joined[c], "req", 2 * c) for c in range(1, chips)]
    attention = pl.pallas_call(
        functools.partial(combine_kernel, heads),
        out_shape=jax.ShapeDtypeStruct((reqs, heads * HEAD_DIM), BF16),
        in_specs=[vmem] * 3 + [anywhere] + [vmem] * len(parts),
        out_specs=vmem,
        compiler_params=params(4),
        name="combine",
    )(payload, key_new, value_new, w_gate[0], *parts)

    near = [attention] + [swap(attention, "req", 2 * c) for c in range(1, chips)]
    far = [swap(x, "req", 1) for x in near]
    block = reqs * req_devices // head_devices
    summed = pl.pallas_call(
        functools.partial(project_kernel, chips),
        out_shape=[
            jax.ShapeDtypeStruct((block, columns), F32 if a == 0 else BF16)
            for a in range(head_devices)
        ],
        in_specs=[smem] + [vmem] * (2 * chips + 1),
        out_specs=[vmem] * head_devices,
        scratch_shapes=[pltpu.VMEM((block * head_devices, w_out.shape[0]), BF16)],
        compiler_params=params(5),
        name="project",
    )(place, *near, *far, w_out)
    later = [(0, t) for t in steps[early:]] + [(1, t) for t in steps]
    blocks = staged_blocks(place, columns, [summed[0]], [w_up, w_down], later, "stage_up_down")
    w_up, w_down = [*first_up, *blocks[: -len(steps)]], blocks[-len(steps) :]
    terms = [summed[0]] + [swap(summed[a], "head", a) for a in range(1, head_devices)]
    state = pl.pallas_call(
        state_kernel,
        out_shape=jax.ShapeDtypeStruct((block, columns), BF16),
        in_specs=[anywhere] + [vmem] * (1 + head_devices),
        out_specs=vmem,
        compiler_params=params(4),
        name="state",
    )(w_down[0], residual_in, *terms)

    pieces = [state] + [swap(state, "head", a) for a in range(1, head_devices)]
    squares = chips == 4 and head_devices == 4
    order = [0, 3, 2, 1] if squares else list(range(head_devices))

    def spread(array):
        return [array] + [swap(array, "req", 2 * c) for c in range(1, chips)]

    if squares:
        own_x, own_y = swap(state, "req", 2), swap(state, "req", 4)
        own_corner = swap(own_x, "req", 4)
        late = stacked([pieces[a] for a in order[1:]], own_x, own_y, own_corner)
        half = late.shape[0] // 2
        late_x, late_y = swap(late, "req", 2), swap(late, "req", 4)
        near = [[state, late], [own_x, late_x], [own_y, late_y], []]
    else:
        first = spread(state)
        rest = spread(stacked(pieces[1:], *first[1:]))
        near = [[first[c], rest[c]] for c in range(chips)]
    all_rows = block * head_devices
    sums, square = [], []
    early_far = {c: [swap(near[c][0], "req", 1)] for c in range(chips - 1)} if squares else {}
    for c in range(chips):
        last = c == chips - 1
        if squares and last:
            near[c] = [stacked(across, square[2])]
        far = early_far.get(c, []) + [swap(x, "req", 1) for x in near[c][len(early_far.get(c, [])) :]]
        count = len(far)
        ready = [x for n in sorted(early_far) if n for x in early_far[n]] if c == 0 else []
        sums = pl.pallas_call(
            functools.partial(hidden_kernel, count, len(ready), c, last, columns * req_devices),
            out_shape=[jax.ShapeDtypeStruct((all_rows, hidden_width), BF16)]
            if last
            else [
                jax.ShapeDtypeStruct((hidden_width, all_rows), F32),
                jax.ShapeDtypeStruct((hidden_width, all_rows), F32),
                jax.ShapeDtypeStruct((all_rows, HEAD_DIM), F32),
            ],
            in_specs=[smem] + [vmem] * (2 * count + 5 + len(sums)) + [anywhere] * len(ready),
            out_specs=[vmem] if last else [vmem] * 3,
            scratch_shapes=[pltpu.VMEM((2, all_rows, columns), BF16)],
            input_output_aliases={} if c == 0 or last else {2 * count + 6 + n: n for n in range(2)},
            compiler_params=params(5),
            cost_estimate=pl.CostEstimate(
                flops=8 * all_rows * columns * hidden_width, bytes_accessed=0, transcendentals=0
            ),
            name="hidden",
        )(
            place, *near[c], *far, gain, *w_gate[2 * c : 2 * c + 2], *w_up[2 * c : 2 * c + 2], *sums, *ready
        )
        if not last:
            square.append(sums[2])
        if squares and c == 0:
            late_x, late_y = stacked([late_x], square[0]), stacked([late_y], square[0])
            near[1][1], near[2][1] = late_x, late_y
            across = [
                own_corner,
                swap(cut_rows(late_x, 0, half), "req", 4),
                swap(cut_rows(late_y, half, half), "req", 2),
            ]
    hidden, = sums


    def down(c, *after):
        far_part, near_part = pl.pallas_call(
            down_kernel,
            out_shape=[
                jax.ShapeDtypeStruct((all_rows, columns), BF16),
                jax.ShapeDtypeStruct((all_rows, columns), F32),
            ],
            in_specs=[vmem] * 3 + [anywhere] * len(after),
            out_specs=[vmem] * 2,
            compiler_params=params(5),
            cost_estimate=pl.CostEstimate(flops=1, bytes_accessed=1, transcendentals=0),
            name="down",
        )(hidden, w_down[2 * c + 1], w_down[2 * c], *after)
        return near_part, swap(far_part, "req", 1)

    def merge(c, layout, halves, passed=(), extra=()):
        layout = [[order.index(a) for a in blocks] for blocks in layout]
        passed = [order.index(a) for a in passed]
        return pl.pallas_call(
            functools.partial(merge_kernel, block, layout, passed),
            out_shape=[
                jax.ShapeDtypeStruct((len(blocks) * block, columns), BF16 if c else F32)
                for blocks in layout
            ],
            in_specs=[vmem] * (2 + len(extra)),
            out_specs=[vmem] * len(layout),
            compiler_params=params(4),
            name="merge",
        )(*halves, *extra)

    def total(blocks, parts):
        return pl.pallas_call(
            functools.partial(total_kernel, len(parts)),
            out_shape=[
                jax.ShapeDtypeStruct((block, columns), BF16 if a else F32) for a in blocks
            ],
            in_specs=[vmem] * len(parts),
            out_specs=[vmem] * len(blocks),
            compiler_params=params(4),
            name="total",
        )(*parts)

    totals = {}
    if squares:
        corner = down(3)
        halves_x = down(1)
        by_x, by_y = merge(3, [[2, 0], [3, 1]], corner)
        halves_y = down(2, by_x)
        halves_own = down(0, by_x)
        by_x, by_y = swap(by_x, "req", 2), swap(by_y, "req", 4)
        layout = [[1, 0], [2, 3]]
        own = merge(0, layout, halves_own)
        to_x = merge(1, layout, halves_x, (3, 1), (by_y,))
        to_y = merge(2, layout, halves_y, (2, 0), (by_x,))
        for n, blocks in enumerate(layout):
            parts = [own[n], swap(to_x[n], "req", 2), swap(to_y[n], "req", 4)]
            totals.update(zip(blocks, total(blocks, parts)))
    else:
        layout = [list(range(1, head_devices)), [0]]
        merged = [merge(c, layout, down(c)) for c in range(chips)]
        for n, blocks in enumerate(layout):
            parts = [merged[0][n]] + [swap(merged[c][n], "req", 2 * c) for c in range(1, chips)]
            totals.update(zip(blocks, total(blocks, parts)))
    output = state.astype(F32) + totals[0]
    for a in range(head_devices - 1, 0, -1):
        output += swap(totals[a], "head", a).astype(F32)
    return output.astype(BF16)


def solution(mesh):
    return jax.shard_map(
        shards,
        mesh=mesh,
        in_specs=(
            P("req", "head"),
            P("req", "head"),
            P("req", "head"),
            P("req", None, "head"),
            P("req", None, "head"),
            P("req", None),
            P("req"),
            P("head", "req"),
            P("head", "req"),
            P(),
            P(None, ("req", "head")),
            P(None, ("req", "head")),
            P(("req", "head"), None),
        ),
        out_specs=P("head", "req"),
        check_vma=False,
    )
```

```python
import functools
import math

import jax
import jax.numpy as jnp
from jax import lax
from jax.experimental import pallas as pl
from jax.experimental.pallas import tpu as pltpu
from jax.sharding import PartitionSpec as P

HEAD_DIM = 128
LO = 64
NEGATIVE_FILL = -1e30
NORM_EPS = 1e-06
BF16 = jnp.bfloat16
F32 = jnp.float32


def swap(array, axis, bits):
    size = lax.axis_size(axis)
    return lax.ppermute(array, axis, [(i, i ^ bits) for i in range(size)])


def whole(shape):
    return pl.BlockSpec(shape, lambda *_: (0,) * len(shape))


def in_vmem(array):
    return pltpu.with_memory_space_constraint(array, pltpu.VMEM)


def in_hbm(array):
    return pltpu.with_memory_space_constraint(array, pltpu.HBM)


def params(mebibytes=8):
    return pltpu.CompilerParams(vmem_limit_bytes=mebibytes * 1024 * 1024)


def stage_kernel(count, pieces, *refs):
    sources, outs, sems = refs[:count], refs[-1 - count : -1], refs[-1]
    copies = []
    for n in range(count):
        rows = sources[n].shape[0] // pieces // 16 * 16
        for p in range(pieces):
            size = rows if p < pieces - 1 else sources[n].shape[0] - rows * (pieces - 1)
            here = pl.ds(p * rows, size)
            copies.append(
                pltpu.make_async_copy(
                    sources[n].at[here], outs[n].at[here], sems.at[n * pieces + p]
                )
            )
    for copy in copies:
        copy.start()
    for copy in copies:
        copy.wait()


def staged(after, *arrays, name):
    pieces = 4
    size = sum(math.prod(array.shape) * 2 for array in arrays)
    return pl.pallas_call(
        functools.partial(stage_kernel, len(arrays), pieces),
        out_shape=[jax.ShapeDtypeStruct(array.shape, array.dtype) for array in arrays],
        in_specs=[pl.BlockSpec(memory_space=pl.ANY)] * (len(arrays) + len(after)),
        out_specs=[pl.BlockSpec(memory_space=pl.ANY)] * len(arrays),
        scratch_shapes=[pltpu.SemaphoreType.DMA((len(arrays) * pieces,))],
        compiler_params=params(1),
        cost_estimate=pl.CostEstimate(flops=0, bytes_accessed=size, transcendentals=0),
        name=name,
    )(*[in_hbm(array) for array in arrays], *after)


def split_kernel(count, wanted, place, *refs):
    sources, outs, sems = refs[:count], refs[-1 - len(wanted) : -1], refs[-1]
    copies = []
    for k, ((n, t), out) in enumerate(zip(wanted, outs)):
        width = out.shape[1]
        here = pl.ds(pl.multiple_of((place[0] ^ t) * width, width), width)
        copies.append(pltpu.make_async_copy(sources[n].at[:, here], out, sems.at[k]))
    for copy in copies:
        copy.start()
    for copy in copies:
        copy.wait()


def staged_blocks(place, width, after, arrays, wanted, name):
    anywhere = pl.BlockSpec(memory_space=pl.ANY)
    shapes = [jax.ShapeDtypeStruct((arrays[n].shape[0], width), arrays[n].dtype) for n, _ in wanted]
    return pl.pallas_call(
        functools.partial(split_kernel, len(arrays), wanted),
        out_shape=shapes,
        in_specs=[pl.BlockSpec(memory_space=pltpu.SMEM)] + [anywhere] * (len(arrays) + len(after)),
        out_specs=[anywhere] * len(wanted),
        scratch_shapes=[pltpu.SemaphoreType.DMA((len(wanted),))],
        compiler_params=params(1),
        cost_estimate=pl.CostEstimate(
            flops=0,
            bytes_accessed=sum(2 * math.prod(shape.shape) for shape in shapes),
            transcendentals=0,
        ),
        name=name,
    )(place, *[in_hbm(array) for array in arrays], *after)


def pack_kernel(page_len, place, lengths, table, queries, out):
    del place
    reqs, slots = table.shape
    query_rows = queries.shape[0] * queries.shape[1] // HEAD_DIM
    inverse_rows = out.shape[0] - query_rows
    high = lax.broadcasted_iota(jnp.int32, (inverse_rows, slots), 0)
    lane = lax.broadcasted_iota(jnp.int32, (2 * LO, slots), 0)
    first = lax.broadcasted_iota(jnp.int32, (1, slots), 1) * page_len
    total = jnp.zeros((inverse_rows, 2 * LO), F32)
    for r in range(reqs):
        ids = table[pl.ds(r, 1), :]
        tokens = jnp.clip(lengths[r] - first, 0, page_len)
        row_hit = jnp.where((ids >> 6) == high, 1.0, 0.0).astype(BF16)
        held = jnp.where(lane < LO, r + 1, tokens)
        lane_hit = jnp.where((ids & (LO - 1)) == (lane & (LO - 1)), held, 0).astype(F32).astype(BF16)
        total += lax.dot_general(
            row_hit, lane_hit, (((1,), (1,)), ((), ())), preferred_element_type=F32
        )
    own = queries[...].astype(F32).reshape(query_rows, HEAD_DIM)
    out[pl.ds(0, query_rows), :] = own.astype(BF16)
    out[pl.ds(query_rows, inverse_rows), :] = total.astype(BF16)


def stack_kernel(count, *refs):
    out = refs[-1]
    at = 0
    for piece in refs[:count]:
        out[pl.ds(at, piece.shape[0]), :] = piece[...]
        at += piece.shape[0]


def stacked(pieces, *after):
    vmem = pl.BlockSpec(memory_space=pltpu.VMEM)
    rows = sum(piece.shape[0] for piece in pieces)
    return pl.pallas_call(
        functools.partial(stack_kernel, len(pieces)),
        out_shape=jax.ShapeDtypeStruct((rows, pieces[0].shape[1]), pieces[0].dtype),
        in_specs=[vmem] * len(pieces) + [pl.BlockSpec(memory_space=pl.ANY)] * len(after),
        out_specs=vmem,
        compiler_params=params(4),
        name="stack",
    )(*pieces, *after)


def rows_kernel(first, source, out):
    out[...] = source[pl.ds(first, out.shape[0]), :]


def cut_rows(array, first, size):
    vmem = pl.BlockSpec(memory_space=pltpu.VMEM)
    return pl.pallas_call(
        functools.partial(rows_kernel, first),
        out_shape=jax.ShapeDtypeStruct((size, array.shape[1]), array.dtype),
        in_specs=[vmem],
        out_specs=vmem,
        compiler_params=params(2),
        name="rows",
    )(array)


def attend_kernel(
    devices, heads, kv_local, reqs, step_pages, place, near, far, keys, value_pool, *refs
):
    w_out, w_up, refs = refs[0], refs[1], refs[2:]
    outs, refs = refs[:-11], refs[-11:]
    outs, w_out_copy, w_up_copies = outs[:devices], outs[devices], outs[devices + 1 :]
    query, score, top, weight, acc, found, index, values, sem, value_sem, out_sem = refs
    chips = len(outs) // 2
    pages = keys.shape[0]
    steps = pages // step_pages
    rows = reqs * heads
    stride = near.shape[0] // chips
    inverse_rows = stride - rows
    group = heads // kv_local
    scale = 1.0 / math.sqrt(HEAD_DIM)
    lane = lax.broadcasted_iota(jnp.int32, (heads, HEAD_DIM), 1)
    head = lax.broadcasted_iota(jnp.int32, (heads, HEAD_DIM), 0)

    cut = pages // value_sem.shape[0]
    loads = [
        pltpu.make_async_copy(
            value_pool.at[pl.ds(n * cut, cut)], values.at[pl.ds(n * cut, cut)], value_sem.at[n]
        )
        for n in range(value_sem.shape[0])
    ]
    for load in loads:
        load.start()

    wanted = place[0] * (pages // LO) + lax.broadcasted_iota(jnp.int32, (8, inverse_rows), 0)
    pick = jnp.where(lax.broadcasted_iota(jnp.int32, (8, inverse_rows), 1) == wanted, 1.0, 0.0)
    half = lax.broadcasted_iota(jnp.int32, (8, 2 * LO), 1)
    total = jnp.zeros((8, 2 * LO), F32)
    for side, ref in enumerate((near, far)):
        for chip in range(chips):
            at = (side * chips + chip) * rows
            query[pl.ds(at, rows), :] = ref[pl.ds(chip * stride, rows), :].astype(F32)
            part = jnp.dot(
                pick.astype(BF16),
                ref[pl.ds(chip * stride + rows, inverse_rows), :],
                preferred_element_type=F32,
            )
            base = (side * chips + chip) * reqs - 1
            total += jnp.where((half < LO) & (part > 0.0), part + base, part)
    found[...] = total.astype(jnp.int32)
    copy = pltpu.make_async_copy(found, index, sem)
    copy.start()
    top[...] = jnp.full(top.shape, NEGATIVE_FILL, F32)
    weight[...] = jnp.zeros(weight.shape, F32)
    acc[...] = jnp.zeros(acc.shape, F32)
    copy.wait()

    def rows_of(page):
        return pl.ds(pl.multiple_of(index[page // LO, page % LO] * heads, heads), heads)

    def tokens_of(page):
        return index[page // LO, LO + page % LO]

    @pl.loop(0, steps)
    def _(step):
        first = step * step_pages
        scores = []
        for p in range(step_pages):
            q = query[rows_of(first + p), :]
            q = jnp.concatenate(
                [jnp.where(head // group == kv, q, 0.0) for kv in range(kv_local)], axis=1
            ).astype(BF16)
            s = lax.dot_general(
                q, keys[first + p], (((1,), (1,)), ((), ())), preferred_element_type=F32
            ) * scale
            scores.append(jnp.where(lane < tokens_of(first + p), s, NEGATIVE_FILL))
        best = [jnp.max(s, axis=1, keepdims=True) for s in scores]
        for p in range(step_pages):
            score[first + p] = scores[p]
        for p in range(step_pages):
            at = rows_of(first + p)
            top[at, :] = jnp.maximum(top[at, :], best[p])

    top[...] = top[...].astype(BF16).astype(F32)
    for load in loads:
        load.wait()
    weight_loads = [pltpu.make_async_copy(w_out, w_out_copy, out_sem.at[len(w_up_copies)])]
    for t, copied in enumerate(w_up_copies):
        width = copied.shape[1]
        here = pl.ds(pl.multiple_of((place[0] ^ t) * width, width), width)
        weight_loads.append(pltpu.make_async_copy(w_up.at[:, here], copied, out_sem.at[t]))
    for load in weight_loads:
        load.start()

    @pl.loop(0, steps)
    def _(step):
        first = step * step_pages
        sums, parts = [], []
        for p in range(step_pages):
            page = first + p
            w = jnp.exp(score[page] - top[rows_of(page), :])
            w = jnp.where(lane < tokens_of(page), w, 0.0).astype(BF16)
            a = jnp.dot(w, values[page], preferred_element_type=F32)
            part = a[:, :HEAD_DIM]
            for kv in range(1, kv_local):
                part = jnp.where(
                    head // group == kv, a[:, kv * HEAD_DIM : (kv + 1) * HEAD_DIM], part
                )
            parts.append(part)
            sums.append(jnp.sum(w.astype(F32), axis=1, keepdims=True))
        for p in range(step_pages):
            at = rows_of(first + p)
            acc[at, :] += parts[p]
            weight[at, :] += sums[p]

    lane3 = lax.broadcasted_iota(jnp.int32, (reqs, heads, HEAD_DIM), 2)
    head3 = lax.broadcasted_iota(jnp.int32, (reqs, heads, HEAD_DIM), 1)
    for n, out in enumerate(outs):
        at = pl.ds(n * rows, rows)
        out[pl.ds(0, rows), :] = acc[at, :].astype(BF16)
        t = top[at, :].reshape(reqs, heads, HEAD_DIM)
        s = weight[at, :].reshape(reqs, heads, HEAD_DIM)
        s_high = s.astype(BF16).astype(F32)
        stats = jnp.where(lane3 == head3 + 2 * heads, s - s_high, 0.0)
        stats = jnp.where(lane3 == head3 + heads, s_high, stats)
        stats = jnp.where(lane3 == head3, t, stats)
        out[pl.ds(rows, reqs), :] = jnp.sum(stats, axis=1).astype(BF16)
    for load in weight_loads:
        load.wait()


def join_kernel(heads, reqs, *refs):
    count = len(refs) // 3
    rows = reqs * heads
    lane = lax.broadcasted_iota(jnp.int32, (reqs, HEAD_DIM), 1)
    lane3 = lax.broadcasted_iota(jnp.int32, (reqs, heads, HEAD_DIM), 2)
    head3 = lax.broadcasted_iota(jnp.int32, (reqs, heads, HEAD_DIM), 1)

    def wide(array):
        return jnp.sum(jnp.where(lane3 == head3, array[:, None, :], 0.0), axis=2, keepdims=True)

    for n in range(count):
        pair, out = (refs[n], refs[count + n]), refs[2 * count + n]
        stats = [ref[pl.ds(rows, reqs), :].astype(F32) for ref in pair]
        best = jnp.maximum(*stats)
        weight, acc = 0.0, 0.0
        for stat, ref in zip(stats, pair):
            factor = jnp.exp(stat - best)
            weight += factor * (
                pltpu.roll(stat, HEAD_DIM - heads, 1) + pltpu.roll(stat, HEAD_DIM - 2 * heads, 1)
            )
            part = ref[pl.ds(0, rows), :].astype(F32).reshape(reqs, heads, HEAD_DIM)
            acc += wide(factor) * part
        high = weight.astype(BF16).astype(F32)
        low = pltpu.roll(weight - high, 2 * heads, 1)
        joined = jnp.where(lane < 2 * heads, pltpu.roll(high, heads, 1), low)
        joined = jnp.where(lane < heads, best, jnp.where(lane < 3 * heads, joined, 0.0))
        out[pl.ds(0, rows), :] = acc.reshape(rows, HEAD_DIM).astype(BF16)
        out[pl.ds(rows, reqs), :] = joined.astype(BF16)


def combine_kernel(heads, queries, key_new, value_new, *refs):
    parts, out = refs[1:-1], refs[-1]
    reqs = key_new.shape[0]
    rows = reqs * heads
    lane3 = lax.broadcasted_iota(jnp.int32, (reqs, heads, HEAD_DIM), 2)
    head3 = lax.broadcasted_iota(jnp.int32, (reqs, heads, HEAD_DIM), 1)
    diagonal = lane3 == head3

    def narrow(array):
        return jnp.sum(jnp.where(diagonal, array.reshape(reqs, heads, HEAD_DIM), 0.0), axis=1)

    def wide(array):
        return jnp.sum(jnp.where(diagonal, array[:, None, :], 0.0), axis=2, keepdims=True)

    def per_head(ref):
        kv_local = ref.shape[1] // HEAD_DIM
        array = ref[...].astype(F32)
        return jnp.concatenate(
            [
                jnp.broadcast_to(
                    array[:, None, kv * HEAD_DIM : (kv + 1) * HEAD_DIM],
                    (reqs, heads // kv_local, HEAD_DIM),
                )
                for kv in range(kv_local)
            ],
            axis=1,
        )

    own = queries[pl.ds(0, rows), :].astype(F32).reshape(reqs, heads, HEAD_DIM) * per_head(key_new)
    own = jnp.sum(own, axis=2, keepdims=True) * (1.0 / math.sqrt(HEAD_DIM))
    own = narrow(jnp.broadcast_to(own, (reqs, heads, HEAD_DIM)))
    stats = [part[pl.ds(rows, reqs), :].astype(F32) for part in parts]
    best = functools.reduce(jnp.maximum, stats, own)
    own_factor = jnp.exp(own - best)
    factors = [jnp.exp(stat - best) for stat in stats]
    total = own_factor
    for stat, factor in zip(stats, factors):
        total += factor * (
            pltpu.roll(stat, HEAD_DIM - heads, 1) + pltpu.roll(stat, HEAD_DIM - 2 * heads, 1)
        )
    share = 1.0 / total
    attention = wide(own_factor * share) * per_head(value_new)
    for part, factor in zip(parts, factors):
        attention += wide(factor * share) * part[pl.ds(0, rows), :].astype(F32).reshape(
            reqs, heads, HEAD_DIM
        )
    out[...] = attention.reshape(reqs, heads * HEAD_DIM).astype(BF16)


def project_kernel(chips, place, *refs):
    near, far, w_out = refs[:chips], refs[chips : 2 * chips], refs[2 * chips]
    outs, lines = refs[2 * chips + 1 : -1], refs[-1]
    reqs = near[0].shape[0]
    block = outs[0].shape[0]

    for side, line in enumerate((near, far)):
        for chip in range(chips):
            first = (place[0] ^ (2 * chip + side)) * reqs
            at = ((first // block) ^ place[1]) * block + first % block
            lines[pl.ds(pl.multiple_of(at, reqs), reqs), :] = line[chip][...]

    product = jnp.dot(lines[...], w_out[...], preferred_element_type=F32)
    for a, out in enumerate(outs):
        out[...] = product[a * block : (a + 1) * block].astype(out.dtype)


def state_kernel(ready, residual, *refs):
    del ready
    total = residual[...].astype(F32)
    for part in refs[:-1]:
        total += part[...].astype(F32)
    refs[-1][...] = total.astype(BF16)


def gain_kernel(gain, out):
    out[...] = gain[...].astype(F32)


def hidden_kernel(groups, waits, chip, last, total_width, place, *refs):
    pieces, refs = refs[: 2 * groups], refs[2 * groups :]
    gain, w_gate, w_up = refs[0], refs[1:3], refs[3:5]
    before = refs[5:8] if chip else None
    outs, lines = refs[(8 if chip else 5) + waits : -1], refs[-1]
    rows = lines.shape[1]
    units = w_gate[0].shape[0]
    contract = (((1,), (1,)), ((), ()))
    square = [None] * groups
    for side in range(2):
        scale = gain[pl.ds(place[0] ^ (2 * chip + side), 1), :]
        at = 0
        for n, piece in enumerate(pieces[side * groups : (side + 1) * groups]):
            state = piece[...].astype(F32)
            part = jnp.sum(state * state, axis=1, keepdims=True)
            square[n] = part if side == 0 else square[n] + part
            lines[side, pl.ds(at, piece.shape[0]), :] = (state * scale).astype(BF16)
            at += piece.shape[0]
    square = jnp.broadcast_to(jnp.concatenate(square, axis=0), (rows, HEAD_DIM))
    if before is not None:
        square = square + before[2][...]
    if last:
        factor = lax.rsqrt(square.T[0:1, :] * (1.0 / total_width) + NORM_EPS)
    for first in range(0, units, units):
        here = slice(first, first + units)
        sums = []
        for n, weight in enumerate((w_gate, w_up)):
            total = None if before is None else before[n][here, :]
            for side in range(2):
                part = lax.dot_general(
                    weight[side][here, :], lines[side], contract, preferred_element_type=F32
                )
                total = part if total is None else total + part
            sums.append(total)
        if last:
            gate = sums[0] * factor
            hidden = gate / (1.0 + jnp.exp(-gate)) * (sums[1] * factor)
            outs[0][:, here] = hidden.T.astype(BF16)
        else:
            outs[0][here, :], outs[1][here, :] = sums
    if not last:
        outs[2][...] = square


def down_kernel(count, hidden, *refs):
    for weight, out in zip(refs[:count], refs[-count:]):
        out[...] = jnp.dot(hidden[...], weight[...], preferred_element_type=F32).astype(out.dtype)


def merge_kernel(block, layout, passed, mine, other, *refs):
    outs = refs[len(refs) - len(layout) :]
    for out, blocks in zip(outs, layout):
        for n, a in enumerate(blocks):
            here = pl.ds(a * block, block)
            total = mine[here, :] + other[here, :].astype(F32)
            if a in passed:
                total += refs[0][pl.ds(passed.index(a) * block, block), :].astype(F32)
            out[pl.ds(n * block, block), :] = total.astype(out.dtype)


def total_kernel(count, *refs):
    parts, outs = refs[:count], refs[count:]
    at = 0
    for out in outs:
        here = pl.ds(at, out.shape[0])
        at += out.shape[0]
        total = parts[0][here, :]
        for part in parts[1:]:
            total = total + part[here, :].astype(F32)
        out[...] = total.astype(out.dtype)


def shards(
    queries, key_new, value_new, key_pool, value_pool, page_table, lengths, residual_in,
    w_out, norm_gain, w_gate, w_up, w_down,
):
    req_devices = lax.axis_size("req")
    head_devices = lax.axis_size("head")
    chips = req_devices // 2
    reqs = queries.shape[0]
    heads = queries.shape[1] // HEAD_DIM
    kv_local = key_new.shape[1] // HEAD_DIM
    hidden_width = w_down.shape[0]
    rows = reqs * heads
    pages, page_len = key_pool.shape[:2]
    me = lax.axis_index("req")
    place = jnp.stack([me, lax.axis_index("head")]).astype(jnp.int32)
    vmem = pl.BlockSpec(memory_space=pltpu.VMEM)
    smem = pl.BlockSpec(memory_space=pltpu.SMEM)

    inverse_rows = -(-(pages * req_devices // LO) // 16) * 16
    payload = pl.pallas_call(
        functools.partial(pack_kernel, page_len),
        out_shape=jax.ShapeDtypeStruct((rows + inverse_rows, HEAD_DIM), BF16),
        in_specs=[smem, smem, vmem, vmem],
        out_specs=vmem,
        compiler_params=params(),
        name="pack",
    )(place, in_hbm(lengths), in_hbm(page_table), queries)
    near = [payload] + [swap(payload, "req", 2 * c) for c in range(1, chips)]
    columns = w_out.shape[1]
    gain = pl.pallas_call(
        gain_kernel,
        out_shape=jax.ShapeDtypeStruct((req_devices, columns), F32),
        in_specs=[vmem],
        out_specs=vmem,
        compiler_params=params(1),
        name="gain",
    )(norm_gain.reshape(req_devices, columns))
    keys, = staged([payload, gain], key_pool, name="stage_keys")
    near = stacked(near, keys)
    far = swap(near, "req", 1)

    step_pages = 64
    total_rows = rows * req_devices
    anywhere = pl.BlockSpec(memory_space=pl.ANY)
    sent = jax.ShapeDtypeStruct((rows + reqs, HEAD_DIM), BF16)
    copied = jax.ShapeDtypeStruct((hidden_width, columns), BF16)
    steps, early, w_up = range(req_devices), req_devices // 4, w_up.T
    attended = pl.pallas_call(
        functools.partial(attend_kernel, req_devices, heads, kv_local, reqs, step_pages),
        out_shape=[sent] * req_devices
        + [jax.ShapeDtypeStruct(w_out.shape, BF16)]
        + [copied] * early,
        in_specs=[smem, vmem, vmem, vmem] + [anywhere] * 3,
        out_specs=[vmem] * req_devices + [anywhere] * (1 + early),
        scratch_shapes=[
            pltpu.VMEM((total_rows, HEAD_DIM), F32),
            pltpu.VMEM((pages, heads, HEAD_DIM), F32),
            pltpu.VMEM((total_rows, HEAD_DIM), F32),
            pltpu.VMEM((total_rows, HEAD_DIM), F32),
            pltpu.VMEM((total_rows, HEAD_DIM), F32),
            pltpu.VMEM((8, 2 * LO), jnp.int32),
            pltpu.SMEM((8, 2 * LO), jnp.int32),
            pltpu.VMEM(value_pool.shape, BF16),
            pltpu.SemaphoreType.DMA,
            pltpu.SemaphoreType.DMA((4,)),
            pltpu.SemaphoreType.DMA((early + 1,)),
        ],
        compiler_params=params(24),
        name="attend",
    )(place, near, far, keys, in_hbm(value_pool), in_hbm(w_out), in_hbm(w_up))
    partials, w_out, first_up = (
        attended[:req_devices], attended[req_devices], attended[req_devices + 1 :]
    )
    joined = pl.pallas_call(
        functools.partial(join_kernel, heads, reqs),
        out_shape=[sent] * chips,
        in_specs=[vmem] * (2 * chips),
        out_specs=[vmem] * chips,
        compiler_params=params(6),
        name="join",
    )(*partials[:chips], *[swap(part, "req", 1) for part in partials[chips:]])
    w_gate = staged_blocks(
        place, columns, [joined[0]], [w_gate.T], [(0, t) for t in steps], "stage_gate"
    )

    parts = [joined[0]] + [swap(joined[c], "req", 2 * c) for c in range(1, chips)]
    attention = pl.pallas_call(
        functools.partial(combine_kernel, heads),
        out_shape=jax.ShapeDtypeStruct((reqs, heads * HEAD_DIM), BF16),
        in_specs=[vmem] * 3 + [anywhere] + [vmem] * len(parts),
        out_specs=vmem,
        compiler_params=params(4),
        name="combine",
    )(payload, key_new, value_new, w_gate[0], *parts)

    near = [attention] + [swap(attention, "req", 2 * c) for c in range(1, chips)]
    far = [swap(x, "req", 1) for x in near]
    block = reqs * req_devices // head_devices
    summed = pl.pallas_call(
        functools.partial(project_kernel, chips),
        out_shape=[
            jax.ShapeDtypeStruct((block, columns), F32 if a == 0 else BF16)
            for a in range(head_devices)
        ],
        in_specs=[smem] + [vmem] * (2 * chips + 1),
        out_specs=[vmem] * head_devices,
        scratch_shapes=[pltpu.VMEM((block * head_devices, w_out.shape[0]), BF16)],
        compiler_params=params(5),
        name="project",
    )(place, *near, *far, w_out)
    later = [(0, t) for t in steps[early:]] + [(1, t) for t in steps]
    blocks = staged_blocks(place, columns, [summed[0]], [w_up, w_down], later, "stage_up_down")
    w_up, w_down = [*first_up, *blocks[: -len(steps)]], blocks[-len(steps) :]
    terms = [summed[0]] + [swap(summed[a], "head", a) for a in range(head_devices - 1, 0, -1)]
    state = pl.pallas_call(
        state_kernel,
        out_shape=jax.ShapeDtypeStruct((block, columns), BF16),
        in_specs=[anywhere] + [vmem] * (1 + head_devices),
        out_specs=vmem,
        compiler_params=params(4),
        name="state",
    )(w_down[0], residual_in, *terms)

    pieces = [state] + [swap(state, "head", a) for a in range(1, head_devices)]
    squares = chips == 4 and head_devices == 4
    order = [0, 3, 2, 1] if squares else list(range(head_devices))

    def spread(array):
        return [array] + [swap(array, "req", 2 * c) for c in range(1, chips)]

    if squares:
        own_x, own_y = swap(state, "req", 2), swap(state, "req", 4)
        own_corner = swap(own_x, "req", 4)
        late = stacked([pieces[a] for a in order[1:]], own_x, own_y, own_corner)
        half = late.shape[0] // 2
        late_x, late_y = swap(late, "req", 2), swap(late, "req", 4)
        near = [[state, late], [own_x, late_x], [own_y, late_y], []]
    else:
        first = spread(state)
        rest = spread(stacked(pieces[1:], *first[1:]))
        near = [[first[c], rest[c]] for c in range(chips)]
    all_rows = block * head_devices
    sums, square = [], []
    early_far = {c: [swap(near[c][0], "req", 1)] for c in range(chips - 1)} if squares else {}
    for c in range(chips):
        last = c == chips - 1
        if squares and last:
            near[c] = [stacked(across, square[1])]
        far = early_far.get(c, []) + [swap(x, "req", 1) for x in near[c][len(early_far.get(c, [])) :]]
        count = len(far)
        ready = early_far.get(2, []) if c == 1 else []
        sums = pl.pallas_call(
            functools.partial(hidden_kernel, count, len(ready), c, last, columns * req_devices),
            out_shape=[jax.ShapeDtypeStruct((all_rows, hidden_width), BF16)]
            if last
            else [
                jax.ShapeDtypeStruct((hidden_width, all_rows), F32),
                jax.ShapeDtypeStruct((hidden_width, all_rows), F32),
                jax.ShapeDtypeStruct((all_rows, HEAD_DIM), F32),
            ],
            in_specs=[smem] + [vmem] * (2 * count + 5 + len(sums)) + [anywhere] * len(ready),
            out_specs=[vmem] if last else [vmem] * 3,
            scratch_shapes=[pltpu.VMEM((2, all_rows, columns), BF16)],
            input_output_aliases={} if c == 0 or last else {2 * count + 6 + n: n for n in range(2)},
            compiler_params=params(8),
            cost_estimate=pl.CostEstimate(
                flops=8 * all_rows * columns * hidden_width, bytes_accessed=0, transcendentals=0
            ),
            name="hidden",
        )(
            place, *near[c], *far, gain, *w_gate[2 * c : 2 * c + 2], *w_up[2 * c : 2 * c + 2], *sums, *ready
        )
        if not last:
            square.append(sums[2])
        if squares and c == 0:
            late_x, late_y = stacked([late_x], square[0]), stacked([late_y], square[0])
            near[1][1], near[2][1] = late_x, late_y
            across = [
                own_corner,
                swap(cut_rows(late_x, 0, half), "req", 4),
                swap(cut_rows(late_y, half, half), "req", 2),
            ]
    hidden, = sums


    def down(wanted, *after):
        weights = [w_down[2 * c + 1] for c in wanted] + [w_down[2 * c] for c in wanted]
        parts = pl.pallas_call(
            functools.partial(down_kernel, len(weights)),
            out_shape=[jax.ShapeDtypeStruct((all_rows, columns), BF16) for _ in wanted]
            + [jax.ShapeDtypeStruct((all_rows, columns), F32) for _ in wanted],
            in_specs=[vmem] * (1 + len(weights)) + [anywhere] * len(after),
            out_specs=[vmem] * len(weights),
            compiler_params=params(5),
            cost_estimate=pl.CostEstimate(flops=1, bytes_accessed=1, transcendentals=0),
            name="down",
        )(hidden, *weights, *after)
        far_parts, near_parts = parts[: len(wanted)], parts[len(wanted) :]
        return [(mine, swap(other, "req", 1)) for mine, other in zip(near_parts, far_parts)]

    def merge(c, layout, halves, passed=(), extra=()):
        layout = [[order.index(a) for a in blocks] for blocks in layout]
        passed = [order.index(a) for a in passed]
        return pl.pallas_call(
            functools.partial(merge_kernel, block, layout, passed),
            out_shape=[
                jax.ShapeDtypeStruct((len(blocks) * block, columns), BF16 if c else F32)
                for blocks in layout
            ],
            in_specs=[vmem] * (2 + len(extra)),
            out_specs=[vmem] * len(layout),
            compiler_params=params(4),
            name="merge",
        )(*halves, *extra)

    def total(blocks, parts):
        return pl.pallas_call(
            functools.partial(total_kernel, len(parts)),
            out_shape=[
                jax.ShapeDtypeStruct((block, columns), BF16 if a else F32) for a in blocks
            ],
            in_specs=[vmem] * len(parts),
            out_specs=[vmem] * len(blocks),
            compiler_params=params(4),
            name="total",
        )(*parts)

    totals = {}
    if squares:
        (corner,), (halves_x,) = down([3]), down([1])
        by_x, by_y = merge(3, [[2, 0], [3, 1]], corner)
        (halves_y,), (halves_own,) = down([2], by_x), down([0], by_x)
        by_x, by_y = swap(by_x, "req", 2), swap(by_y, "req", 4)
        layout = [[1, 0], [2, 3]]
        own = merge(0, layout, halves_own)
        to_x = merge(1, layout, halves_x, (3, 1), (by_y,))
        to_y = merge(2, layout, halves_y, (2, 0), (by_x,))
        for n, blocks in enumerate(layout):
            parts = [own[n], swap(to_x[n], "req", 2), swap(to_y[n], "req", 4)]
            totals.update(zip(blocks, total(blocks, parts)))
    else:
        layout = [list(range(1, head_devices)), [0]]
        merged = [merge(c, layout, down([c])[0]) for c in range(chips)]
        for n, blocks in enumerate(layout):
            parts = [merged[0][n]] + [swap(merged[c][n], "req", 2 * c) for c in range(1, chips)]
            totals.update(zip(blocks, total(blocks, parts)))
    output = state.astype(F32) + totals[0]
    for a in range(head_devices - 1, 0, -1):
        output += swap(totals[a], "head", a).astype(F32)
    return output.astype(BF16)


def solution(mesh):
    return jax.shard_map(
        shards,
        mesh=mesh,
        in_specs=(
            P("req", "head"),
            P("req", "head"),
            P("req", "head"),
            P("req", None, "head"),
            P("req", None, "head"),
            P("req", None),
            P("req"),
            P("head", "req"),
            P("head", "req"),
            P(),
            P(None, ("req", "head")),
            P(None, ("req", "head")),
            P(("req", "head"), None),
        ),
        out_specs=P("head", "req"),
        check_vma=False,
    )
```

```python
import functools
import math

import jax
import jax.numpy as jnp
from jax import lax
from jax.experimental import pallas as pl
from jax.experimental.pallas import tpu as pltpu
from jax.sharding import PartitionSpec as P

HEAD_DIM = 128
LO = 64
NEGATIVE_FILL = -1e30
NORM_EPS = 1e-06
BF16 = jnp.bfloat16
F32 = jnp.float32


def swap(array, axis, bits):
    size = lax.axis_size(axis)
    return lax.ppermute(array, axis, [(i, i ^ bits) for i in range(size)])


def in_vmem(array):
    return pltpu.with_memory_space_constraint(array, pltpu.VMEM)


def in_hbm(array):
    return pltpu.with_memory_space_constraint(array, pltpu.HBM)


def params(mebibytes=8):
    return pltpu.CompilerParams(vmem_limit_bytes=mebibytes * 1024 * 1024)


def stage_kernel(count, pieces, *refs):
    sources, outs, sems = refs[:count], refs[-1 - count : -1], refs[-1]
    copies = []
    for n in range(count):
        rows = sources[n].shape[0] // pieces // 16 * 16
        for p in range(pieces):
            size = rows if p < pieces - 1 else sources[n].shape[0] - rows * (pieces - 1)
            here = pl.ds(p * rows, size)
            copies.append(
                pltpu.make_async_copy(
                    sources[n].at[here], outs[n].at[here], sems.at[n * pieces + p]
                )
            )
    for copy in copies:
        copy.start()
    for copy in copies:
        copy.wait()


def staged(after, *arrays, name):
    pieces = 4
    size = sum(math.prod(array.shape) * 2 for array in arrays)
    return pl.pallas_call(
        functools.partial(stage_kernel, len(arrays), pieces),
        out_shape=[jax.ShapeDtypeStruct(array.shape, array.dtype) for array in arrays],
        in_specs=[pl.BlockSpec(memory_space=pl.ANY)] * (len(arrays) + len(after)),
        out_specs=[pl.BlockSpec(memory_space=pl.ANY)] * len(arrays),
        scratch_shapes=[pltpu.SemaphoreType.DMA((len(arrays) * pieces,))],
        compiler_params=params(1),
        cost_estimate=pl.CostEstimate(flops=0, bytes_accessed=size, transcendentals=0),
        name=name,
    )(*[in_hbm(array) for array in arrays], *after)


def split_kernel(count, wanted, place, *refs):
    sources, outs, sems = refs[:count], refs[-1 - len(wanted) : -1], refs[-1]
    copies = []
    for k, ((n, t), out) in enumerate(zip(wanted, outs)):
        width = out.shape[1]
        here = pl.ds(pl.multiple_of((place[0] ^ t) * width, width), width)
        copies.append(pltpu.make_async_copy(sources[n].at[:, here], out, sems.at[k]))
    for copy in copies:
        copy.start()
    for copy in copies:
        copy.wait()


def keys_kernel(pieces, keys, *refs):
    keys_copy, top, weight, acc, sems = refs[-5:]
    cut = keys.shape[0] // pieces
    copies = [
        pltpu.make_async_copy(
            keys.at[pl.ds(n * cut, cut)], keys_copy.at[pl.ds(n * cut, cut)], sems.at[n]
        )
        for n in range(pieces)
    ]
    for copy in copies:
        copy.start()
    top[...] = jnp.full(top.shape, NEGATIVE_FILL, F32)
    weight[...] = jnp.zeros(weight.shape, F32)
    acc[...] = jnp.zeros(acc.shape, F32)
    for copy in copies:
        copy.wait()


def staged_blocks(place, width, after, arrays, wanted, name):
    anywhere = pl.BlockSpec(memory_space=pl.ANY)
    shapes = [jax.ShapeDtypeStruct((arrays[n].shape[0], width), arrays[n].dtype) for n, _ in wanted]
    return pl.pallas_call(
        functools.partial(split_kernel, len(arrays), wanted),
        out_shape=shapes,
        in_specs=[pl.BlockSpec(memory_space=pltpu.SMEM)] + [anywhere] * (len(arrays) + len(after)),
        out_specs=[anywhere] * len(wanted),
        scratch_shapes=[pltpu.SemaphoreType.DMA((len(wanted),))],
        compiler_params=params(1),
        cost_estimate=pl.CostEstimate(
            flops=0,
            bytes_accessed=sum(2 * math.prod(shape.shape) for shape in shapes),
            transcendentals=0,
        ),
        name=name,
    )(place, *[in_hbm(array) for array in arrays], *after)


def pack_kernel(page_len, place, lengths, table, queries, out, held_queries, sem):
    del place
    copy = pltpu.make_async_copy(queries, held_queries, sem)
    copy.start()
    reqs, slots = table.shape
    query_rows = queries.shape[0] * queries.shape[1] // HEAD_DIM
    inverse_rows = out.shape[0] - query_rows
    high = lax.broadcasted_iota(jnp.int32, (inverse_rows, slots), 0)
    lane = lax.broadcasted_iota(jnp.int32, (2 * LO, slots), 0)
    first = lax.broadcasted_iota(jnp.int32, (1, slots), 1) * page_len
    total = jnp.zeros((inverse_rows, 2 * LO), F32)
    for r in range(reqs):
        ids = table[pl.ds(r, 1), :]
        tokens = jnp.clip(lengths[r] - first, 0, page_len)
        row_hit = jnp.where((ids >> 6) == high, 1.0, 0.0).astype(BF16)
        held = jnp.where(lane < LO, r + 1, tokens)
        lane_hit = jnp.where((ids & (LO - 1)) == (lane & (LO - 1)), held, 0).astype(F32).astype(BF16)
        total += lax.dot_general(
            row_hit, lane_hit, (((1,), (1,)), ((), ())), preferred_element_type=F32
        )
    copy.wait()
    own = held_queries[...].astype(F32).reshape(query_rows, HEAD_DIM)
    out[pl.ds(0, query_rows), :] = own.astype(BF16)
    out[pl.ds(query_rows, inverse_rows), :] = total.astype(BF16)


def stack_kernel(count, *refs):
    out = refs[-1]
    at = 0
    for piece in refs[:count]:
        out[pl.ds(at, piece.shape[0]), :] = piece[...]
        at += piece.shape[0]


def stacked(pieces, *after):
    vmem = pl.BlockSpec(memory_space=pltpu.VMEM)
    rows = sum(piece.shape[0] for piece in pieces)
    return pl.pallas_call(
        functools.partial(stack_kernel, len(pieces)),
        out_shape=jax.ShapeDtypeStruct((rows, pieces[0].shape[1]), pieces[0].dtype),
        in_specs=[vmem] * len(pieces) + [pl.BlockSpec(memory_space=pl.ANY)] * len(after),
        out_specs=vmem,
        compiler_params=params(4),
        name="stack",
    )(*pieces, *after)


def rows_kernel(first, source, out):
    out[...] = source[pl.ds(first, out.shape[0]), :]


def cut_rows(array, first, size):
    vmem = pl.BlockSpec(memory_space=pltpu.VMEM)
    return pl.pallas_call(
        functools.partial(rows_kernel, first),
        out_shape=jax.ShapeDtypeStruct((size, array.shape[1]), array.dtype),
        in_specs=[vmem],
        out_specs=vmem,
        compiler_params=params(2),
        name="rows",
    )(array)


def attend_kernel(
    devices, heads, kv_local, reqs, step_pages, place, *refs
):
    sources, refs = refs[:devices], refs[devices:]
    (keys, value_pool, w_out, w_up), refs = refs[:4], refs[7:]
    outs, (top, weight, acc), refs = refs[:-11], refs[-11:-8], refs[-8:]
    outs, w_out_copy, w_up_copies = outs[:devices], outs[devices], outs[devices + 1 :]
    query, score, found, index, values, sem, value_sem, out_sem = refs
    chips = len(outs) // 2
    pages = keys.shape[0]
    steps = pages // step_pages
    rows = reqs * heads
    inverse_rows = sources[0].shape[0] - rows
    group = heads // kv_local
    scale = 1.0 / math.sqrt(HEAD_DIM)
    lane = lax.broadcasted_iota(jnp.int32, (heads, HEAD_DIM), 1)
    head = lax.broadcasted_iota(jnp.int32, (heads, HEAD_DIM), 0)

    cut = pages // value_sem.shape[0]
    loads = [
        pltpu.make_async_copy(
            value_pool.at[pl.ds(n * cut, cut)], values.at[pl.ds(n * cut, cut)], value_sem.at[n]
        )
        for n in range(value_sem.shape[0])
    ]
    for load in loads:
        load.start()

    wanted = place[0] * (pages // LO) + lax.broadcasted_iota(jnp.int32, (8, inverse_rows), 0)
    pick = jnp.where(lax.broadcasted_iota(jnp.int32, (8, inverse_rows), 1) == wanted, 1.0, 0.0)
    half = lax.broadcasted_iota(jnp.int32, (8, 2 * LO), 1)
    total = jnp.zeros((8, 2 * LO), F32)
    for n, source in enumerate(sources):
        query[pl.ds(n * rows, rows), :] = source[pl.ds(0, rows), :].astype(F32)
        part = jnp.dot(
            pick.astype(BF16), source[pl.ds(rows, inverse_rows), :], preferred_element_type=F32
        )
        total += jnp.where((half < LO) & (part > 0.0), part + (n * reqs - 1), part)
    found[...] = total.astype(jnp.int32)
    copy = pltpu.make_async_copy(found, index, sem)
    copy.start()
    copy.wait()

    def rows_of(page):
        return pl.ds(pl.multiple_of(index[page // LO, page % LO] * heads, heads), heads)

    def tokens_of(page):
        return index[page // LO, LO + page % LO]

    @pl.loop(0, steps)
    def _(step):
        first = step * step_pages
        scores = []
        for p in range(step_pages):
            q = query[rows_of(first + p), :]
            q = jnp.concatenate(
                [jnp.where(head // group == kv, q, 0.0) for kv in range(kv_local)], axis=1
            ).astype(BF16)
            s = lax.dot_general(
                q, keys[first + p], (((1,), (1,)), ((), ())), preferred_element_type=F32
            ) * scale
            scores.append(jnp.where(lane < tokens_of(first + p), s, NEGATIVE_FILL))
        best = [jnp.max(s, axis=1, keepdims=True).astype(BF16).astype(F32) for s in scores]
        for p in range(step_pages):
            score[first + p] = scores[p]
        for p in range(step_pages):
            at = rows_of(first + p)
            top[at, :] = jnp.maximum(top[at, :], best[p])

    for load in loads:
        load.wait()
    weight_loads = [pltpu.make_async_copy(w_out, w_out_copy, out_sem.at[len(w_up_copies)])]
    for t, copied in enumerate(w_up_copies):
        width = copied.shape[1]
        here = pl.ds(pl.multiple_of((place[0] ^ t) * width, width), width)
        weight_loads.append(pltpu.make_async_copy(w_up.at[:, here], copied, out_sem.at[t]))
    for load in weight_loads:
        load.start()

    @pl.loop(0, steps)
    def _(step):
        first = step * step_pages
        sums, parts = [], []
        for p in range(step_pages):
            page = first + p
            w = jnp.exp(score[page] - top[rows_of(page), :])
            w = jnp.where(lane < tokens_of(page), w, 0.0).astype(BF16)
            a = jnp.dot(w, values[page], preferred_element_type=F32)
            part = a[:, :HEAD_DIM]
            for kv in range(1, kv_local):
                part = jnp.where(
                    head // group == kv, a[:, kv * HEAD_DIM : (kv + 1) * HEAD_DIM], part
                )
            parts.append(part)
            sums.append(jnp.sum(w.astype(F32), axis=1, keepdims=True))
        for p in range(step_pages):
            at = rows_of(first + p)
            acc[at, :] += parts[p]
            weight[at, :] += sums[p]

    lane3 = lax.broadcasted_iota(jnp.int32, (reqs, heads, HEAD_DIM), 2)
    head3 = lax.broadcasted_iota(jnp.int32, (reqs, heads, HEAD_DIM), 1)
    for n, out in enumerate(outs):
        at = pl.ds(n * rows, rows)
        out[pl.ds(0, rows), :] = acc[at, :].astype(BF16)
        t = top[at, :].reshape(reqs, heads, HEAD_DIM)
        s = weight[at, :].reshape(reqs, heads, HEAD_DIM)
        s_high = s.astype(BF16).astype(F32)
        stats = jnp.where(lane3 == head3 + 2 * heads, s - s_high, 0.0)
        stats = jnp.where(lane3 == head3 + heads, s_high, stats)
        stats = jnp.where(lane3 == head3, t, stats)
        out[pl.ds(rows, reqs), :] = jnp.sum(stats, axis=1).astype(BF16)
    for load in weight_loads:
        load.wait()


def join_kernel(heads, reqs, *refs):
    count = len(refs) // 3
    rows = reqs * heads
    lane = lax.broadcasted_iota(jnp.int32, (reqs, HEAD_DIM), 1)
    lane3 = lax.broadcasted_iota(jnp.int32, (reqs, heads, HEAD_DIM), 2)
    head3 = lax.broadcasted_iota(jnp.int32, (reqs, heads, HEAD_DIM), 1)

    def wide(array):
        return jnp.sum(jnp.where(lane3 == head3, array[:, None, :], 0.0), axis=2, keepdims=True)

    for n in range(count):
        pair, out = (refs[n], refs[count + n]), refs[2 * count + n]
        stats = [ref[pl.ds(rows, reqs), :].astype(F32) for ref in pair]
        best = jnp.maximum(*stats)
        weight, acc = 0.0, 0.0
        for stat, ref in zip(stats, pair):
            factor = jnp.exp(stat - best)
            weight += factor * (
                pltpu.roll(stat, HEAD_DIM - heads, 1) + pltpu.roll(stat, HEAD_DIM - 2 * heads, 1)
            )
            part = ref[pl.ds(0, rows), :].astype(F32).reshape(reqs, heads, HEAD_DIM)
            acc += wide(factor) * part
        high = weight.astype(BF16).astype(F32)
        low = pltpu.roll(weight - high, 2 * heads, 1)
        joined = jnp.where(lane < 2 * heads, pltpu.roll(high, heads, 1), low)
        joined = jnp.where(lane < heads, best, jnp.where(lane < 3 * heads, joined, 0.0))
        out[pl.ds(0, rows), :] = acc.reshape(rows, HEAD_DIM).astype(BF16)
        out[pl.ds(rows, reqs), :] = joined.astype(BF16)


def combine_kernel(heads, queries, key_new, value_new, *refs):
    parts, out = refs[1:-1], refs[-1]
    reqs = key_new.shape[0]
    rows = reqs * heads
    lane3 = lax.broadcasted_iota(jnp.int32, (reqs, heads, HEAD_DIM), 2)
    head3 = lax.broadcasted_iota(jnp.int32, (reqs, heads, HEAD_DIM), 1)
    diagonal = lane3 == head3

    def narrow(array):
        return jnp.sum(jnp.where(diagonal, array.reshape(reqs, heads, HEAD_DIM), 0.0), axis=1)

    def wide(array):
        return jnp.sum(jnp.where(diagonal, array[:, None, :], 0.0), axis=2, keepdims=True)

    def per_head(ref):
        kv_local = ref.shape[1] // HEAD_DIM
        array = ref[...].astype(F32)
        return jnp.concatenate(
            [
                jnp.broadcast_to(
                    array[:, None, kv * HEAD_DIM : (kv + 1) * HEAD_DIM],
                    (reqs, heads // kv_local, HEAD_DIM),
                )
                for kv in range(kv_local)
            ],
            axis=1,
        )

    own = queries[pl.ds(0, rows), :].astype(F32).reshape(reqs, heads, HEAD_DIM) * per_head(key_new)
    own = jnp.sum(own, axis=2, keepdims=True) * (1.0 / math.sqrt(HEAD_DIM))
    own = narrow(jnp.broadcast_to(own, (reqs, heads, HEAD_DIM)))
    stats = [part[pl.ds(rows, reqs), :].astype(F32) for part in parts]
    best = functools.reduce(jnp.maximum, stats, own)
    own_factor = jnp.exp(own - best)
    factors = [jnp.exp(stat - best) for stat in stats]
    total = own_factor
    for stat, factor in zip(stats, factors):
        total += factor * (
            pltpu.roll(stat, HEAD_DIM - heads, 1) + pltpu.roll(stat, HEAD_DIM - 2 * heads, 1)
        )
    share = 1.0 / total
    attention = wide(own_factor * share) * per_head(value_new)
    for part, factor in zip(parts, factors):
        attention += wide(factor * share) * part[pl.ds(0, rows), :].astype(F32).reshape(
            reqs, heads, HEAD_DIM
        )
    out[...] = attention.reshape(reqs, heads * HEAD_DIM).astype(BF16)


def project_kernel(chips, place, *refs):
    near, far, w_out = refs[:chips], refs[chips : 2 * chips], refs[2 * chips]
    outs, lines = refs[2 * chips + 1 : -1], refs[-1]
    reqs = near[0].shape[0]
    block = outs[0].shape[0]

    for side, line in enumerate((near, far)):
        for chip in range(chips):
            first = (place[0] ^ (2 * chip + side)) * reqs
            at = ((first // block) ^ place[1]) * block + first % block
            lines[pl.ds(pl.multiple_of(at, reqs), reqs), :] = line[chip][...]

    product = jnp.dot(lines[...], w_out[...], preferred_element_type=F32)
    for a, out in enumerate(outs):
        out[...] = product[a * block : (a + 1) * block].astype(out.dtype)


def state_kernel(ready, residual, *refs):
    del ready
    total = residual[...].astype(F32)
    for part in refs[:-1]:
        total += part[...].astype(F32)
    refs[-1][...] = total.astype(BF16)


def gain_kernel(gain, out):
    out[...] = gain[...].astype(F32)


def hidden_kernel(groups, waits, chip, last, total_width, place, *refs):
    pieces, refs = refs[: 2 * groups], refs[2 * groups :]
    gain, w_gate, w_up = refs[0], refs[1:3], refs[3:5]
    before = refs[5:8] if chip else None
    outs, lines = refs[(8 if chip else 5) + waits : -1], refs[-1]
    rows = lines.shape[1]
    units = w_gate[0].shape[0]
    contract = (((1,), (1,)), ((), ()))
    square = [None] * groups
    for side in range(2):
        scale = gain[pl.ds(place[0] ^ (2 * chip + side), 1), :]
        at = 0
        for n, piece in enumerate(pieces[side * groups : (side + 1) * groups]):
            state = piece[...].astype(F32)
            part = jnp.sum(state * state, axis=1, keepdims=True)
            square[n] = part if side == 0 else square[n] + part
            lines[side, pl.ds(at, piece.shape[0]), :] = (state * scale).astype(BF16)
            at += piece.shape[0]
    square = jnp.broadcast_to(jnp.concatenate(square, axis=0), (rows, HEAD_DIM))
    if before is not None:
        square = square + before[2][...]
    if last:
        factor = lax.rsqrt(square.T[0:1, :] * (1.0 / total_width) + NORM_EPS)
    for first in range(0, units, 512):
        here = slice(first, min(first + 512, units))
        sums = []
        for n, weight in enumerate((w_gate, w_up)):
            total = None if before is None else before[n][here, :]
            for side in range(2):
                part = lax.dot_general(
                    weight[side][here, :], lines[side], contract, preferred_element_type=F32
                )
                total = part if total is None else total + part
            sums.append(total)
        if last:
            gate = sums[0] * factor
            hidden = gate / (1.0 + jnp.exp(-gate)) * (sums[1] * factor)
            outs[0][:, here] = hidden.T.astype(BF16)
        else:
            outs[0][here, :], outs[1][here, :] = sums
    if not last:
        outs[2][...] = square
    elif waits:
        product = jnp.dot(outs[0][...], refs[8][...], preferred_element_type=F32)
        outs[1][...] = product.astype(BF16)


def down_kernel(count, hidden, *refs):
    for weight, out in zip(refs[:count], refs[-count:]):
        out[...] = jnp.dot(hidden[...], weight[...], preferred_element_type=F32).astype(out.dtype)


def merge_kernel(block, layout, passed, mine, other, *refs):
    outs = refs[len(refs) - len(layout) :]
    for out, blocks in zip(outs, layout):
        for n, a in enumerate(blocks):
            here = pl.ds(a * block, block)
            total = mine[here, :] + other[here, :].astype(F32)
            if a in passed:
                total += refs[0][pl.ds(passed.index(a) * block, block), :].astype(F32)
            out[pl.ds(n * block, block), :] = total.astype(out.dtype)


def total_kernel(count, *refs):
    parts, outs = refs[:count], refs[count:]
    at = 0
    for out in outs:
        here = pl.ds(at, out.shape[0])
        at += out.shape[0]
        total = parts[0][here, :]
        for part in parts[1:]:
            total = total + part[here, :].astype(F32)
        out[...] = total.astype(out.dtype)


def shards(
    queries, key_new, value_new, key_pool, value_pool, page_table, lengths, residual_in,
    w_out, norm_gain, w_gate, w_up, w_down,
):
    req_devices = lax.axis_size("req")
    head_devices = lax.axis_size("head")
    chips = req_devices // 2
    reqs = queries.shape[0]
    heads = queries.shape[1] // HEAD_DIM
    kv_local = key_new.shape[1] // HEAD_DIM
    hidden_width = w_down.shape[0]
    rows = reqs * heads
    pages, page_len = key_pool.shape[:2]
    me = lax.axis_index("req")
    place = jnp.stack([me, lax.axis_index("head")]).astype(jnp.int32)
    vmem = pl.BlockSpec(memory_space=pltpu.VMEM)
    smem = pl.BlockSpec(memory_space=pltpu.SMEM)
    anywhere = pl.BlockSpec(memory_space=pl.ANY)

    inverse_rows = -(-(pages * req_devices // LO) // 16) * 16
    payload = pl.pallas_call(
        functools.partial(pack_kernel, page_len),
        out_shape=jax.ShapeDtypeStruct((rows + inverse_rows, HEAD_DIM), BF16),
        in_specs=[smem, smem, vmem, anywhere],
        out_specs=vmem,
        scratch_shapes=[pltpu.VMEM(queries.shape, BF16), pltpu.SemaphoreType.DMA],
        compiler_params=params(),
        name="pack",
    )(place, in_hbm(lengths), in_hbm(page_table), in_hbm(queries))
    near = [payload] + [swap(payload, "req", 2 * c) for c in range(1, chips)]
    columns = w_out.shape[1]
    gain = pl.pallas_call(
        gain_kernel,
        out_shape=jax.ShapeDtypeStruct((req_devices, columns), F32),
        in_specs=[vmem],
        out_specs=vmem,
        compiler_params=params(1),
        name="gain",
    )(norm_gain.reshape(req_devices, columns))
    total_rows = rows * req_devices
    running = jax.ShapeDtypeStruct((total_rows, HEAD_DIM), F32)
    keys, *terms = pl.pallas_call(
        functools.partial(keys_kernel, 4),
        out_shape=[jax.ShapeDtypeStruct(key_pool.shape, BF16)] + [running] * 3,
        in_specs=[anywhere] * 3,
        out_specs=[anywhere] + [vmem] * 3,
        scratch_shapes=[pltpu.SemaphoreType.DMA((4,))],
        compiler_params=params(1),
        cost_estimate=pl.CostEstimate(
            flops=0, bytes_accessed=2 * math.prod(key_pool.shape), transcendentals=0
        ),
        name="stage_keys",
    )(in_hbm(key_pool), payload, gain)
    near = [payload] + [stacked([x], keys) for x in near[1:]]
    far = [swap(x, "req", 1) for x in near]

    step_pages = 64
    sent = jax.ShapeDtypeStruct((rows + reqs, HEAD_DIM), BF16)
    copied = jax.ShapeDtypeStruct((hidden_width, columns), BF16)
    steps, early, w_up = range(req_devices), req_devices // 4, w_up.T
    attended = pl.pallas_call(
        functools.partial(attend_kernel, req_devices, heads, kv_local, reqs, step_pages),
        out_shape=[sent] * req_devices
        + [jax.ShapeDtypeStruct(w_out.shape, BF16)]
        + [copied] * early
        + [running] * 3,
        in_specs=[smem] + [vmem] * (req_devices + 1) + [anywhere] * 3 + [vmem] * 3,
        out_specs=[vmem] * req_devices + [anywhere] * (1 + early) + [vmem] * 3,
        input_output_aliases={
            req_devices + 5 + n: req_devices + 1 + early + n for n in range(3)
        },
        scratch_shapes=[
            pltpu.VMEM((total_rows, HEAD_DIM), F32),
            pltpu.VMEM((pages, heads, HEAD_DIM), F32),
            pltpu.VMEM((8, 2 * LO), jnp.int32),
            pltpu.SMEM((8, 2 * LO), jnp.int32),
            pltpu.VMEM(value_pool.shape, BF16),
            pltpu.SemaphoreType.DMA,
            pltpu.SemaphoreType.DMA((4,)),
            pltpu.SemaphoreType.DMA((early + 1,)),
        ],
        compiler_params=params(20),
        name="attend",
    )(place, *near, *far, keys, in_hbm(value_pool), in_hbm(w_out), in_hbm(w_up), *terms)
    partials, w_out, first_up = (
        attended[:req_devices], attended[req_devices], attended[req_devices + 1 : -3]
    )
    joined = pl.pallas_call(
        functools.partial(join_kernel, heads, reqs),
        out_shape=[sent] * chips,
        in_specs=[vmem] * (2 * chips),
        out_specs=[vmem] * chips,
        compiler_params=params(6),
        name="join",
    )(*partials[:chips], *[swap(part, "req", 1) for part in partials[chips:]])
    w_gate = staged_blocks(
        place, columns, [joined[0]], [w_gate.T], [(0, t) for t in steps], "stage_gate"
    )

    parts = [joined[0]] + [swap(joined[c], "req", 2 * c) for c in range(1, chips)]
    attention = pl.pallas_call(
        functools.partial(combine_kernel, heads),
        out_shape=jax.ShapeDtypeStruct((reqs, heads * HEAD_DIM), BF16),
        in_specs=[vmem] * 3 + [anywhere] + [vmem] * len(parts),
        out_specs=vmem,
        compiler_params=params(4),
        name="combine",
    )(payload, key_new, value_new, w_gate[0], *parts)

    near = [attention] + [swap(attention, "req", 2 * c) for c in range(1, chips)]
    far = [swap(x, "req", 1) for x in near]
    block = reqs * req_devices // head_devices
    summed = pl.pallas_call(
        functools.partial(project_kernel, chips),
        out_shape=[
            jax.ShapeDtypeStruct((block, columns), F32 if a == 0 else BF16)
            for a in range(head_devices)
        ],
        in_specs=[smem] + [vmem] * (2 * chips + 1),
        out_specs=[vmem] * head_devices,
        scratch_shapes=[pltpu.VMEM((block * head_devices, w_out.shape[0]), BF16)],
        compiler_params=params(5),
        name="project",
    )(place, *near, *far, w_out)
    later = [(0, t) for t in steps[early:]] + [(1, t) for t in steps]
    blocks = staged_blocks(place, columns, [summed[0]], [w_up, w_down], later, "stage_up_down")
    w_up, w_down = [*first_up, *blocks[: -len(steps)]], blocks[-len(steps) :]
    terms = [summed[0]] + [swap(summed[a], "head", a) for a in range(head_devices - 1, 0, -1)]
    state = pl.pallas_call(
        state_kernel,
        out_shape=jax.ShapeDtypeStruct((block, columns), BF16),
        in_specs=[anywhere] + [vmem] * (1 + head_devices),
        out_specs=vmem,
        compiler_params=params(4),
        name="state",
    )(w_down[0], residual_in, *terms)

    pieces = [state] + [swap(state, "head", a) for a in range(1, head_devices)]
    squares = chips == 4 and head_devices == 4
    order = [0, 3, 2, 1] if squares else list(range(head_devices))

    def spread(array):
        return [array] + [swap(array, "req", 2 * c) for c in range(1, chips)]

    if squares:
        own_x, own_y = swap(state, "req", 2), swap(state, "req", 4)
        own_corner = swap(own_x, "req", 4)
        late = stacked([pieces[a] for a in order[1:]], own_x, own_y, own_corner)
        half = late.shape[0] // 2
        late_x, late_y = swap(late, "req", 2), swap(late, "req", 4)
        near = [[state, late], [own_x, late_x], [own_y, late_y], []]
    else:
        first = spread(state)
        rest = spread(stacked(pieces[1:], *first[1:]))
        near = [[first[c], rest[c]] for c in range(chips)]
    all_rows = block * head_devices
    sums, square = [], []
    early_far = {c: [swap(near[c][0], "req", 1)] for c in range(chips - 1)} if squares else {}
    for c in range(chips):
        last = c == chips - 1
        if squares and last:
            near[c] = [across[0]] + [stacked([x], square[2]) for x in across[1:]]
        far = early_far.get(c, []) + [swap(x, "req", 1) for x in near[c][len(early_far.get(c, [])) :]]
        count = len(far)
        ready = early_far.get(2, []) if c == 1 else []
        if squares and last:
            ready = [w_down[2 * c + 1]]
        sums = pl.pallas_call(
            functools.partial(hidden_kernel, count, len(ready), c, last, columns * req_devices),
            out_shape=[jax.ShapeDtypeStruct((all_rows, hidden_width), BF16)]
            + [jax.ShapeDtypeStruct((all_rows, columns), BF16)] * len(ready)
            if last
            else [
                jax.ShapeDtypeStruct((hidden_width, all_rows), F32),
                jax.ShapeDtypeStruct((hidden_width, all_rows), F32),
                jax.ShapeDtypeStruct((all_rows, HEAD_DIM), F32),
            ],
            in_specs=[smem]
            + [vmem] * (2 * count + 5 + len(sums))
            + [vmem if last else anywhere] * len(ready),
            out_specs=[vmem] * (1 + len(ready) if last else 3),
            scratch_shapes=[pltpu.VMEM((2, all_rows, columns), BF16)],
            input_output_aliases={} if c == 0 or last else {2 * count + 6 + n: n for n in range(2)},
            compiler_params=params(5),
            cost_estimate=pl.CostEstimate(
                flops=8 * all_rows * columns * hidden_width, bytes_accessed=0, transcendentals=0
            ),
            name="hidden",
        )(
            place, *near[c], *far, gain, *w_gate[2 * c : 2 * c + 2], *w_up[2 * c : 2 * c + 2], *sums, *ready
        )
        if not last:
            square.append(sums[2])
        if squares and c == 0:
            late_x, late_y = stacked([late_x], square[0]), stacked([late_y], square[0])
            near[1][1], near[2][1] = late_x, late_y
            across = [
                own_corner,
                swap(cut_rows(late_x, 0, half), "req", 4),
                swap(cut_rows(late_y, half, half), "req", 2),
            ]
    hidden = sums[0]

    def down(wanted, *after, near_only=()):
        weights = [w_down[2 * c + 1] for c in wanted]
        weights += [w_down[2 * c] for c in (*wanted, *near_only)]
        parts = pl.pallas_call(
            functools.partial(down_kernel, len(weights)),
            out_shape=[jax.ShapeDtypeStruct((all_rows, columns), BF16) for _ in wanted]
            + [jax.ShapeDtypeStruct((all_rows, columns), F32) for _ in (*wanted, *near_only)],
            in_specs=[vmem] * (1 + len(weights)) + [anywhere] * len(after),
            out_specs=[vmem] * len(weights),
            compiler_params=params(5),
            cost_estimate=pl.CostEstimate(flops=1, bytes_accessed=1, transcendentals=0),
            name="down",
        )(hidden, *weights, *after)
        far_parts, near_parts = parts[: len(wanted)], parts[len(wanted) :]
        pairs = [(mine, swap(other, "req", 1)) for mine, other in zip(near_parts, far_parts)]
        return pairs + list(near_parts[len(wanted) :])

    def merge(c, layout, halves, passed=(), extra=()):
        layout = [[order.index(a) for a in blocks] for blocks in layout]
        passed = [order.index(a) for a in passed]
        return pl.pallas_call(
            functools.partial(merge_kernel, block, layout, passed),
            out_shape=[
                jax.ShapeDtypeStruct((len(blocks) * block, columns), BF16 if c else F32)
                for blocks in layout
            ],
            in_specs=[vmem] * (2 + len(extra)),
            out_specs=[vmem] * len(layout),
            compiler_params=params(4),
            name="merge",
        )(*halves, *extra)

    def total(blocks, parts):
        return pl.pallas_call(
            functools.partial(total_kernel, len(parts)),
            out_shape=[
                jax.ShapeDtypeStruct((block, columns), BF16 if a else F32) for a in blocks
            ],
            in_specs=[vmem] * len(parts),
            out_specs=[vmem] * len(blocks),
            compiler_params=params(4),
            name="total",
        )(*parts)

    totals = {}
    if squares:
        other = swap(sums[1], "req", 1)
        halves_x, corner = down([1], near_only=[3])
        corner = (corner, other)
        by_x, by_y = merge(3, [[2, 0], [3, 1]], corner)
        (halves_y,), (halves_own,) = down([2], by_x), down([0], by_x)
        by_x, by_y = swap(by_x, "req", 2), swap(by_y, "req", 4)
        layout = [[1, 0], [2, 3]]
        own = merge(0, layout, halves_own)
        to_x = merge(1, layout, halves_x, (3, 1), (by_y,))
        to_y = merge(2, layout, halves_y, (2, 0), (by_x,))
        for n, blocks in enumerate(layout):
            parts = [own[n], swap(to_x[n], "req", 2), swap(to_y[n], "req", 4)]
            totals.update(zip(blocks, total(blocks, parts)))
    else:
        layout = [list(range(1, head_devices)), [0]]
        merged = [merge(c, layout, down([c])[0]) for c in range(chips)]
        for n, blocks in enumerate(layout):
            parts = [merged[0][n]] + [swap(merged[c][n], "req", 2 * c) for c in range(1, chips)]
            totals.update(zip(blocks, total(blocks, parts)))
    output = state.astype(F32) + totals[0]
    for a in range(head_devices - 1, 0, -1):
        output += swap(totals[a], "head", a).astype(F32)
    return output.astype(BF16)


def solution(mesh):
    return jax.shard_map(
        shards,
        mesh=mesh,
        in_specs=(
            P("req", "head"),
            P("req", "head"),
            P("req", "head"),
            P("req", None, "head"),
            P("req", None, "head"),
            P("req", None),
            P("req"),
            P("head", "req"),
            P("head", "req"),
            P(),
            P(None, ("req", "head")),
            P(None, ("req", "head")),
            P(("req", "head"), None),
        ),
        out_specs=P("head", "req"),
        check_vma=False,
    )
```

```python
import functools
import math

import jax
import jax.numpy as jnp
from jax import lax
from jax.experimental import pallas as pl
from jax.experimental.pallas import tpu as pltpu
from jax.sharding import PartitionSpec as P

HEAD_DIM = 128
LO = 64
NEGATIVE_FILL = -1e30
NORM_EPS = 1e-06
BF16 = jnp.bfloat16
F32 = jnp.float32


def swap(array, axis, bits):
    size = lax.axis_size(axis)
    return lax.ppermute(array, axis, [(i, i ^ bits) for i in range(size)])


def in_vmem(array):
    return pltpu.with_memory_space_constraint(array, pltpu.VMEM)


def in_hbm(array):
    return pltpu.with_memory_space_constraint(array, pltpu.HBM)


def params(mebibytes=8):
    return pltpu.CompilerParams(vmem_limit_bytes=mebibytes * 1024 * 1024)


def stage_kernel(count, pieces, *refs):
    sources, outs, sems = refs[:count], refs[-1 - count : -1], refs[-1]
    copies = []
    for n in range(count):
        rows = sources[n].shape[0] // pieces // 16 * 16
        for p in range(pieces):
            size = rows if p < pieces - 1 else sources[n].shape[0] - rows * (pieces - 1)
            here = pl.ds(p * rows, size)
            copies.append(
                pltpu.make_async_copy(
                    sources[n].at[here], outs[n].at[here], sems.at[n * pieces + p]
                )
            )
    for copy in copies:
        copy.start()
    for copy in copies:
        copy.wait()


def staged(after, *arrays, name):
    pieces = 4
    size = sum(math.prod(array.shape) * 2 for array in arrays)
    return pl.pallas_call(
        functools.partial(stage_kernel, len(arrays), pieces),
        out_shape=[jax.ShapeDtypeStruct(array.shape, array.dtype) for array in arrays],
        in_specs=[pl.BlockSpec(memory_space=pl.ANY)] * (len(arrays) + len(after)),
        out_specs=[pl.BlockSpec(memory_space=pl.ANY)] * len(arrays),
        scratch_shapes=[pltpu.SemaphoreType.DMA((len(arrays) * pieces,))],
        compiler_params=params(1),
        cost_estimate=pl.CostEstimate(flops=0, bytes_accessed=size, transcendentals=0),
        name=name,
    )(*[in_hbm(array) for array in arrays], *after)


def split_kernel(count, wanted, place, *refs):
    sources, outs, sems = refs[:count], refs[-1 - len(wanted) : -1], refs[-1]
    copies = []
    for k, ((n, t), out) in enumerate(zip(wanted, outs)):
        width = out.shape[1]
        here = pl.ds(pl.multiple_of((place[0] ^ t) * width, width), width)
        copies.append(pltpu.make_async_copy(sources[n].at[:, here], out, sems.at[k]))
    for copy in copies:
        copy.start()
    for copy in copies:
        copy.wait()


def keys_kernel(pieces, keys, *refs):
    keys_copy, top, weight, acc, sems = refs[-5:]
    cut = keys.shape[0] // pieces
    copies = [
        pltpu.make_async_copy(
            keys.at[pl.ds(n * cut, cut)], keys_copy.at[pl.ds(n * cut, cut)], sems.at[n]
        )
        for n in range(pieces)
    ]
    for copy in copies:
        copy.start()
    top[...] = jnp.full(top.shape, NEGATIVE_FILL, F32)
    weight[...] = jnp.zeros(weight.shape, F32)
    acc[...] = jnp.zeros(acc.shape, F32)
    for copy in copies:
        copy.wait()


def staged_blocks(place, width, after, arrays, wanted, name):
    anywhere = pl.BlockSpec(memory_space=pl.ANY)
    shapes = [jax.ShapeDtypeStruct((arrays[n].shape[0], width), arrays[n].dtype) for n, _ in wanted]
    return pl.pallas_call(
        functools.partial(split_kernel, len(arrays), wanted),
        out_shape=shapes,
        in_specs=[pl.BlockSpec(memory_space=pltpu.SMEM)] + [anywhere] * (len(arrays) + len(after)),
        out_specs=[anywhere] * len(wanted),
        scratch_shapes=[pltpu.SemaphoreType.DMA((len(wanted),))],
        compiler_params=params(1),
        cost_estimate=pl.CostEstimate(
            flops=0,
            bytes_accessed=sum(2 * math.prod(shape.shape) for shape in shapes),
            transcendentals=0,
        ),
        name=name,
    )(place, *[in_hbm(array) for array in arrays], *after)


def pack_kernel(page_len, place, lengths, table, queries, out, held_queries, sem):
    del place
    copy = pltpu.make_async_copy(queries, held_queries, sem)
    copy.start()
    reqs, slots = table.shape
    query_rows = queries.shape[0] * queries.shape[1] // HEAD_DIM
    inverse_rows = out.shape[0] - query_rows
    high = lax.broadcasted_iota(jnp.int32, (inverse_rows, slots), 0)
    lane = lax.broadcasted_iota(jnp.int32, (2 * LO, slots), 0)
    first = lax.broadcasted_iota(jnp.int32, (1, slots), 1) * page_len
    total = jnp.zeros((inverse_rows, 2 * LO), F32)
    for r in range(reqs):
        ids = table[pl.ds(r, 1), :]
        tokens = jnp.clip(lengths[r] - first, 0, page_len)
        row_hit = jnp.where((ids >> 6) == high, 1.0, 0.0).astype(BF16)
        held = jnp.where(lane < LO, r + 1, tokens)
        lane_hit = jnp.where((ids & (LO - 1)) == (lane & (LO - 1)), held, 0).astype(F32).astype(BF16)
        total += lax.dot_general(
            row_hit, lane_hit, (((1,), (1,)), ((), ())), preferred_element_type=F32
        )
    copy.wait()
    own = held_queries[...].astype(F32).reshape(query_rows, HEAD_DIM)
    out[pl.ds(0, query_rows), :] = own.astype(BF16)
    out[pl.ds(query_rows, inverse_rows), :] = total.astype(BF16)


def stack_kernel(count, *refs):
    out = refs[-1]
    at = 0
    for piece in refs[:count]:
        out[pl.ds(at, piece.shape[0]), :] = piece[...]
        at += piece.shape[0]


def stacked(pieces, *after):
    vmem = pl.BlockSpec(memory_space=pltpu.VMEM)
    rows = sum(piece.shape[0] for piece in pieces)
    return pl.pallas_call(
        functools.partial(stack_kernel, len(pieces)),
        out_shape=jax.ShapeDtypeStruct((rows, pieces[0].shape[1]), pieces[0].dtype),
        in_specs=[vmem] * len(pieces) + [pl.BlockSpec(memory_space=pl.ANY)] * len(after),
        out_specs=vmem,
        compiler_params=params(4),
        name="stack",
    )(*pieces, *after)


def rows_kernel(first, source, out):
    out[...] = source[pl.ds(first, out.shape[0]), :]


def cut_rows(array, first, size):
    vmem = pl.BlockSpec(memory_space=pltpu.VMEM)
    return pl.pallas_call(
        functools.partial(rows_kernel, first),
        out_shape=jax.ShapeDtypeStruct((size, array.shape[1]), array.dtype),
        in_specs=[vmem],
        out_specs=vmem,
        compiler_params=params(2),
        name="rows",
    )(array)


def attend_kernel(
    devices, heads, kv_local, reqs, step_pages, place, *refs
):
    sources, refs = refs[:devices], refs[devices:]
    (keys, value_pool, w_out, w_up), refs = refs[:4], refs[7:]
    outs, (top, weight, acc), refs = refs[:-11], refs[-11:-8], refs[-8:]
    outs, w_out_copy, w_up_copies = outs[:devices], outs[devices], outs[devices + 1 :]
    query, score, found, index, values, sem, value_sem, out_sem = refs
    chips = len(outs) // 2
    pages = keys.shape[0]
    steps = pages // step_pages
    rows = reqs * heads
    inverse_rows = sources[0].shape[0] - rows
    group = heads // kv_local
    scale = 1.0 / math.sqrt(HEAD_DIM)
    lane = lax.broadcasted_iota(jnp.int32, (heads, HEAD_DIM), 1)
    head = lax.broadcasted_iota(jnp.int32, (heads, HEAD_DIM), 0)

    cut = pages // value_sem.shape[0]
    loads = [
        pltpu.make_async_copy(
            value_pool.at[pl.ds(n * cut, cut)], values.at[pl.ds(n * cut, cut)], value_sem.at[n]
        )
        for n in range(value_sem.shape[0])
    ]
    for load in loads:
        load.start()

    wanted = place[0] * (pages // LO) + lax.broadcasted_iota(jnp.int32, (8, inverse_rows), 0)
    pick = jnp.where(lax.broadcasted_iota(jnp.int32, (8, inverse_rows), 1) == wanted, 1.0, 0.0)
    half = lax.broadcasted_iota(jnp.int32, (8, 2 * LO), 1)
    total = jnp.zeros((8, 2 * LO), F32)
    for n, source in enumerate(sources):
        query[pl.ds(n * rows, rows), :] = source[pl.ds(0, rows), :].astype(query.dtype)
        part = jnp.dot(
            pick.astype(BF16), source[pl.ds(rows, inverse_rows), :], preferred_element_type=F32
        )
        total += jnp.where((half < LO) & (part > 0.0), part + (n * reqs - 1), part)
    found[...] = total.astype(jnp.int32)
    copy = pltpu.make_async_copy(found, index, sem)
    copy.start()
    copy.wait()

    def rows_of(page):
        return pl.ds(pl.multiple_of(index[page // LO, page % LO] * heads, heads), heads)

    def tokens_of(page):
        return index[page // LO, LO + page % LO]

    @pl.loop(0, steps)
    def _(step):
        first = step * step_pages
        scores = []
        for p in range(step_pages):
            q = query[rows_of(first + p), :].astype(F32)
            q = jnp.concatenate(
                [jnp.where(head // group == kv, q, 0.0) for kv in range(kv_local)], axis=1
            ).astype(BF16)
            s = lax.dot_general(
                q, keys[first + p], (((1,), (1,)), ((), ())), preferred_element_type=F32
            ) * scale
            scores.append(jnp.where(lane < tokens_of(first + p), s, NEGATIVE_FILL))
        best = [jnp.max(s, axis=1, keepdims=True).astype(BF16).astype(F32) for s in scores]
        for p in range(step_pages):
            score[first + p] = scores[p]
        for p in range(step_pages):
            at = rows_of(first + p)
            top[at, :] = jnp.maximum(top[at, :], best[p])

    for load in loads:
        load.wait()
    weight_loads = [pltpu.make_async_copy(w_out, w_out_copy, out_sem.at[len(w_up_copies)])]
    for t, copied in enumerate(w_up_copies):
        width = copied.shape[1]
        here = pl.ds(pl.multiple_of((place[0] ^ t) * width, width), width)
        weight_loads.append(pltpu.make_async_copy(w_up.at[:, here], copied, out_sem.at[t]))
    for load in weight_loads:
        load.start()

    @pl.loop(0, steps)
    def _(step):
        first = step * step_pages
        sums, parts = [], []
        for p in range(step_pages):
            page = first + p
            w = jnp.exp(score[page] - top[rows_of(page), :])
            w = jnp.where(lane < tokens_of(page), w, 0.0).astype(BF16)
            a = jnp.dot(w, values[page], preferred_element_type=F32)
            part = a[:, :HEAD_DIM]
            for kv in range(1, kv_local):
                part = jnp.where(
                    head // group == kv, a[:, kv * HEAD_DIM : (kv + 1) * HEAD_DIM], part
                )
            parts.append(part)
            sums.append(jnp.sum(w.astype(F32), axis=1, keepdims=True))
        for p in range(step_pages):
            at = rows_of(first + p)
            acc[at, :] += parts[p]
            weight[at, :] += sums[p]

    lane3 = lax.broadcasted_iota(jnp.int32, (reqs, heads, HEAD_DIM), 2)
    head3 = lax.broadcasted_iota(jnp.int32, (reqs, heads, HEAD_DIM), 1)
    for n, out in enumerate(outs):
        at = pl.ds(n * rows, rows)
        out[pl.ds(0, rows), :] = acc[at, :].astype(BF16)
        t = top[at, :].reshape(reqs, heads, HEAD_DIM)
        s = weight[at, :].reshape(reqs, heads, HEAD_DIM)
        s_high = s.astype(BF16).astype(F32)
        stats = jnp.where(lane3 == head3 + 2 * heads, s - s_high, 0.0)
        stats = jnp.where(lane3 == head3 + heads, s_high, stats)
        stats = jnp.where(lane3 == head3, t, stats)
        out[pl.ds(rows, reqs), :] = jnp.sum(stats, axis=1).astype(BF16)
    for load in weight_loads:
        load.wait()


def join_kernel(heads, reqs, *refs):
    count = len(refs) // 3
    rows = reqs * heads
    lane = lax.broadcasted_iota(jnp.int32, (reqs, HEAD_DIM), 1)
    lane3 = lax.broadcasted_iota(jnp.int32, (reqs, heads, HEAD_DIM), 2)
    head3 = lax.broadcasted_iota(jnp.int32, (reqs, heads, HEAD_DIM), 1)

    def wide(array):
        return jnp.sum(jnp.where(lane3 == head3, array[:, None, :], 0.0), axis=2, keepdims=True)

    for n in range(count):
        pair, out = (refs[n], refs[count + n]), refs[2 * count + n]
        stats = [ref[pl.ds(rows, reqs), :].astype(F32) for ref in pair]
        best = jnp.maximum(*stats)
        weight, acc = 0.0, 0.0
        for stat, ref in zip(stats, pair):
            factor = jnp.exp(stat - best)
            weight += factor * (
                pltpu.roll(stat, HEAD_DIM - heads, 1) + pltpu.roll(stat, HEAD_DIM - 2 * heads, 1)
            )
            part = ref[pl.ds(0, rows), :].astype(F32).reshape(reqs, heads, HEAD_DIM)
            acc += wide(factor) * part
        high = weight.astype(BF16).astype(F32)
        low = pltpu.roll(weight - high, 2 * heads, 1)
        joined = jnp.where(lane < 2 * heads, pltpu.roll(high, heads, 1), low)
        joined = jnp.where(lane < heads, best, jnp.where(lane < 3 * heads, joined, 0.0))
        out[pl.ds(0, rows), :] = acc.reshape(rows, HEAD_DIM).astype(BF16)
        out[pl.ds(rows, reqs), :] = joined.astype(BF16)


def combine_kernel(heads, queries, key_new, value_new, *refs):
    parts, out = refs[1:-1], refs[-1]
    reqs = key_new.shape[0]
    rows = reqs * heads
    lane3 = lax.broadcasted_iota(jnp.int32, (reqs, heads, HEAD_DIM), 2)
    head3 = lax.broadcasted_iota(jnp.int32, (reqs, heads, HEAD_DIM), 1)
    diagonal = lane3 == head3

    def narrow(array):
        return jnp.sum(jnp.where(diagonal, array.reshape(reqs, heads, HEAD_DIM), 0.0), axis=1)

    def wide(array):
        return jnp.sum(jnp.where(diagonal, array[:, None, :], 0.0), axis=2, keepdims=True)

    def per_head(ref):
        kv_local = ref.shape[1] // HEAD_DIM
        array = ref[...].astype(F32)
        return jnp.concatenate(
            [
                jnp.broadcast_to(
                    array[:, None, kv * HEAD_DIM : (kv + 1) * HEAD_DIM],
                    (reqs, heads // kv_local, HEAD_DIM),
                )
                for kv in range(kv_local)
            ],
            axis=1,
        )

    own = queries[pl.ds(0, rows), :].astype(F32).reshape(reqs, heads, HEAD_DIM) * per_head(key_new)
    own = jnp.sum(own, axis=2, keepdims=True) * (1.0 / math.sqrt(HEAD_DIM))
    own = narrow(jnp.broadcast_to(own, (reqs, heads, HEAD_DIM)))
    stats = [part[pl.ds(rows, reqs), :].astype(F32) for part in parts]
    best = functools.reduce(jnp.maximum, stats, own)
    own_factor = jnp.exp(own - best)
    factors = [jnp.exp(stat - best) for stat in stats]
    total = own_factor
    for stat, factor in zip(stats, factors):
        total += factor * (
            pltpu.roll(stat, HEAD_DIM - heads, 1) + pltpu.roll(stat, HEAD_DIM - 2 * heads, 1)
        )
    share = 1.0 / total
    attention = wide(own_factor * share) * per_head(value_new)
    for part, factor in zip(parts, factors):
        attention += wide(factor * share) * part[pl.ds(0, rows), :].astype(F32).reshape(
            reqs, heads, HEAD_DIM
        )
    out[...] = attention.reshape(reqs, heads * HEAD_DIM).astype(BF16)


def project_kernel(chips, place, *refs):
    near, far, w_out = refs[:chips], refs[chips : 2 * chips], refs[2 * chips]
    outs, lines = refs[2 * chips + 1 : -1], refs[-1]
    reqs = near[0].shape[0]
    block = outs[0].shape[0]

    for side, line in enumerate((near, far)):
        for chip in range(chips):
            first = (place[0] ^ (2 * chip + side)) * reqs
            at = ((first // block) ^ place[1]) * block + first % block
            lines[pl.ds(pl.multiple_of(at, reqs), reqs), :] = line[chip][...]

    product = jnp.dot(lines[...], w_out[...], preferred_element_type=F32)
    for a, out in enumerate(outs):
        out[...] = product[a * block : (a + 1) * block].astype(out.dtype)


def state_kernel(ready, residual, *refs):
    del ready
    total = residual[...].astype(F32)
    for part in refs[:-1]:
        total += part[...].astype(F32)
    refs[-1][...] = total.astype(BF16)


def gain_kernel(gain, out):
    out[...] = gain[...].astype(F32)


def hidden_kernel(groups, waits, chip, last, total_width, place, *refs):
    pieces, refs = refs[: 2 * groups], refs[2 * groups :]
    gain, w_gate, w_up = refs[0], refs[1:3], refs[3:5]
    before = refs[5:8] if chip else None
    outs, lines = refs[(8 if chip else 5) + waits : -1], refs[-1]
    rows = lines.shape[1]
    units = w_gate[0].shape[0]
    contract = (((1,), (1,)), ((), ()))
    square = [None] * groups
    for side in range(2):
        scale = gain[pl.ds(place[0] ^ (2 * chip + side), 1), :]
        at = 0
        for n, piece in enumerate(pieces[side * groups : (side + 1) * groups]):
            state = piece[...].astype(F32)
            part = jnp.sum(state * state, axis=1, keepdims=True)
            square[n] = part if side == 0 else square[n] + part
            lines[side, pl.ds(at, piece.shape[0]), :] = (state * scale).astype(BF16)
            at += piece.shape[0]
    square = jnp.broadcast_to(jnp.concatenate(square, axis=0), (rows, HEAD_DIM))
    if before is not None:
        square = square + before[2][...]
    if last:
        factor = lax.rsqrt(square.T[0:1, :] * (1.0 / total_width) + NORM_EPS)
    for first in range(0, units, 512):
        here = slice(first, min(first + 512, units))
        sums = []
        for n, weight in enumerate((w_gate, w_up)):
            total = None if before is None else before[n][here, :]
            for side in range(2):
                part = lax.dot_general(
                    weight[side][here, :], lines[side], contract, preferred_element_type=F32
                )
                total = part if total is None else total + part
            sums.append(total)
        if last:
            gate = sums[0] * factor
            hidden = gate / (1.0 + jnp.exp(-gate)) * (sums[1] * factor)
            outs[0][:, here] = hidden.T.astype(BF16)
        else:
            outs[0][here, :], outs[1][here, :] = sums
    if not last:
        outs[2][...] = square
    elif waits:
        product = jnp.dot(outs[0][...], refs[8][...], preferred_element_type=F32)
        outs[1][...] = product.astype(BF16)


def down_kernel(count, hidden, *refs):
    for weight, out in zip(refs[:count], refs[-count:]):
        out[...] = jnp.dot(hidden[...], weight[...], preferred_element_type=F32).astype(out.dtype)


def merge_kernel(block, layout, passed, mine, other, *refs):
    outs = refs[len(refs) - len(layout) :]
    for out, blocks in zip(outs, layout):
        for n, a in enumerate(blocks):
            here = pl.ds(a * block, block)
            total = mine[here, :] + other[here, :].astype(F32)
            if a in passed:
                total += refs[0][pl.ds(passed.index(a) * block, block), :].astype(F32)
            out[pl.ds(n * block, block), :] = total.astype(out.dtype)


def total_kernel(count, *refs):
    parts, outs = refs[:count], refs[count:]
    at = 0
    for out in outs:
        here = pl.ds(at, out.shape[0])
        at += out.shape[0]
        total = parts[0][here, :]
        for part in parts[1:]:
            total = total + part[here, :].astype(F32)
        out[...] = total.astype(out.dtype)


def shards(
    queries, key_new, value_new, key_pool, value_pool, page_table, lengths, residual_in,
    w_out, norm_gain, w_gate, w_up, w_down,
):
    req_devices = lax.axis_size("req")
    head_devices = lax.axis_size("head")
    chips = req_devices // 2
    reqs = queries.shape[0]
    heads = queries.shape[1] // HEAD_DIM
    kv_local = key_new.shape[1] // HEAD_DIM
    hidden_width = w_down.shape[0]
    rows = reqs * heads
    pages, page_len = key_pool.shape[:2]
    me = lax.axis_index("req")
    place = jnp.stack([me, lax.axis_index("head")]).astype(jnp.int32)
    vmem = pl.BlockSpec(memory_space=pltpu.VMEM)
    smem = pl.BlockSpec(memory_space=pltpu.SMEM)
    anywhere = pl.BlockSpec(memory_space=pl.ANY)

    inverse_rows = -(-(pages * req_devices // LO) // 16) * 16
    payload = pl.pallas_call(
        functools.partial(pack_kernel, page_len),
        out_shape=jax.ShapeDtypeStruct((rows + inverse_rows, HEAD_DIM), BF16),
        in_specs=[smem, smem, vmem, anywhere],
        out_specs=vmem,
        scratch_shapes=[pltpu.VMEM(queries.shape, BF16), pltpu.SemaphoreType.DMA],
        compiler_params=params(),
        name="pack",
    )(place, in_hbm(lengths), in_hbm(page_table), in_hbm(queries))
    near = [payload] + [swap(payload, "req", 2 * c) for c in range(1, chips)]
    columns = w_out.shape[1]
    gain = pl.pallas_call(
        gain_kernel,
        out_shape=jax.ShapeDtypeStruct((req_devices, columns), F32),
        in_specs=[vmem],
        out_specs=vmem,
        compiler_params=params(1),
        name="gain",
    )(norm_gain.reshape(req_devices, columns))
    total_rows = rows * req_devices
    running = jax.ShapeDtypeStruct((total_rows, HEAD_DIM), F32)
    keys, *terms = pl.pallas_call(
        functools.partial(keys_kernel, 4),
        out_shape=[jax.ShapeDtypeStruct(key_pool.shape, BF16)] + [running] * 3,
        in_specs=[anywhere] * 3,
        out_specs=[anywhere] + [vmem] * 3,
        scratch_shapes=[pltpu.SemaphoreType.DMA((4,))],
        compiler_params=params(1),
        cost_estimate=pl.CostEstimate(
            flops=0, bytes_accessed=2 * math.prod(key_pool.shape), transcendentals=0
        ),
        name="stage_keys",
    )(in_hbm(key_pool), payload, gain)
    near = [payload] + [stacked([x], keys) for x in near[1:]]
    far = [swap(x, "req", 1) for x in near]

    step_pages = 96
    sent = jax.ShapeDtypeStruct((rows + reqs, HEAD_DIM), BF16)
    copied = jax.ShapeDtypeStruct((hidden_width, columns), BF16)
    steps, early, w_up = range(req_devices), req_devices // 4, w_up.T
    attended = pl.pallas_call(
        functools.partial(attend_kernel, req_devices, heads, kv_local, reqs, step_pages),
        out_shape=[sent] * req_devices
        + [jax.ShapeDtypeStruct(w_out.shape, BF16)]
        + [copied] * early
        + [running] * 3,
        in_specs=[smem] + [vmem] * (req_devices + 1) + [anywhere] * 3 + [vmem] * 3,
        out_specs=[vmem] * req_devices + [anywhere] * (1 + early) + [vmem] * 3,
        input_output_aliases={
            req_devices + 5 + n: req_devices + 1 + early + n for n in range(3)
        },
        scratch_shapes=[
            pltpu.VMEM((total_rows, HEAD_DIM), F32 if heads % 16 else BF16),
            pltpu.VMEM((pages, heads, HEAD_DIM), F32),
            pltpu.VMEM((8, 2 * LO), jnp.int32),
            pltpu.SMEM((8, 2 * LO), jnp.int32),
            pltpu.VMEM(value_pool.shape, BF16),
            pltpu.SemaphoreType.DMA,
            pltpu.SemaphoreType.DMA((4,)),
            pltpu.SemaphoreType.DMA((early + 1,)),
        ],
        compiler_params=params(20),
        name="attend",
    )(place, *near, *far, keys, in_hbm(value_pool), in_hbm(w_out), in_hbm(w_up), *terms)
    partials, w_out, first_up = (
        attended[:req_devices], attended[req_devices], attended[req_devices + 1 : -3]
    )
    joined = pl.pallas_call(
        functools.partial(join_kernel, heads, reqs),
        out_shape=[sent] * chips,
        in_specs=[vmem] * (2 * chips),
        out_specs=[vmem] * chips,
        compiler_params=params(6),
        name="join",
    )(*partials[:chips], *[swap(part, "req", 1) for part in partials[chips:]])
    w_gate = staged_blocks(
        place, columns, [joined[0]], [w_gate.T], [(0, t) for t in steps], "stage_gate"
    )

    parts = [joined[0]] + [swap(joined[c], "req", 2 * c) for c in range(1, chips)]
    attention = pl.pallas_call(
        functools.partial(combine_kernel, heads),
        out_shape=jax.ShapeDtypeStruct((reqs, heads * HEAD_DIM), BF16),
        in_specs=[vmem] * 3 + [anywhere] + [vmem] * len(parts),
        out_specs=vmem,
        compiler_params=params(4),
        name="combine",
    )(payload, key_new, value_new, w_gate[0], *parts)

    near = [attention] + [swap(attention, "req", 2 * c) for c in range(1, chips)]
    far = [swap(x, "req", 1) for x in near]
    block = reqs * req_devices // head_devices
    summed = pl.pallas_call(
        functools.partial(project_kernel, chips),
        out_shape=[
            jax.ShapeDtypeStruct((block, columns), F32 if a == 0 else BF16)
            for a in range(head_devices)
        ],
        in_specs=[smem] + [vmem] * (2 * chips + 1),
        out_specs=[vmem] * head_devices,
        scratch_shapes=[pltpu.VMEM((block * head_devices, w_out.shape[0]), BF16)],
        compiler_params=params(5),
        name="project",
    )(place, *near, *far, w_out)
    later = [(0, t) for t in steps[early:]] + [(1, t) for t in steps]
    blocks = staged_blocks(place, columns, [summed[0]], [w_up, w_down], later, "stage_up_down")
    w_up, w_down = [*first_up, *blocks[: -len(steps)]], blocks[-len(steps) :]
    terms = [summed[0]] + [swap(summed[a], "head", a) for a in range(head_devices - 1, 0, -1)]
    state = pl.pallas_call(
        state_kernel,
        out_shape=jax.ShapeDtypeStruct((block, columns), BF16),
        in_specs=[anywhere] + [vmem] * (1 + head_devices),
        out_specs=vmem,
        compiler_params=params(4),
        name="state",
    )(w_down[0], residual_in, *terms)

    pieces = [state] + [swap(state, "head", a) for a in range(1, head_devices)]
    squares = chips == 4 and head_devices == 4
    order = [0, 3, 2, 1] if squares else list(range(head_devices))

    def spread(array):
        return [array] + [swap(array, "req", 2 * c) for c in range(1, chips)]

    if squares:
        own_x, own_y = swap(state, "req", 2), swap(state, "req", 4)
        own_corner = swap(own_x, "req", 4)
        late = stacked([pieces[a] for a in order[1:]], own_x, own_y, own_corner)
        half = late.shape[0] // 2
        late_x, late_y = swap(late, "req", 2), swap(late, "req", 4)
        near = [[state, late], [own_x, late_x], [own_y, late_y], []]
    else:
        first = spread(state)
        rest = spread(stacked(pieces[1:], *first[1:]))
        near = [[first[c], rest[c]] for c in range(chips)]
    all_rows = block * head_devices
    sums, square = [], []
    early_far = {c: [swap(near[c][0], "req", 1)] for c in range(chips - 1)} if squares else {}
    for c in range(chips):
        last = c == chips - 1
        if squares and last:
            near[c] = [across[0]] + [stacked([x], square[2]) for x in across[1:]]
        far = early_far.get(c, []) + [swap(x, "req", 1) for x in near[c][len(early_far.get(c, [])) :]]
        count = len(far)
        ready = early_far.get(2, []) if c == 1 else []
        if squares and last:
            ready = [w_down[2 * c + 1]]
        sums = pl.pallas_call(
            functools.partial(hidden_kernel, count, len(ready), c, last, columns * req_devices),
            out_shape=[jax.ShapeDtypeStruct((all_rows, hidden_width), BF16)]
            + [jax.ShapeDtypeStruct((all_rows, columns), BF16)] * len(ready)
            if last
            else [
                jax.ShapeDtypeStruct((hidden_width, all_rows), F32),
                jax.ShapeDtypeStruct((hidden_width, all_rows), F32),
                jax.ShapeDtypeStruct((all_rows, HEAD_DIM), F32),
            ],
            in_specs=[smem]
            + [vmem] * (2 * count + 5 + len(sums))
            + [vmem if last else anywhere] * len(ready),
            out_specs=[vmem] * (1 + len(ready) if last else 3),
            scratch_shapes=[pltpu.VMEM((2, all_rows, columns), BF16)],
            input_output_aliases={} if c == 0 or last else {2 * count + 6 + n: n for n in range(2)},
            compiler_params=params(5),
            cost_estimate=pl.CostEstimate(
                flops=8 * all_rows * columns * hidden_width, bytes_accessed=0, transcendentals=0
            ),
            name="hidden",
        )(
            place, *near[c], *far, gain, *w_gate[2 * c : 2 * c + 2], *w_up[2 * c : 2 * c + 2], *sums, *ready
        )
        if not last:
            square.append(sums[2])
        if squares and c == 0:
            late_x, late_y = stacked([late_x], square[0]), stacked([late_y], square[0])
            near[1][1], near[2][1] = late_x, late_y
            across = [
                own_corner,
                swap(cut_rows(late_x, 0, half), "req", 4),
                swap(cut_rows(late_y, half, half), "req", 2),
            ]
    hidden = sums[0]

    def down(wanted, *after, near_only=()):
        weights = [w_down[2 * c + 1] for c in wanted]
        weights += [w_down[2 * c] for c in (*wanted, *near_only)]
        parts = pl.pallas_call(
            functools.partial(down_kernel, len(weights)),
            out_shape=[jax.ShapeDtypeStruct((all_rows, columns), BF16) for _ in wanted]
            + [jax.ShapeDtypeStruct((all_rows, columns), F32) for _ in (*wanted, *near_only)],
            in_specs=[vmem] * (1 + len(weights)) + [anywhere] * len(after),
            out_specs=[vmem] * len(weights),
            compiler_params=params(5),
            cost_estimate=pl.CostEstimate(flops=1, bytes_accessed=1, transcendentals=0),
            name="down",
        )(hidden, *weights, *after)
        far_parts, near_parts = parts[: len(wanted)], parts[len(wanted) :]
        pairs = [(mine, swap(other, "req", 1)) for mine, other in zip(near_parts, far_parts)]
        return pairs + list(near_parts[len(wanted) :])

    def merge(c, layout, halves, passed=(), extra=()):
        layout = [[order.index(a) for a in blocks] for blocks in layout]
        passed = [order.index(a) for a in passed]
        return pl.pallas_call(
            functools.partial(merge_kernel, block, layout, passed),
            out_shape=[
                jax.ShapeDtypeStruct((len(blocks) * block, columns), BF16 if c else F32)
                for blocks in layout
            ],
            in_specs=[vmem] * (2 + len(extra)),
            out_specs=[vmem] * len(layout),
            compiler_params=params(4),
            name="merge",
        )(*halves, *extra)

    def total(blocks, parts):
        return pl.pallas_call(
            functools.partial(total_kernel, len(parts)),
            out_shape=[
                jax.ShapeDtypeStruct((block, columns), BF16 if a else F32) for a in blocks
            ],
            in_specs=[vmem] * len(parts),
            out_specs=[vmem] * len(blocks),
            compiler_params=params(4),
            name="total",
        )(*parts)

    totals = {}
    if squares:
        other = swap(sums[1], "req", 1)
        halves_x, corner = down([1], near_only=[3])
        corner = (corner, other)
        by_x, by_y = merge(3, [[2, 0], [3, 1]], corner)
        (halves_y,), (halves_own,) = down([2], by_x), down([0], by_x)
        by_x, by_y = swap(by_x, "req", 2), swap(by_y, "req", 4)
        layout = [[1, 0], [2, 3]]
        own = merge(0, layout, halves_own)
        to_x = merge(1, layout, halves_x, (3, 1), (by_y,))
        to_y = merge(2, layout, halves_y, (2, 0), (by_x,))
        for n, blocks in enumerate(layout):
            parts = [own[n], swap(to_x[n], "req", 2), swap(to_y[n], "req", 4)]
            totals.update(zip(blocks, total(blocks, parts)))
    else:
        layout = [list(range(1, head_devices)), [0]]
        merged = [merge(c, layout, down([c])[0]) for c in range(chips)]
        for n, blocks in enumerate(layout):
            parts = [merged[0][n]] + [swap(merged[c][n], "req", 2 * c) for c in range(1, chips)]
            totals.update(zip(blocks, total(blocks, parts)))
    output = state.astype(F32) + totals[0]
    for a in range(head_devices - 1, 0, -1):
        output += swap(totals[a], "head", a).astype(F32)
    return output.astype(BF16)


def solution(mesh):
    return jax.shard_map(
        shards,
        mesh=mesh,
        in_specs=(
            P("req", "head"),
            P("req", "head"),
            P("req", "head"),
            P("req", None, "head"),
            P("req", None, "head"),
            P("req", None),
            P("req"),
            P("head", "req"),
            P("head", "req"),
            P(),
            P(None, ("req", "head")),
            P(None, ("req", "head")),
            P(("req", "head"), None),
        ),
        out_specs=P("head", "req"),
        check_vma=False,
    )
```
